128 devices in a mesh: dp: 32 (over x, z, core), tensor: 4 (over y).
Axes of the slice: x: 4, y: 4, z: 4, core: 2. Of those that a mesh axis runs over, the one named last changes fastest.
Arguments:
- tokens: bfloat16 [1024, 198, 384], P('dp'), may hold values from -6 to 6
- keep_mask: int32 [1024, 198], P('dp'), may hold values from 0 to 1, as said below
- norm1_gain: float32 [384], replicated, may hold values from 0.1 to 1.9
- norm1_shift: float32 [384], replicated, may hold values from -3 to 3
- w_qkv: bfloat16 [384, 1152], replicated, may hold values from -0.3125 to 0.3125
- bias_q: float32 [384], replicated, may hold values from -3 to 3
- bias_v: float32 [384], replicated, may hold values from -3 to 3
- w_out: bfloat16 [384, 384], replicated, may hold values from -1.75 to 1.75
- bias_out: float32 [384], replicated, may hold values from -3 to 3
- norm2_gain: float32 [384], replicated, may hold values from 0.1 to 1.9
- norm2_shift: float32 [384], replicated, may hold values from -3 to 3
- w_up: bfloat16 [384, 1536], P(None, 'tensor'), may hold values from -0.3125 to 0.3125
- bias_up: float32 [1536], P('tensor'), may hold values from -3 to 3
- w_down: bfloat16 [1536, 384], P('tensor'), may hold values from -0.15625 to 0.15625
- bias_down: float32 [384], replicated, may hold values from -3 to 3
- cotangent: bfloat16 [1024, 198, 384], P('dp'), may hold values from -6 to 6
Outputs:
- out: float32 [1024, 198, 384], P('dp')
- grad_tokens: float32 [1024, 198, 384], P('dp')
- grad_norm1_gain: float32 [384], replicated
- grad_norm1_shift: float32 [384], replicated
- grad_w_qkv: float32 [384, 1152], replicated
- grad_bias_q: float32 [384], replicated
- grad_bias_v: float32 [384], replicated
- grad_w_out: float32 [384, 384], replicated
- grad_bias_out: float32 [384], replicated
- grad_norm2_gain: float32 [384], replicated
- grad_norm2_shift: float32 [384], replicated
- grad_w_up: float32 [384, 1536], P(None, 'tensor')
- grad_bias_up: float32 [1536], P('tensor')
- grad_w_down: float32 [1536, 384], P('tensor')
- grad_bias_down: float32 [384], replicated
The draws below stay inside these ranges and needn't reach their ends.
Inputs may be any that keep to these rules, and one draw needn't show every extreme that they name: `keep_mask`: slots 0 and 1 of every image (class and distillation tokens) are 1; every image keeps at least one of its 196 patch slots.
All inputs are finite; a program needn't handle non-finite values.
Results may differ from the reference program's by a relative error of at most 0.025.
Values may be sent and summed in bfloat16 or wider, within the bound.
No kernel may reach another device: no remote copies, remote signals or barrier semaphores. Data moves between devices by JAX's collectives and lax.ppermute only.
A program may use at most 384 MiB of HBM per device.

```python
from functools import partial
import jax
import jax.numpy as jnp
from jax import lax

D = 384
HEADS = 6
HEAD_DIM = 64
FF = 1536
SEQ = 198
IMAGES = 1024


def draw_keep_mask(key, part):
    key = jax.random.fold_in(key, 7)
    patch_count = SEQ - 2
    key_shift, key_less, key_order = jax.random.split(key, 3)
    shift_level = jax.random.randint(key_shift, (IMAGES, 1), 0, 4)
    reduction = jax.random.randint(key_less, (IMAGES, 1), 0, patch_count // 8 + 1)
    kept_count = jnp.clip(jnp.right_shift(jnp.int32(patch_count), shift_level) - reduction, 1, patch_count)
    random_keys = jax.random.randint(key_order, (IMAGES, patch_count), 0, 4096) * patch_count
    random_keys = random_keys + jnp.arange(patch_count, dtype=jnp.int32)[None, :]
    ordering = jnp.argsort(random_keys, axis=1, stable=True)
    ranking = jnp.argsort(ordering, axis=1, stable=True)
    patch_keep = (ranking < kept_count).astype(jnp.int32)
    leading_kept = jnp.ones((IMAGES, 2), jnp.int32)
    return jnp.concatenate([leading_kept, patch_keep], axis=1)


def steps_of(own_key, extent, cuts, least, top_value):
    def one(dim, parts):
        draws = jax.random.uniform(jax.random.fold_in(jax.random.fold_in(own_key, 6), dim), (parts,), jnp.float32, least / len(cuts), top_value / len(cuts))
        return jnp.repeat(jnp.exp(draws), extent[dim] // parts).reshape((-1,) + (1,) * (len(extent) - dim - 1))

    loudness = one(*cuts[0])
    for cut in cuts[1:]:
        loudness = loudness * one(*cut)
    return loudness


def bell_draw(key, dims, deviation, bound, shards=(), held_as=jnp.bfloat16):
    drawn = jax.random.normal(key, dims, jnp.float32) * deviation
    if len(shards) > 0:
        drawn = steps_of(key, dims, shards, -0.22, 0.18) * drawn
    return jnp.clip(drawn, min=-bound, max=bound).astype(held_as)


def setup_inputs(seed: int = 0) -> dict:
    seeds = jax.random.split(jax.random.key(seed), 17)
    tokens = bell_draw(seeds[0], (IMAGES, SEQ, D), 1.0, 6.0, ((0, 32),))
    keep_mask = draw_keep_mask(jax.random.fold_in(seeds[16], 71), 0)
    norm1_gain = jnp.clip(1.0 + 0.18 * jax.random.normal(seeds[2], (D,), jnp.float32), 0.1, 1.9)
    norm1_shift = bell_draw(seeds[3], (D,), 0.5, 3.0, (), jnp.float32)
    w_qkv = bell_draw(seeds[4], (D, 3 * D), D ** -0.5, 0.3125)
    bias_q = bell_draw(seeds[5], (D,), 0.5, 3.0, (), jnp.float32)
    bias_v = bell_draw(seeds[6], (D,), 0.5, 3.0, (), jnp.float32)
    w_out = bell_draw(seeds[7], (D, D), (D // 32) ** -0.5, 1.75)
    bias_out = bell_draw(seeds[8], (D,), 0.5, 3.0, (), jnp.float32)
    norm2_gain = jnp.clip(1.0 + 0.18 * jax.random.normal(seeds[9], (D,), jnp.float32), 0.1, 1.9)
    norm2_shift = bell_draw(seeds[10], (D,), 0.5, 3.0, (), jnp.float32)
    w_up = bell_draw(seeds[11], (D, FF), D ** -0.5, 0.3125, ((1, 4),))
    bias_up = bell_draw(seeds[12], (FF,), 0.5, 3.0, ((0, 4),), jnp.float32)
    w_down = bell_draw(seeds[13], (FF, D), FF ** -0.5, 0.15625, ((0, 4),))
    bias_down = bell_draw(seeds[14], (D,), 0.5, 3.0, (), jnp.float32)
    cotangent = bell_draw(seeds[15], (IMAGES, SEQ, D), 1.0, 6.0, ((0, 32),))
    return {"tokens": tokens, "keep_mask": keep_mask, "norm1_gain": norm1_gain, "norm1_shift": norm1_shift, "w_qkv": w_qkv, "bias_q": bias_q, "bias_v": bias_v, "w_out": w_out, "bias_out": bias_out, "norm2_gain": norm2_gain, "norm2_shift": norm2_shift, "w_up": w_up, "bias_up": bias_up, "w_down": w_down, "bias_down": bias_down, "cotangent": cotangent}


@jax.custom_vjp
def low(v):
    return lax.optimization_barrier(v.astype(jnp.bfloat16)).astype(jnp.float32)

@jax.custom_vjp
def low_back(v):
    return v

def low_keep(v):
    return (low(v), None)

def low_pass(kept, grad):
    return (grad,)

def back_keep(v):
    return (v, None)

def back_low(kept, grad):
    return (low(grad),)
low.defvjp(low_keep, low_pass)
low_back.defvjp(back_keep, back_low)
EPSILON = 1e-06

def norm_rows(values, norm_gain, norm_shift):
    row_mean = lax.optimization_barrier(jnp.mean(values, -1, keepdims=True))
    centered = values - row_mean
    variance = lax.optimization_barrier(jnp.mean(centered * centered, -1, keepdims=True))
    return centered * lax.rsqrt(variance + EPSILON) * norm_gain + norm_shift

def matmul_high(left, right):
    return jnp.einsum('gsd,de->gse', left, right, precision=lax.Precision.HIGHEST)

def layer_group(weights_all, group_inputs):
    gain_one, shift_one, qkv_matrix, query_bias, value_bias, out_matrix, out_bias, gain_two, shift_two, up_matrix, up_bias, down_matrix, down_bias = weights_all
    inputs, keep = group_inputs
    image_count = inputs.shape[0]
    hidden_one = low(norm_rows(inputs, gain_one, shift_one))
    mixed = low_back(matmul_high(hidden_one, qkv_matrix))
    query = low(mixed[..., :D] + query_bias).reshape(image_count, SEQ, HEADS, HEAD_DIM)
    key_part = low(mixed[..., D:2 * D]).reshape(image_count, SEQ, HEADS, HEAD_DIM)
    value = low(mixed[..., 2 * D:] + value_bias).reshape(image_count, SEQ, HEADS, HEAD_DIM)
    raw_scores = low_back(jnp.einsum('gqhc,gkhc->ghqk', query, key_part, precision=lax.Precision.HIGHEST))
    scores = raw_scores * HEAD_DIM ** (-0.5)
    scores = jnp.where(keep[:, None, None, :] > 0, scores, -1e+30)
    row_top = lax.optimization_barrier(jnp.max(scores, -1, keepdims=True))
    weights_exp = jnp.exp(scores - row_top)
    probs = weights_exp / lax.optimization_barrier(jnp.sum(weights_exp, -1, keepdims=True))
    attended = jnp.einsum('ghqk,gkhc->gqhc', low(probs), value, precision=lax.Precision.HIGHEST)
    attended = low_back(low(attended.reshape(image_count, SEQ, D)))
    projected = low_back(matmul_high(attended, out_matrix))
    middle = inputs + keep[..., None] * (projected + out_bias)
    hidden_two = low(norm_rows(middle, gain_two, shift_two))
    upper = low_back(matmul_high(hidden_two, up_matrix)) + up_bias
    activation = low(jax.nn.gelu(upper))
    lowered = low_back(matmul_high(activation, down_matrix))
    return middle + keep[..., None] * (lowered + down_bias)

def reference(tokens, keep_mask, norm1_gain, norm1_shift, w_qkv, bias_q, bias_v, w_out, bias_out, norm2_gain, norm2_shift, w_up, bias_up, w_down, bias_down, cotangent):
    weights_all = tuple((arr.astype(jnp.float32) for arr in (norm1_gain, norm1_shift, w_qkv, bias_q, bias_v, w_out, bias_out, norm2_gain, norm2_shift, w_up, bias_up, w_down, bias_down)))
    inputs = tokens.astype(jnp.float32)
    keep = keep_mask.astype(jnp.float32).reshape(IMAGES // 8, 8, SEQ)

    def forward(inputs_all, weights_in):
        token_groups = inputs_all.reshape(IMAGES // 8, 8, SEQ, D)
        step_fn = jax.checkpoint(partial(layer_group, weights_in))
        result = lax.map(step_fn, (token_groups, keep))
        return result.reshape(IMAGES, SEQ, D)
    out, pull_back = jax.vjp(forward, inputs, weights_all)
    grad_inputs, grad_weights = pull_back(cotangent.astype(jnp.float32))
    return (out, grad_inputs, grad_weights[0], grad_weights[1], grad_weights[2], grad_weights[3], grad_weights[4], grad_weights[5], grad_weights[6], grad_weights[7], grad_weights[8], grad_weights[9], grad_weights[10], grad_weights[11], grad_weights[12])
```

```python
import functools

import jax
import jax.numpy as jnp
from jax import lax
from jax.experimental import pallas as pl
from jax.experimental.pallas import tpu as pltpu
from jax.sharding import PartitionSpec as P

HEADS = 6
HEAD_DIM = 64
WIDTH = 384
SLOTS = 198
SLOT_ROWS = 208
IMAGES = 32
BIN = 256
MAX_BINS = 8
EPSILON = 1e-06
MASKED = -1e30
ABSENT = -4096.0
MIB = 1024 * 1024
BF = jnp.bfloat16
F32 = jnp.float32
GELU_C = 0.7978845608028654
GELU_A = 0.044715


def nn(left, right):
    return lax.dot_general(left, right, (((1,), (0,)), ((), ())), preferred_element_type=F32)


def nt(left, right):
    return lax.dot_general(left, right, (((1,), (1,)), ((), ())), preferred_element_type=F32)


def iota(shape, dim):
    return lax.broadcasted_iota(jnp.int32, shape, dim)


def eye(size):
    return jnp.where(iota((size, size), 0) == iota((size, size), 1), 1.0, 0.0).astype(BF)


def bins_here(plan, me):
    return (plan[3, 0] - me + 3) // 4


def bin_at(rank):
    def index(j, plan, me):
        last = jnp.maximum(bins_here(plan, me[0]) - 1, 0)
        return (jnp.minimum(j, last),) + (0,) * (rank - 1)

    return index


def bin_spec(*tail):
    return pl.BlockSpec((None,) + tail, bin_at(len(tail) + 1))


def whole(*shape):
    zeros = (0,) * len(shape)
    return pl.BlockSpec(shape, lambda *_: zeros, pipeline_mode=pl.Buffered(1))


def row_stats(values):
    mean = jnp.mean(values, 0, keepdims=True)
    centered = values - mean
    inverse = lax.rsqrt(jnp.mean(centered * centered, 0, keepdims=True) + EPSILON)
    return mean, inverse


def plan_kernel(count, rank, plan, order, load):
    def clear(i, carry):
        order[rank[i]] = i
        load[i] = 0
        return carry

    lax.fori_loop(0, IMAGES, clear, 0)

    def place(k, used):
        image = order[k]
        size = count[image]
        found, filled = lax.while_loop(
            lambda c: c[1] + size > BIN, lambda c: (c[0] + 1, load[c[0] + 1]), (0, load[0])
        )
        plan[0, image] = found
        plan[1, image] = filled
        plan[2, image] = size
        load[found] = filled + size
        return jnp.maximum(used, found + 1)

    plan[3, 0] = lax.fori_loop(0, IMAGES, place, 0)


def make_plan(count, rank):
    smem = pl.BlockSpec(memory_space=pltpu.SMEM)
    return pl.pallas_call(
        plan_kernel,
        out_shape=jax.ShapeDtypeStruct((4, IMAGES), jnp.int32),
        in_specs=[smem, smem],
        out_specs=smem,
        scratch_shapes=[pltpu.SMEM((IMAGES,), jnp.int32), pltpu.SMEM((IMAGES,), jnp.int32)],
        name="plan",
    )(count, rank)


def attend_kernel(
    plan, me, tok, cot, posm, wqkv, wout, vec,
    xt_o, ct_o, stat_o, h1_o, qk_o, vtok_o, e_o, linv_o, at_o, mid_o,
    x32, c32, wqkv_t, wout_t, vecs, xb, cb, segr, segc, mask,
):
    j = pl.program_id(0)

    @pl.when(j == 0)
    def _():
        step = 11

        def widen(n, carry):
            for src, dst in ((tok, x32), (cot, c32)):
                part = src[pl.ds(n * step, step)].astype(F32)
                for c in range(3):
                    dst[c, pl.ds(n * step * IMAGES, step * IMAGES), :] = part[
                        :, :, 128 * c : 128 * c + 128
                    ].reshape(step * IMAGES, 128)
            return carry

        lax.fori_loop(0, SLOTS // step, widen, 0)
        tail = (SLOT_ROWS - SLOTS) * IMAGES
        for c in range(3):
            x32[c, pl.ds(SLOTS * IMAGES, tail), :] = jnp.zeros((tail, 128), F32)
            c32[c, pl.ds(SLOTS * IMAGES, tail), :] = jnp.zeros((tail, 128), F32)
        one = eye(WIDTH)
        for m in range(3):
            cols = slice(WIDTH * m, WIDTH * m + WIDTH)
            wqkv_t[cols, :] = nt(one, wqkv[:, cols]).astype(BF)
        wout_t[...] = nt(one, wout[...]).astype(BF)
        columns = vec[...].T
        for m in range(5):
            vecs[m] = jnp.broadcast_to(columns[:, m : m + 1], (WIDTH, BIN))

    @pl.when(j < bins_here(plan, me[0]))
    def _():
        here = 4 * j + me[0]
        xb[...] = jnp.zeros_like(xb)
        cb[...] = jnp.zeros_like(cb)
        segr[...] = jnp.full(segr.shape, -1, jnp.int32)
        segc[...] = jnp.full(segc.shape, -1, jnp.int32)

        def pack(i, carry):
            @pl.when(plan[0, i] == here)
            def _():
                off = plan[1, i]
                size = plan[2, i]
                target = posm[pl.ds(i, 1), :SLOT_ROWS] + off.astype(F32)
                spots = iota((BIN, SLOT_ROWS), 0).astype(F32)
                pick = jnp.where(spots == target, 1.0, 0.0).astype(BF)
                for src, dst in ((x32, xb), (c32, cb)):
                    rows = [src[c, pl.ds(i, SLOT_ROWS, stride=IMAGES), :] for c in range(3)]
                    dst[...] += nn(pick, jnp.concatenate(rows, 1).astype(BF))
                lane = iota(segr.shape, 1)
                segr[...] = jnp.where((lane >= off) & (lane < off + size), i, segr[...])
                row = iota(segc.shape, 0)
                segc[...] = jnp.where((row >= off) & (row < off + size), i, segc[...])

            return carry

        lax.fori_loop(0, IMAGES, pack, 0)
        same = jnp.concatenate([segc[...], segc[...]], 1) == segr[0:1, :]
        mask[...] = jnp.where(same, 0.0, MASKED)
        ct_o[...] = cb[...].T.astype(BF)
        x = xb[...].T
        xt_o[...] = x.astype(BF)
        mean, inverse = row_stats(x)
        stat_o[...] = jnp.concatenate([mean, inverse, jnp.zeros((6, BIN), F32)], 0)
        h1 = ((x - mean) * inverse * vecs[0] + vecs[1]).astype(BF)
        h1_o[...] = h1
        query = ((nn(wqkv_t[0:WIDTH, :], h1) + vecs[2]).astype(BF).astype(F32) * 0.125).astype(BF)
        key = nn(wqkv_t[WIDTH : 2 * WIDTH, :], h1)
        value = nn(wqkv_t[2 * WIDTH :, :], h1) + vecs[3]
        key_tok = key.T.astype(BF)
        vtok_o[...] = value.T.astype(BF)
        value = value.astype(BF)
        qk_o[0:WIDTH, :] = query
        qk_o[WIDTH:, :] = key.astype(BF)
        blank = jnp.zeros((HEAD_DIM, BIN), BF)
        parts = []
        inverses = []
        for h in range(HEADS):
            rows = slice(HEAD_DIM * h, HEAD_DIM * h + HEAD_DIM)
            pair = slice(128 * (h // 2), 128 * (h // 2) + 128)
            own = query[rows, :]
            spread = jnp.concatenate([own, blank] if h % 2 == 0 else [blank, own], 0)
            scores = nn(key_tok[:, pair], spread) + mask[...]
            weights = jnp.exp(scores - jnp.max(scores, 0, keepdims=True))
            low = weights.astype(BF)
            e_o[h] = low
            over = 1.0 / jnp.sum(weights, 0, keepdims=True)
            inverses.append(over)
            parts.append((nn(value[rows, :], low) * over).astype(BF))
        linv_o[...] = jnp.concatenate(inverses + [jnp.zeros((2, BIN), F32)], 0)
        attended = jnp.concatenate(parts, 0)
        at_o[...] = attended
        mid_o[...] = x + (nn(wout_t[...], attended) + vecs[4])


def attend(plan, me, tok, cot, posm, wqkv, wout, vec):
    def out(*tail, dtype=BF):
        return jax.ShapeDtypeStruct((MAX_BINS,) + tail, dtype)

    shapes = [
        ((WIDTH, BIN), BF), ((WIDTH, BIN), BF), ((8, BIN), F32), ((WIDTH, BIN), BF),
        ((2 * WIDTH, BIN), BF), ((BIN, WIDTH), BF), ((HEADS, BIN, BIN), BF), ((8, BIN), F32),
        ((WIDTH, BIN), BF), ((WIDTH, BIN), F32),
    ]
    return pl.pallas_call(
        attend_kernel,
        grid_spec=pltpu.PrefetchScalarGridSpec(
            num_scalar_prefetch=2,
            grid=(MAX_BINS,),
            in_specs=[
                whole(SLOTS, IMAGES, WIDTH), whole(SLOTS, IMAGES, WIDTH), whole(IMAGES, BIN),
                whole(WIDTH, 3 * WIDTH), whole(WIDTH, WIDTH), whole(8, WIDTH),
            ],
            out_specs=[bin_spec(*s) for s, _ in shapes],
            scratch_shapes=[
                pltpu.VMEM((3, SLOT_ROWS * IMAGES, 128), F32),
                pltpu.VMEM((3, SLOT_ROWS * IMAGES, 128), F32),
                pltpu.VMEM((3 * WIDTH, WIDTH), BF),
                pltpu.VMEM((WIDTH, WIDTH), BF),
                pltpu.VMEM((5, WIDTH, BIN), F32),
                pltpu.VMEM((BIN, WIDTH), F32),
                pltpu.VMEM((BIN, WIDTH), F32),
                pltpu.VMEM((8, BIN), jnp.int32),
                pltpu.VMEM((BIN, 128), jnp.int32),
                pltpu.VMEM((BIN, BIN), F32),
            ],
        ),
        out_shape=[out(*s, dtype=d) for s, d in shapes],
        compiler_params=pltpu.CompilerParams(vmem_limit_bytes=56 * MIB),
        cost_estimate=pl.CostEstimate(flops=8 * 10**9, bytes_accessed=30 * 10**6, transcendentals=0),
        name="attend",
    )(plan, me, tok, cot, posm, wqkv, wout, vec)


GROUP_ROWS = 832


def feed_kernel(
    plan, me, mid_i, at_i, ct_i, w0, w1, w2, w3, wout, vec,
    out_o, gm_o, da_o, grads_o, gout_o, gvec_o,
    up_t, down_t, vecs, biases, grads, gout, gvec,
):
    j = pl.program_id(0)
    packs = (w0, w1, w2, w3)

    @pl.when(j == 0)
    def _():
        one = eye(WIDTH)
        for d in range(4):
            up_t[d] = nt(one, packs[d][0:WIDTH, :]).astype(BF)
            down_t[d] = nt(one, packs[d][WIDTH : 2 * WIDTH, :]).astype(BF)
            extra = packs[d][2 * WIDTH : 2 * WIDTH + 16, :].astype(F32)
            bias = extra[0:1, :] + extra[1:2, :] + extra[2:3, :]
            column = jnp.broadcast_to(bias, (8, WIDTH)).T
            biases[d] = jnp.broadcast_to(column[:, 0:1], (WIDTH, BIN))
        columns = vec[...].T
        for m in range(3):
            vecs[m] = jnp.broadcast_to(columns[:, m + 5 : m + 6], (WIDTH, BIN))
        grads[...] = jnp.zeros_like(grads)
        gout[...] = jnp.zeros_like(gout)
        gvec[...] = jnp.zeros_like(gvec)

    @pl.when(j < bins_here(plan, me[0]))
    def _():
        ones = jnp.ones((16, BIN), BF)
        middle = mid_i[...]
        mean, inverse = row_stats(middle)
        unit = (middle - mean) * inverse
        h2 = (unit * vecs[0] + vecs[1]).astype(BF)
        branch = ct_i[...]
        lowered = vecs[2]
        grad_h2 = jnp.zeros((WIDTH, BIN), F32)
        for d in range(4):
            up = nn(up_t[d], h2) + biases[d]
            square = up * up
            tanh = jnp.tanh(up * (GELU_C * GELU_A * square + GELU_C))
            half = 0.5 * tanh + 0.5
            act = up * half
            slope = half + act * (1.0 - tanh) * (3.0 * GELU_C * GELU_A * square + GELU_C)
            act = act.astype(BF)
            lowered = lowered + nn(down_t[d], act)
            grad_up = (nn(packs[d][WIDTH : 2 * WIDTH, :], branch) * slope).astype(BF)
            grads[d, 0:WIDTH, :] += nt(h2, grad_up)
            grads[d, WIDTH : 2 * WIDTH, :] += nt(act, branch)
            grads[d, 2 * WIDTH : 2 * WIDTH + 16, :] += nt(ones, grad_up)
            grad_h2 = grad_h2 + nn(packs[d][0:WIDTH, :], grad_up)
        result = (middle + lowered).astype(BF)
        out_o[...] = nt(eye(BIN), result).astype(BF)
        scaled = grad_h2 * vecs[0]
        first = jnp.mean(scaled, 0, keepdims=True)
        second = jnp.mean(scaled * unit, 0, keepdims=True)
        grad_mid = branch.astype(F32) + inverse * (scaled - first - unit * second)
        gm_o[...] = grad_mid
        low_mid = grad_mid.astype(BF)
        gout[...] += nt(at_i[...], low_mid)
        da_o[...] = nn(wout[...], low_mid).astype(BF)
        gvec[0] += nt(ones, (grad_h2 * unit).astype(BF))
        gvec[1] += nt(ones, grad_h2.astype(BF))
        gvec[2] += nt(ones, branch)
        gvec[3] += nt(ones, low_mid)

    @pl.when(j == MAX_BINS - 1)
    def _():
        grads_o[...] = grads[...].astype(BF)
        gout_o[...] = gout[...].astype(BF)
        gvec_o[...] = jnp.concatenate([gvec[m][0:1] for m in range(4)] + [jnp.zeros((4, WIDTH), F32)], 0)


def feed(plan, me, mid, at, ct, packs, wout, vec):
    return pl.pallas_call(
        feed_kernel,
        grid_spec=pltpu.PrefetchScalarGridSpec(
            num_scalar_prefetch=2,
            grid=(MAX_BINS,),
            in_specs=[bin_spec(WIDTH, BIN)] * 3
            + [whole(2 * WIDTH + 16, WIDTH)] * 4
            + [whole(WIDTH, WIDTH), whole(8, WIDTH)],
            out_specs=[
                bin_spec(BIN, WIDTH),
                bin_spec(WIDTH, BIN),
                bin_spec(WIDTH, BIN),
                whole(4, GROUP_ROWS, WIDTH),
                whole(WIDTH, WIDTH),
                whole(8, WIDTH),
            ],
            scratch_shapes=[
                pltpu.VMEM((4, WIDTH, WIDTH), BF),
                pltpu.VMEM((4, WIDTH, WIDTH), BF),
                pltpu.VMEM((3, WIDTH, BIN), F32),
                pltpu.VMEM((4, WIDTH, BIN), F32),
                pltpu.VMEM((4, GROUP_ROWS, WIDTH), F32),
                pltpu.VMEM((WIDTH, WIDTH), F32),
                pltpu.VMEM((4, 16, WIDTH), F32),
            ],
        ),
        out_shape=[
            jax.ShapeDtypeStruct((MAX_BINS, BIN, WIDTH), BF),
            jax.ShapeDtypeStruct((MAX_BINS, WIDTH, BIN), F32),
            jax.ShapeDtypeStruct((MAX_BINS, WIDTH, BIN), BF),
            jax.ShapeDtypeStruct((4, GROUP_ROWS, WIDTH), BF),
            jax.ShapeDtypeStruct((WIDTH, WIDTH), BF),
            jax.ShapeDtypeStruct((8, WIDTH), F32),
        ],
        compiler_params=pltpu.CompilerParams(vmem_limit_bytes=56 * MIB),
        cost_estimate=pl.CostEstimate(flops=20 * 10**9, bytes_accessed=30 * 10**6, transcendentals=0),
        name="feed",
    )(plan, me, mid, at, ct, *packs, wout, vec)


TAIL_ROWS = 1600


def back_kernel(
    plan, me, xt_i, stat_i, h1_i, qk_i, vtok_i, e_i, linv_i, at_i, gm_i, da_i, wqkv, vec, gout, gvec_i,
    wire_o, grads_o, gain, grads, gvec,
):
    j = pl.program_id(0)

    @pl.when(j == 0)
    def _():
        columns = vec[...].T
        gain[...] = jnp.broadcast_to(columns[:, 0:1], (WIDTH, BIN))
        grads[...] = jnp.zeros_like(grads)
        gvec[...] = jnp.zeros_like(gvec)

    @pl.when(j < bins_here(plan, me[0]))
    def _():
        ones = jnp.ones((16, BIN), BF)
        blank = jnp.zeros((HEAD_DIM, BIN), BF)
        queries = []
        keys = []
        values = []
        for h in range(HEADS):
            rows = slice(HEAD_DIM * h, HEAD_DIM * h + HEAD_DIM)
            krows = slice(WIDTH + HEAD_DIM * h, WIDTH + HEAD_DIM * h + HEAD_DIM)
            pair = slice(128 * (h // 2), 128 * (h // 2) + 128)
            grad_att = (da_i[rows, :].astype(F32) * linv_i[h : h + 1, :]).astype(BF)
            spread = jnp.concatenate([grad_att, blank] if h % 2 == 0 else [blank, grad_att], 0)
            inner = jnp.sum(grad_att.astype(F32) * at_i[rows, :].astype(F32), 0, keepdims=True)
            weights = e_i[h]
            grad_scores = (weights.astype(F32) * (nn(vtok_i[:, pair], spread) - inner)).astype(BF)
            values.append(nt(grad_att, weights).astype(BF))
            queries.append((nn(qk_i[krows, :], grad_scores) * 0.125).astype(BF))
            keys.append(nt(qk_i[rows, :], grad_scores).astype(BF))
        h1 = h1_i[...]
        grad_h1 = jnp.zeros((WIDTH, BIN), F32)
        for m, parts in enumerate((queries, keys, values)):
            mixed = jnp.concatenate(parts, 0)
            grads[m] += nt(h1, mixed)
            grad_h1 = grad_h1 + nn(wqkv[:, WIDTH * m : WIDTH * m + WIDTH], mixed)
            if m != 1:
                gvec[m] += nt(ones, mixed)
        inverse = stat_i[1:2, :]
        unit = (xt_i[...].astype(F32) - stat_i[0:1, :]) * inverse
        scaled = grad_h1 * gain[...]
        first = jnp.mean(scaled, 0, keepdims=True)
        second = jnp.mean(scaled * unit, 0, keepdims=True)
        result = gm_i[...] + inverse * (scaled - first - unit * second)
        wire_o[...] = nt(eye(BIN), result.astype(BF)).astype(BF)
        gvec[1] += nt(ones, (grad_h1 * unit).astype(BF))
        gvec[3] += nt(ones, grad_h1.astype(BF))

    @pl.when(j == MAX_BINS - 1)
    def _():
        for m in range(3):
            grads_o[WIDTH * m : WIDTH * m + WIDTH, :] = grads[m].astype(BF)
        grads_o[3 * WIDTH : 4 * WIDTH, :] = gout[...]
        rows = [gvec[m][0:1] for m in range(4)] + [gvec_i[0:4, :]]
        grads_o[4 * WIDTH : 4 * WIDTH + 16, :] = jnp.concatenate(rows + [jnp.zeros((8, WIDTH), F32)], 0).astype(BF)
        grads_o[4 * WIDTH + 16 :, :] = jnp.zeros((TAIL_ROWS - 4 * WIDTH - 16, WIDTH), BF)


def back(plan, me, saved, wqkv, vec, gout, gvec):
    return pl.pallas_call(
        back_kernel,
        grid_spec=pltpu.PrefetchScalarGridSpec(
            num_scalar_prefetch=2,
            grid=(MAX_BINS,),
            in_specs=[
                bin_spec(WIDTH, BIN), bin_spec(8, BIN), bin_spec(WIDTH, BIN), bin_spec(2 * WIDTH, BIN),
                bin_spec(BIN, WIDTH), bin_spec(HEADS, BIN, BIN), bin_spec(8, BIN), bin_spec(WIDTH, BIN),
                bin_spec(WIDTH, BIN), bin_spec(WIDTH, BIN),
                whole(WIDTH, 3 * WIDTH), whole(8, WIDTH), whole(WIDTH, WIDTH), whole(8, WIDTH),
            ],
            out_specs=[bin_spec(BIN, WIDTH), whole(TAIL_ROWS, WIDTH)],
            scratch_shapes=[
                pltpu.VMEM((WIDTH, BIN), F32),
                pltpu.VMEM((3, WIDTH, WIDTH), F32),
                pltpu.VMEM((4, 16, WIDTH), F32),
            ],
        ),
        out_shape=[
            jax.ShapeDtypeStruct((MAX_BINS, BIN, WIDTH), BF),
            jax.ShapeDtypeStruct((TAIL_ROWS, WIDTH), BF),
        ],
        compiler_params=pltpu.CompilerParams(vmem_limit_bytes=56 * MIB),
        cost_estimate=pl.CostEstimate(flops=10 * 10**9, bytes_accessed=30 * 10**6, transcendentals=0),
        name="back",
    )(plan, me, *saved, wqkv, vec, gout, gvec)


UNPACK_IMAGES = 16


def unpack_kernel(plan, every, base, places, out, picks, spread):
    group = pl.program_id(0)
    lanes = pl.ds(pl.multiple_of(pl.program_id(1) * 128, 128), 128)

    @pl.when(pl.program_id(1) == 0)
    def _():
        picks[...] = jnp.zeros_like(picks)
        flat = places.reshape(SLOTS * UNPACK_IMAGES, 128)

        def build(i, carry):
            off = plan[1, group * UNPACK_IMAGES + i].astype(F32)
            spot = flat[pl.ds(i, SLOTS, stride=UNPACK_IMAGES), :] + off
            lane = iota((SLOTS, 128), 1).astype(F32)
            both = [jnp.where(spot == lane + 128.0 * half, 1.0, 0.0) for half in range(2)]
            picks[i, 0:SLOTS, :] = jnp.concatenate(both, 1).astype(BF)
            return carry

        lax.fori_loop(0, UNPACK_IMAGES, build, 0)

    def place(i, carry):
        at = plan[0, group * UNPACK_IMAGES + i]
        rows = nn(picks[i], every[at % 4, at // 4, :, lanes])
        spread[pl.ds(i, SLOTS, stride=UNPACK_IMAGES), :] = rows[0:SLOTS]
        return carry

    lax.fori_loop(0, UNPACK_IMAGES, place, 0)
    kept = places[...] >= 0.0
    out[...] = jnp.where(kept, spread[...].reshape(SLOTS, UNPACK_IMAGES, 128), base[...].astype(F32))


def unpack(plan, every, base, places):
    block = (SLOTS, UNPACK_IMAGES, 128)
    return pl.pallas_call(
        unpack_kernel,
        grid_spec=pltpu.PrefetchScalarGridSpec(
            num_scalar_prefetch=1,
            grid=(IMAGES // UNPACK_IMAGES, 3),
            in_specs=[
                whole(*every.shape),
                pl.BlockSpec(block, lambda g, c, *_: (0, g, c)),
                pl.BlockSpec(block, lambda g, c, *_: (0, g, 0)),
            ],
            out_specs=pl.BlockSpec(block, lambda g, c, *_: (0, g, c)),
            scratch_shapes=[
                pltpu.VMEM((UNPACK_IMAGES, SLOT_ROWS, BIN), BF),
                pltpu.VMEM((SLOTS * UNPACK_IMAGES, 128), F32),
            ],
        ),
        out_shape=jax.ShapeDtypeStruct((SLOTS, IMAGES, WIDTH), F32),
        compiler_params=pltpu.CompilerParams(vmem_limit_bytes=48 * MIB),
        cost_estimate=pl.CostEstimate(flops=10**9, bytes_accessed=20 * 10**6, transcendentals=0),
        name="unpack",
    )(plan, every, base, places)


def shift_y(values, by):
    return lax.ppermute(values, "tensor", [(i, (i + by) % 4) for i in range(4)])


def swap_core(values):
    return lax.ppermute(values, "dp", [(i, i ^ 1) for i in range(32)])


def shift_x(values, by):
    return lax.ppermute(values, "dp", [(i, (i + 8 * by) % 32) for i in range(32)])


def shift_z(values, by):
    return lax.ppermute(values, "dp", [(i, i // 8 * 8 + (i + 2 * by) % 8) for i in range(32)])


def add_up(parts):
    total = parts[0].astype(F32)
    for part in parts[1:]:
        total = total + part.astype(F32)
    return total.astype(BF)


def pick_block(values, index, axis, size):
    return lax.dynamic_slice_in_dim(values, index * size, size, axis)


def scatter_core(values, axis):
    half = values.shape[axis] // 2
    core = lax.axis_index("dp") % 2
    return add_up([pick_block(values, core, axis, half), swap_core(pick_block(values, 1 - core, axis, half))])


def gather_core(values, axis):
    core = lax.axis_index("dp") % 2
    other = swap_core(values)
    low = jnp.where(core == 0, values, other)
    high = jnp.where(core == 0, other, values)
    return jnp.concatenate([low, high], axis)


def scatter_x(values, axis):
    part = values.shape[axis] // 4
    x = lax.axis_index("dp") // 8
    own = pick_block(values, x, axis, part)
    return add_up([own] + [shift_x(pick_block(values, (x + d) % 4, axis, part), d) for d in (1, 3, 2)])


def gather_x(values, axis):
    x = lax.axis_index("dp") // 8
    moved = [values] + [shift_x(values, d) for d in (1, 2, 3)]
    return jnp.concatenate([lax.select_n((x - k) % 4, *moved) for k in range(4)], axis)


def sum_z(values):
    return add_up([values] + [shift_z(values, d) for d in (1, 3, 2)])


def sum_y(values):
    return add_up([values] + [shift_y(values, d) for d in (1, 3, 2)])


def gather_y(values):
    return lax.all_gather(values, "tensor")


def local(
    tokens, keep_mask, norm1_gain, norm1_shift, w_qkv, bias_q, bias_v, w_out, bias_out,
    norm2_gain, norm2_shift, w_up, bias_up, w_down, bias_down, cotangent,
):
    me = lax.axis_index("tensor").astype(jnp.int32).reshape(1)
    tok = jnp.transpose(tokens, (1, 0, 2))
    cot = jnp.transpose(cotangent, (1, 0, 2))

    high = lax.reduce_precision(bias_up, 8, 7)
    middle = lax.reduce_precision(bias_up - high, 8, 7)
    lowest = bias_up - high - middle
    rows = jnp.concatenate([jnp.stack([high, middle, lowest]), jnp.zeros((13, WIDTH), F32)], 0)
    own = jnp.concatenate([w_up, w_down, rows.astype(BF)], 0)
    packs = [own, shift_y(own, 1), shift_y(own, 2), shift_y(own, 3)]

    keep = keep_mask > 0
    before = (jnp.arange(SLOTS)[:, None] < jnp.arange(SLOTS)[None, :]).astype(BF)
    position = jnp.dot(keep.astype(BF), before, preferred_element_type=F32)
    position = jnp.where(keep, position, ABSENT)
    places = jnp.broadcast_to(position.T[:, :, None], (SLOTS, IMAGES, 128))
    posm = jnp.pad(position, ((0, 0), (0, BIN - SLOTS)), constant_values=ABSENT)
    count = jnp.sum(keep_mask, 1)
    index = jnp.arange(IMAGES)
    ahead = (count[None, :] > count[:, None]) | (
        (count[None, :] == count[:, None]) & (index[None, :] < index[:, None])
    )
    rank = jnp.sum(ahead.astype(jnp.int32), 1)
    plan = make_plan(count, rank)
    vec = jnp.stack(
        [norm1_gain, norm1_shift, bias_q, bias_v, bias_out, norm2_gain, norm2_shift, bias_down]
    )

    xt, ct, stat, h1, qk, vtok, weights, linv, at, mid = attend(
        plan, me, tok, cot, posm, w_qkv, w_out, vec
    )
    out_wire, grad_mid, grad_att, mlp_grads, gout, gvec = feed(plan, me, mid, at, ct, packs, w_out, vec)

    part = scatter_core(mlp_grads, 1)
    part = scatter_x(part, 1)
    part = add_up([part[0]] + [shift_y(part[d], 4 - d) for d in (1, 3, 2)])
    part = sum_z(part)
    part = gather_core(gather_x(part, 0), 0)

    grad_wire, tail_grads = back(
        plan, me, (xt, stat, h1, qk, vtok, weights, linv, at, grad_mid, grad_att), w_qkv, vec, gout, gvec
    )
    tail = scatter_core(tail_grads, 0)
    tail = scatter_x(tail, 0)
    tail = sum_y(sum_z(tail))
    tail = gather_core(gather_x(tail, 0), 0)

    out = unpack(plan, gather_y(out_wire), tok, places)
    grad_tokens = unpack(plan, gather_y(grad_wire), cot, places)

    part = part.astype(F32)
    tail = tail.astype(F32)
    small = tail[4 * WIDTH : 4 * WIDTH + 8]
    return (
        jnp.transpose(out, (1, 0, 2)),
        jnp.transpose(grad_tokens, (1, 0, 2)),
        small[1],
        small[3],
        jnp.concatenate([tail[WIDTH * m : WIDTH * m + WIDTH] for m in range(3)], 1),
        small[0],
        small[2],
        tail[3 * WIDTH : 4 * WIDTH],
        small[7],
        small[4],
        small[5],
        part[0:WIDTH],
        part[2 * WIDTH],
        part[WIDTH : 2 * WIDTH],
        small[6],
    )


def solution(mesh):
    rows = P("dp", None, None)
    return jax.shard_map(
        local,
        mesh=mesh,
        in_specs=(
            rows, P("dp", None), P(), P(), P(), P(), P(), P(), P(), P(), P(),
            P(None, "tensor"), P("tensor"), P("tensor", None), P(), rows,
        ),
        out_specs=(
            rows, rows, P(), P(), P(), P(), P(), P(), P(), P(), P(),
            P(None, "tensor"), P("tensor"), P("tensor", None), P(),
        ),
        check_vma=False,
    )
```

```python
import functools

import jax
import jax.numpy as jnp
from jax import lax
from jax.experimental import pallas as pl
from jax.experimental.pallas import tpu as pltpu
from jax.sharding import PartitionSpec as P

HEADS = 6
HEAD_DIM = 64
WIDTH = 384
SLOTS = 198
SLOT_ROWS = 208
IMAGES = 32
BIN = 256
MAX_BINS = 8
EPSILON = 1e-06
SENT_BINS = 5
LOW_BINS = (SENT_BINS + 1) // 2
MASKED = -1e30
ABSENT = -4096.0
MIB = 1024 * 1024
BF = jnp.bfloat16
F32 = jnp.float32
GELU_C = 0.7978845608028654
GELU_A = 0.044715


def nn(left, right):
    return lax.dot_general(left, right, (((1,), (0,)), ((), ())), preferred_element_type=F32)


def nt(left, right):
    return lax.dot_general(left, right, (((1,), (1,)), ((), ())), preferred_element_type=F32)


def iota(shape, dim):
    return lax.broadcasted_iota(jnp.int32, shape, dim)


def eye(size):
    return jnp.where(iota((size, size), 0) == iota((size, size), 1), 1.0, 0.0).astype(BF)


def bins_here(plan, me):
    return (plan[3, 0] - me + 3) // 4


def bin_at(rank):
    def index(j, plan, me):
        last = jnp.maximum(bins_here(plan, me[0]) - 1, 0)
        return (jnp.minimum(j, last),) + (0,) * (rank - 1)

    return index


def sent_at(j, plan, me):
    return (jnp.minimum(bin_at(1)(j, plan, me)[0], SENT_BINS - 1), 0, 0)


def more_at(j, plan, me):
    return (jnp.maximum(bin_at(1)(j, plan, me)[0] - SENT_BINS, 0), 0, 0)


WIRE_SPECS = [pl.BlockSpec((None, BIN, WIDTH), sent_at), pl.BlockSpec((None, BIN, WIDTH), more_at)]
WIRE_SHAPES = [
    jax.ShapeDtypeStruct((SENT_BINS, BIN, WIDTH), BF),
    jax.ShapeDtypeStruct((MAX_BINS - SENT_BINS, BIN, WIDTH), BF),
]


def write_wire(j, rows, sent, more):
    wire = nt(eye(BIN), rows).astype(BF)

    @pl.when(j < SENT_BINS)
    def _():
        sent[...] = wire

    @pl.when(j >= SENT_BINS)
    def _():
        more[...] = wire


def bin_spec(*tail):
    return pl.BlockSpec((None,) + tail, bin_at(len(tail) + 1))


def whole(*shape):
    zeros = (0,) * len(shape)
    return pl.BlockSpec(shape, lambda *_: zeros, pipeline_mode=pl.Buffered(1))


def as_columns(vectors):
    rows = [v[...].reshape(1, WIDTH) for v in vectors]
    rows.append(jnp.zeros((8 - len(rows), WIDTH), F32))
    return jnp.concatenate(rows, 0).T


def spread_columns(vectors, to):
    columns = as_columns(vectors)
    for m in range(len(vectors)):
        to[m] = jnp.broadcast_to(columns[:, m : m + 1], (WIDTH, BIN))


def row_stats(values):
    mean = jnp.mean(values, 0, keepdims=True)
    centered = values - mean
    inverse = lax.rsqrt(jnp.mean(centered * centered, 0, keepdims=True) + EPSILON)
    return mean, inverse


def prepare_kernel(keep, plan, posm, places, wide, stage, table, order, load, sem):
    wide[...] = jnp.zeros_like(wide)
    wide[:, 0:SLOTS] = keep[...]
    kept = wide[...] > 0
    ones = jnp.where(kept, 1.0, 0.0)
    before = jnp.where(iota((BIN, BIN), 0) < iota((BIN, BIN), 1), 1.0, 0.0).astype(BF)
    posm[...] = jnp.where(kept, nn(ones.astype(BF), before), ABSENT)
    count = jnp.broadcast_to(jnp.sum(ones, 1, keepdims=True), (IMAGES, 128))
    across = count.T[0:IMAGES, :]
    down_count = count[:, 0:IMAGES]
    earlier = iota((IMAGES, IMAGES), 1) < iota((IMAGES, IMAGES), 0)
    ahead = (across > down_count) | ((across == down_count) & earlier)
    rank = jnp.sum(jnp.where(ahead, 1.0, 0.0), 1, keepdims=True)
    stage[0] = count.astype(jnp.int32)
    stage[1] = jnp.broadcast_to(rank, (IMAGES, 128)).astype(jnp.int32)
    copy = pltpu.make_async_copy(stage, table, sem)
    copy.start()
    for n in range(SLOTS):
        places[n] = jnp.broadcast_to(posm[:, n : n + 1], (IMAGES, 128))
    copy.wait()

    def clear(i, carry):
        order[table[1, i, 0]] = i
        load[i] = 0
        return carry

    lax.fori_loop(0, IMAGES, clear, 0)

    def place(k, used):
        image = order[k]
        size = table[0, image, 0]
        found, filled = lax.while_loop(
            lambda c: c[1] + size > BIN,
            lambda c: (c[0] + 1, load[jnp.minimum(c[0] + 1, IMAGES - 1)]),
            (0, load[0]),
        )
        plan[0, image] = found
        plan[1, image] = filled
        plan[2, image] = size
        load[found] = filled + size
        return jnp.maximum(used, found + 1)

    plan[3, 0] = lax.fori_loop(0, IMAGES, place, 0)


def pack_kernel(up, down, bias, own):
    own[0:WIDTH, :] = up[...]
    own[WIDTH : 2 * WIDTH, :] = down[...]
    whole_bias = bias[...].reshape(1, WIDTH)
    high = whole_bias.astype(BF).astype(F32)
    middle = (whole_bias - high).astype(BF).astype(F32)
    lowest = whole_bias - high - middle
    rows = jnp.concatenate([high, middle, lowest, jnp.zeros((13, WIDTH), F32)], 0)
    own[2 * WIDTH :, :] = rows.astype(BF)


def pack_weights(up, down, bias):
    vmem = pl.BlockSpec(memory_space=pltpu.VMEM)
    return pl.pallas_call(
        pack_kernel,
        out_shape=jax.ShapeDtypeStruct((2 * WIDTH + 16, WIDTH), BF),
        in_specs=[vmem] * 3,
        out_specs=vmem,
        name="pack",
    )(up, down, bias)


def prepare(keep):
    vmem = pl.BlockSpec(memory_space=pltpu.VMEM)
    return pl.pallas_call(
        prepare_kernel,
        out_shape=[
            jax.ShapeDtypeStruct((4, IMAGES), jnp.int32),
            jax.ShapeDtypeStruct((IMAGES, BIN), F32),
            jax.ShapeDtypeStruct((SLOTS, IMAGES, 128), F32),
        ],
        in_specs=[vmem],
        out_specs=[pl.BlockSpec(memory_space=pltpu.SMEM), vmem, vmem],
        scratch_shapes=[
            pltpu.VMEM((IMAGES, BIN), jnp.int32),
            pltpu.VMEM((2, IMAGES, 128), jnp.int32),
            pltpu.SMEM((2, IMAGES, 128), jnp.int32),
            pltpu.SMEM((IMAGES,), jnp.int32),
            pltpu.SMEM((IMAGES,), jnp.int32),
            pltpu.SemaphoreType.DMA,
        ],
        name="prepare",
    )(keep)


PIECE_SLOTS = 66


def attend_kernel(
    plan, me, tok, cot, posm, wqkv, wout, v0, v1, v2, v3, v4,
    xt_o, ct_o, stat_o, h1_o, qk_o, vtok_o, e_o, linv_o, at_o, mid_o,
    x32, c32, wqkv_t, wout_t, vecs, xb, cb, segr, segc, mask, tok_v, cot_v, sems,
):
    j = pl.program_id(0)

    @pl.when(j == 0)
    def _():
        copies = []
        for n in range(SLOTS // PIECE_SLOTS):
            part = pl.ds(n * PIECE_SLOTS, PIECE_SLOTS)
            for k, (source, target) in enumerate(((tok, tok_v), (cot, cot_v))):
                copies.append(pltpu.make_async_copy(source.at[part], target.at[part], sems.at[k, n]))
        for copy in copies:
            copy.start()
        one = eye(WIDTH)
        for m in range(3):
            cols = slice(WIDTH * m, WIDTH * m + WIDTH)
            wqkv_t[cols, :] = nt(one, wqkv[:, cols]).astype(BF)
        wout_t[...] = nt(one, wout[...]).astype(BF)
        spread_columns((v0, v1, v2, v3, v4), vecs)
        tail = (SLOT_ROWS - SLOTS) * IMAGES
        for c in range(3):
            x32[c, pl.ds(SLOTS * IMAGES, tail), :] = jnp.zeros((tail, 128), F32)
            c32[c, pl.ds(SLOTS * IMAGES, tail), :] = jnp.zeros((tail, 128), F32)
        for n in range(SLOTS // PIECE_SLOTS):
            for k, (source, target) in enumerate(((tok_v, x32), (cot_v, c32))):
                copies[2 * n + k].wait()

                def widen(m, carry):
                    first = n * PIECE_SLOTS + m * 11
                    part = source[pl.ds(first, 11)].astype(F32)
                    for c in range(3):
                        target[c, pl.ds(first * IMAGES, 11 * IMAGES), :] = part[
                            :, :, 128 * c : 128 * c + 128
                        ].reshape(11 * IMAGES, 128)
                    return carry

                lax.fori_loop(0, PIECE_SLOTS // 11, widen, 0)

    @pl.when(j < bins_here(plan, me[0]))
    def _():
        here = 4 * j + me[0]
        xb[...] = jnp.zeros_like(xb)
        cb[...] = jnp.zeros_like(cb)
        segr[...] = jnp.full(segr.shape, -1, jnp.int32)
        segc[...] = jnp.full(segc.shape, -1, jnp.int32)

        def pack(i, carry):
            @pl.when(plan[0, i] == here)
            def _():
                off = plan[1, i]
                size = plan[2, i]
                target = posm[pl.ds(i, 1), :SLOT_ROWS] + off.astype(F32)
                spots = iota((BIN, SLOT_ROWS), 0).astype(F32)
                pick = jnp.where(spots == target, 1.0, 0.0).astype(BF)
                for src, dst in ((x32, xb), (c32, cb)):
                    rows = [src[c, pl.ds(i, SLOT_ROWS, stride=IMAGES), :] for c in range(3)]
                    dst[...] += nn(pick, jnp.concatenate(rows, 1).astype(BF))
                lane = iota(segr.shape, 1)
                segr[...] = jnp.where((lane >= off) & (lane < off + size), i, segr[...])
                row = iota(segc.shape, 0)
                segc[...] = jnp.where((row >= off) & (row < off + size), i, segc[...])

            return carry

        lax.fori_loop(0, IMAGES, pack, 0)
        same = jnp.concatenate([segc[...], segc[...]], 1) == segr[0:1, :]
        mask[...] = jnp.where(same, 0.0, MASKED)
        ct_o[...] = cb[...].T.astype(BF)
        x = xb[...].T
        xt_o[...] = x.astype(BF)
        mean, inverse = row_stats(x)
        stat_o[...] = jnp.concatenate([mean, inverse, jnp.zeros((6, BIN), F32)], 0)
        h1 = ((x - mean) * inverse * vecs[0] + vecs[1]).astype(BF)
        h1_o[...] = h1
        query = ((nn(wqkv_t[0:WIDTH, :], h1) + vecs[2]).astype(BF).astype(F32) * 0.125).astype(BF)
        key = nn(wqkv_t[WIDTH : 2 * WIDTH, :], h1)
        value = nn(wqkv_t[2 * WIDTH :, :], h1) + vecs[3]
        key_tok = key.T.astype(BF)
        vtok_o[...] = value.T.astype(BF)
        value = value.astype(BF)
        qk_o[0:WIDTH, :] = query
        qk_o[WIDTH:, :] = key.astype(BF)
        blank = jnp.zeros((HEAD_DIM, BIN), BF)
        parts = []
        inverses = []
        for h in range(HEADS):
            rows = slice(HEAD_DIM * h, HEAD_DIM * h + HEAD_DIM)
            pair = slice(128 * (h // 2), 128 * (h // 2) + 128)
            own = query[rows, :]
            spread = jnp.concatenate([own, blank] if h % 2 == 0 else [blank, own], 0)
            scores = nn(key_tok[:, pair], spread) + mask[...]
            weights = jnp.exp(scores - jnp.max(scores, 0, keepdims=True))
            low = weights.astype(BF)
            e_o[h] = low
            over = 1.0 / jnp.sum(weights, 0, keepdims=True)
            inverses.append(over)
            parts.append((nn(value[rows, :], low) * over).astype(BF))
        linv_o[...] = jnp.concatenate(inverses + [jnp.zeros((2, BIN), F32)], 0)
        attended = jnp.concatenate(parts, 0)
        at_o[...] = attended
        mid_o[...] = x + (nn(wout_t[...], attended) + vecs[4])


def attend(plan, me, tok, cot, posm, wqkv, wout, vectors):
    def out(*tail, dtype=BF):
        return jax.ShapeDtypeStruct((MAX_BINS,) + tail, dtype)

    shapes = [
        ((WIDTH, BIN), BF), ((WIDTH, BIN), BF), ((8, BIN), F32), ((WIDTH, BIN), BF),
        ((2 * WIDTH, BIN), BF), ((BIN, WIDTH), BF), ((HEADS, BIN, BIN), BF), ((8, BIN), F32),
        ((WIDTH, BIN), BF), ((WIDTH, BIN), F32),
    ]
    return pl.pallas_call(
        attend_kernel,
        grid_spec=pltpu.PrefetchScalarGridSpec(
            num_scalar_prefetch=2,
            grid=(MAX_BINS,),
            in_specs=[
                pl.BlockSpec(memory_space=pl.ANY), pl.BlockSpec(memory_space=pl.ANY), whole(IMAGES, BIN),
                whole(WIDTH, 3 * WIDTH), whole(WIDTH, WIDTH),
            ] + [whole(WIDTH)] * 5,
            out_specs=[bin_spec(*s) for s, _ in shapes],
            scratch_shapes=[
                pltpu.VMEM((3, SLOT_ROWS * IMAGES, 128), F32),
                pltpu.VMEM((3, SLOT_ROWS * IMAGES, 128), F32),
                pltpu.VMEM((3 * WIDTH, WIDTH), BF),
                pltpu.VMEM((WIDTH, WIDTH), BF),
                pltpu.VMEM((5, WIDTH, BIN), F32),
                pltpu.VMEM((BIN, WIDTH), F32),
                pltpu.VMEM((BIN, WIDTH), F32),
                pltpu.VMEM((8, BIN), jnp.int32),
                pltpu.VMEM((BIN, 128), jnp.int32),
                pltpu.VMEM((BIN, BIN), F32),
                pltpu.VMEM((SLOTS, IMAGES, WIDTH), BF),
                pltpu.VMEM((SLOTS, IMAGES, WIDTH), BF),
                pltpu.SemaphoreType.DMA((2, SLOTS // PIECE_SLOTS)),
            ],
        ),
        out_shape=[out(*s, dtype=d) for s, d in shapes],
        compiler_params=pltpu.CompilerParams(vmem_limit_bytes=56 * MIB),
        cost_estimate=pl.CostEstimate(flops=10**6, bytes_accessed=10**5, transcendentals=0),
        name="attend",
    )(plan, me, tok, cot, posm, wqkv, wout, *vectors)


GROUP_ROWS = 832
X_ROWS = GROUP_ROWS // 4


def feed_kernel(
    plan, me, mid_i, at_i, ct_i, w0, w1, w2, w3, wout, v0, v1, v2,
    sent_o, more_o, gm_o, da_o, p0_o, p1_o, p2_o, p3_o, gout_o, gvec_o,
    up_t, down_t, vecs, biases, grads, gout, gvec,
):
    j = pl.program_id(0)
    packs = (w0, w1, w2, w3)

    @pl.when(j == 0)
    def _():
        one = eye(WIDTH)
        for d in range(4):
            up_t[d] = nt(one, packs[d][0:WIDTH, :]).astype(BF)
            down_t[d] = nt(one, packs[d][WIDTH : 2 * WIDTH, :]).astype(BF)
            extra = packs[d][2 * WIDTH : 2 * WIDTH + 16, :].astype(F32)
            bias = extra[0:1, :] + extra[1:2, :] + extra[2:3, :]
            column = jnp.broadcast_to(bias, (8, WIDTH)).T
            biases[d] = jnp.broadcast_to(column[:, 0:1], (WIDTH, BIN))
        spread_columns((v0, v1, v2), vecs)
        grads[...] = jnp.zeros_like(grads)
        gout[...] = jnp.zeros_like(gout)
        gvec[...] = jnp.zeros_like(gvec)

    @pl.when(j < bins_here(plan, me[0]))
    def _():
        ones = jnp.ones((16, BIN), BF)
        middle = mid_i[...]
        mean, inverse = row_stats(middle)
        unit = (middle - mean) * inverse
        h2 = (unit * vecs[0] + vecs[1]).astype(BF)
        branch = ct_i[...]
        lowered = vecs[2]
        grad_h2 = jnp.zeros((WIDTH, BIN), F32)
        for d in range(4):
            up = nn(up_t[d], h2) + biases[d]
            square = up * up
            tanh = jnp.tanh(up * (GELU_C * GELU_A * square + GELU_C))
            half = 0.5 * tanh + 0.5
            act = up * half
            slope = half + act * (1.0 - tanh) * (3.0 * GELU_C * GELU_A * square + GELU_C)
            act = act.astype(BF)
            lowered = lowered + nn(down_t[d], act)
            grad_up = (nn(packs[d][WIDTH : 2 * WIDTH, :], branch) * slope).astype(BF)
            grads[d, 0:WIDTH, :] += nt(h2, grad_up)
            grads[d, WIDTH : 2 * WIDTH, :] += nt(act, branch)
            grads[d, 2 * WIDTH : 2 * WIDTH + 16, :] += nt(ones, grad_up)
            grad_h2 = grad_h2 + nn(packs[d][0:WIDTH, :], grad_up)
        result = (middle + lowered).astype(BF)
        write_wire(j, result, sent_o, more_o)
        scaled = grad_h2 * vecs[0]
        first = jnp.mean(scaled, 0, keepdims=True)
        second = jnp.mean(scaled * unit, 0, keepdims=True)
        grad_mid = branch.astype(F32) + inverse * (scaled - first - unit * second)
        gm_o[...] = grad_mid
        low_mid = grad_mid.astype(BF)
        gout[...] += nt(at_i[...], low_mid)
        da_o[...] = nn(wout[...], low_mid).astype(BF)
        gvec[0] += nt(ones, (grad_h2 * unit).astype(BF))
        gvec[1] += nt(ones, grad_h2.astype(BF))
        gvec[2] += nt(ones, branch)
        gvec[3] += nt(ones, low_mid)

    @pl.when(j == pl.num_programs(0) - 1)
    def _():
        for d, piece in enumerate((p0_o, p1_o, p2_o, p3_o)):
            rows = pl.ds(pl.multiple_of(((me[1] + d) & 3) * X_ROWS, 8), X_ROWS)
            piece[...] = grads[:, rows, :].astype(BF)
        gout_o[...] = gout[...].astype(BF)
        gvec_o[...] = jnp.concatenate([gvec[m][0:1] for m in range(4)] + [jnp.zeros((4, WIDTH), F32)], 0)


def feed(plan, me, mid, at, ct, packs, wout, vectors):
    return pl.pallas_call(
        feed_kernel,
        grid_spec=pltpu.PrefetchScalarGridSpec(
            num_scalar_prefetch=2,
            grid=(MAX_BINS,),
            in_specs=[bin_spec(WIDTH, BIN)] * 3
            + [whole(2 * WIDTH + 16, WIDTH)] * 4
            + [whole(WIDTH, WIDTH)]
            + [whole(WIDTH)] * 3,
            out_specs=[
                *WIRE_SPECS,
                bin_spec(WIDTH, BIN),
                bin_spec(WIDTH, BIN),
                *[whole(4, X_ROWS, WIDTH)] * 4,
                whole(WIDTH, WIDTH),
                whole(8, WIDTH),
            ],
            scratch_shapes=[
                pltpu.VMEM((4, WIDTH, WIDTH), BF),
                pltpu.VMEM((4, WIDTH, WIDTH), BF),
                pltpu.VMEM((3, WIDTH, BIN), F32),
                pltpu.VMEM((4, WIDTH, BIN), F32),
                pltpu.VMEM((4, GROUP_ROWS, WIDTH), F32),
                pltpu.VMEM((WIDTH, WIDTH), F32),
                pltpu.VMEM((4, 16, WIDTH), F32),
            ],
        ),
        out_shape=[
            *WIRE_SHAPES,
            jax.ShapeDtypeStruct((MAX_BINS, WIDTH, BIN), F32),
            jax.ShapeDtypeStruct((MAX_BINS, WIDTH, BIN), BF),
            *[jax.ShapeDtypeStruct((4, X_ROWS, WIDTH), BF)] * 4,
            jax.ShapeDtypeStruct((WIDTH, WIDTH), BF),
            jax.ShapeDtypeStruct((8, WIDTH), F32),
        ],
        compiler_params=pltpu.CompilerParams(vmem_limit_bytes=56 * MIB),
        cost_estimate=pl.CostEstimate(flops=10**6, bytes_accessed=10**5, transcendentals=0),
        name="feed",
    )(plan, me, mid, at, ct, *packs, wout, *vectors)


TAIL_ROWS = 1600


def back_kernel(
    plan, me, xt_i, stat_i, h1_i, qk_i, vtok_i, e_i, linv_i, at_i, gm_i, da_i, wqkv, v0, gout, gvec_i,
    sent_o, more_o, mine_o, theirs_o, gain, grads, gvec, grads_o,
):
    j = pl.program_id(0)

    @pl.when(j == 0)
    def _():
        gain[...] = jnp.broadcast_to(as_columns((v0,))[:, 0:1], (WIDTH, BIN))
        grads[...] = jnp.zeros_like(grads)
        gvec[...] = jnp.zeros_like(gvec)

    @pl.when(j < bins_here(plan, me[0]))
    def _():
        ones = jnp.ones((16, BIN), BF)
        blank = jnp.zeros((HEAD_DIM, BIN), BF)
        queries = []
        keys = []
        values = []
        for h in range(HEADS):
            rows = slice(HEAD_DIM * h, HEAD_DIM * h + HEAD_DIM)
            krows = slice(WIDTH + HEAD_DIM * h, WIDTH + HEAD_DIM * h + HEAD_DIM)
            pair = slice(128 * (h // 2), 128 * (h // 2) + 128)
            grad_att = (da_i[rows, :].astype(F32) * linv_i[h : h + 1, :]).astype(BF)
            spread = jnp.concatenate([grad_att, blank] if h % 2 == 0 else [blank, grad_att], 0)
            inner = jnp.sum(grad_att.astype(F32) * at_i[rows, :].astype(F32), 0, keepdims=True)
            weights = e_i[h]
            grad_scores = (weights.astype(F32) * (nn(vtok_i[:, pair], spread) - inner)).astype(BF)
            values.append(nt(grad_att, weights).astype(BF))
            queries.append((nn(qk_i[krows, :], grad_scores) * 0.125).astype(BF))
            keys.append(nt(qk_i[rows, :], grad_scores).astype(BF))
        h1 = h1_i[...]
        grad_h1 = jnp.zeros((WIDTH, BIN), F32)
        for m, parts in enumerate((queries, keys, values)):
            mixed = jnp.concatenate(parts, 0)
            grads[m] += nt(h1, mixed)
            grad_h1 = grad_h1 + nn(wqkv[:, WIDTH * m : WIDTH * m + WIDTH], mixed)
            if m != 1:
                gvec[m] += nt(ones, mixed)
        inverse = stat_i[1:2, :]
        unit = (xt_i[...].astype(F32) - stat_i[0:1, :]) * inverse
        scaled = grad_h1 * gain[...]
        first = jnp.mean(scaled, 0, keepdims=True)
        second = jnp.mean(scaled * unit, 0, keepdims=True)
        result = gm_i[...] + inverse * (scaled - first - unit * second)
        write_wire(j, result.astype(BF), sent_o, more_o)
        gvec[1] += nt(ones, (grad_h1 * unit).astype(BF))
        gvec[3] += nt(ones, grad_h1.astype(BF))

    @pl.when(j == pl.num_programs(0) - 1)
    def _():
        for m in range(3):
            grads_o[WIDTH * m : WIDTH * m + WIDTH, :] = grads[m].astype(BF)
        grads_o[3 * WIDTH : 4 * WIDTH, :] = gout[...]
        rows = [gvec[m][0:1] for m in range(4)] + [gvec_i[0:4, :]]
        grads_o[4 * WIDTH : 4 * WIDTH + 16, :] = jnp.concatenate(rows + [jnp.zeros((8, WIDTH), F32)], 0).astype(BF)
        grads_o[4 * WIDTH + 16 :, :] = jnp.zeros((TAIL_ROWS - 4 * WIDTH - 16, WIDTH), BF)
        half = TAIL_ROWS // 2
        mine_o[...] = grads_o[pl.ds(pl.multiple_of(me[2] * half, 16), half), :]
        theirs_o[...] = grads_o[pl.ds(pl.multiple_of((1 - me[2]) * half, 16), half), :]


def back(plan, me, saved, wqkv, gain, gout, gvec):
    return pl.pallas_call(
        back_kernel,
        grid_spec=pltpu.PrefetchScalarGridSpec(
            num_scalar_prefetch=2,
            grid=(MAX_BINS,),
            in_specs=[
                bin_spec(WIDTH, BIN), bin_spec(8, BIN), bin_spec(WIDTH, BIN), bin_spec(2 * WIDTH, BIN),
                bin_spec(BIN, WIDTH), bin_spec(HEADS, BIN, BIN), bin_spec(8, BIN), bin_spec(WIDTH, BIN),
                bin_spec(WIDTH, BIN), bin_spec(WIDTH, BIN),
                whole(WIDTH, 3 * WIDTH), whole(WIDTH), whole(WIDTH, WIDTH), whole(8, WIDTH),
            ],
            out_specs=[*WIRE_SPECS, *[whole(TAIL_ROWS // 2, WIDTH)] * 2],
            scratch_shapes=[
                pltpu.VMEM((WIDTH, BIN), F32),
                pltpu.VMEM((3, WIDTH, WIDTH), F32),
                pltpu.VMEM((4, 16, WIDTH), F32),
                pltpu.VMEM((TAIL_ROWS, WIDTH), BF),
            ],
        ),
        out_shape=[*WIRE_SHAPES, *[jax.ShapeDtypeStruct((TAIL_ROWS // 2, WIDTH), BF)] * 2],
        compiler_params=pltpu.CompilerParams(vmem_limit_bytes=56 * MIB),
        cost_estimate=pl.CostEstimate(flops=10**6, bytes_accessed=10**5, transcendentals=0),
        name="back",
    )(plan, me, *saved, wqkv, gain, gout, gvec)


UNPACK_IMAGES = 16


def unpack_kernel(
    side, plan, me, own, own_more, before, far_low, far_high, after, more_before, more_far, more_after, base, places, out,
    near, picks, rows, sems,
):
    group = pl.program_id(0)
    bins = before.shape[0]
    low = far_low.shape[0]
    rest = MAX_BINS - bins
    lanes = pl.ds(pl.multiple_of(pl.program_id(1) * 128, 128), 128)
    extra = pl.ds(side * rest, rest)
    pieces = (
        (own, near.at[0, pl.ds(0, bins)]),
        (before, near.at[1, pl.ds(0, bins)]),
        (far_low, near.at[2, pl.ds(0, low)]),
        (far_high, near.at[2, pl.ds(low, bins - low)]),
        (after, near.at[3, pl.ds(0, bins)]),
    )
    more = (
        (own_more, near.at[0, pl.ds(bins, rest)]),
        (more_before.at[extra], near.at[1, pl.ds(bins, rest)]),
        (more_far.at[extra], near.at[2, pl.ds(bins, rest)]),
        (more_after.at[extra], near.at[3, pl.ds(bins, rest)]),
    )
    first = (group == 0) & (pl.program_id(1) == 0)

    @pl.when(first)
    def _():
        for k, (source, target) in enumerate(pieces):
            pltpu.make_async_copy(source, target, sems.at[k]).start()

    @pl.when(first & (plan[3, 0] > 4 * bins))
    def _():
        copies = [pltpu.make_async_copy(*pair, sems.at[5 + k]) for k, pair in enumerate(more)]
        for copy in copies:
            copy.start()
        for copy in copies:
            copy.wait()

    @pl.when(pl.program_id(1) == 0)
    def _():
        flat = places.reshape(SLOTS * UNPACK_IMAGES, 128)
        picks[...] = jnp.zeros_like(picks)
        lane = iota((SLOTS, 128), 1).astype(F32)

        def build(i, carry):
            off = plan[1, group * UNPACK_IMAGES + i].astype(F32)
            spot = flat[pl.ds(i, SLOTS, stride=UNPACK_IMAGES), :] + off
            both = [jnp.where(spot == lane + 128.0 * half, 1.0, 0.0) for half in range(2)]
            picks[i, 0:SLOTS, :] = jnp.concatenate(both, 1).astype(BF)
            return carry

        lax.fori_loop(0, UNPACK_IMAGES, build, 0)

    @pl.when(first)
    def _():
        for k, (source, target) in enumerate(pieces):
            pltpu.make_async_copy(source, target, sems.at[k]).wait()

    for i in range(UNPACK_IMAGES):
        at = plan[0, group * UNPACK_IMAGES + i]
        rows[i] = nn(picks[i], near[(at - me[0]) & 3, at // 4, :, lanes])
    for half in range(2):
        eight = pl.ds(8 * half, 8)
        moved = jnp.swapaxes(rows[eight], 0, 1)[0:SLOTS]
        out[:, eight, :] = jnp.where(places[:, eight, :] >= 0.0, moved, base[:, eight, :].astype(F32))


def unpack(side, plan, me, nears, more, base, places):
    block = (SLOTS, UNPACK_IMAGES, 128)
    return pl.pallas_call(
        functools.partial(unpack_kernel, side),
        grid_spec=pltpu.PrefetchScalarGridSpec(
            num_scalar_prefetch=2,
            grid=(IMAGES // UNPACK_IMAGES, 3),
            in_specs=[pl.BlockSpec(memory_space=pl.ANY)] * 9
            + [
                pl.BlockSpec(block, lambda g, c, *_: (0, g, c)),
                pl.BlockSpec(block, lambda g, c, *_: (0, g, 0)),
            ],
            out_specs=pl.BlockSpec(block, lambda g, c, *_: (0, g, c)),
            scratch_shapes=[
                pltpu.VMEM((4, MAX_BINS, BIN, WIDTH), BF),
                pltpu.VMEM((UNPACK_IMAGES, SLOT_ROWS, BIN), BF),
                pltpu.VMEM((UNPACK_IMAGES, SLOT_ROWS, 128), F32),
                pltpu.SemaphoreType.DMA((9,)),
            ],
        ),
        out_shape=jax.ShapeDtypeStruct((SLOTS, IMAGES, WIDTH), F32),
        compiler_params=pltpu.CompilerParams(vmem_limit_bytes=48 * MIB),
        cost_estimate=pl.CostEstimate(flops=10**6, bytes_accessed=10**5, transcendentals=0),
        name="unpack",
    )(plan, me, *nears, *more, base, places)


PART_PIECE = GROUP_ROWS // 8
TAIL_PIECE = TAIL_ROWS // 8
PIECE = PART_PIECE + TAIL_PIECE


def finish_kernel(
    me, mine, other, w_up, w_down, b_up, w_qkv, w_out, bias_q, gain1, bias_v, shift1, gain2, shift2,
    bias_down, bias_out, part, tail,
):
    x, core = me[1], me[2]
    for k in range(4):
        place = (x + 4 - k) & 3
        for source, own in ((mine, core), (other, 1 - core)):
            at = pl.multiple_of(place * (2 * PART_PIECE) + own * PART_PIECE, 8)
            part[pl.ds(at, PART_PIECE), :] = source[PIECE * k : PIECE * k + PART_PIECE, :].astype(F32)
            at = pl.multiple_of(own * (4 * TAIL_PIECE) + place * TAIL_PIECE, 8)
            tail[pl.ds(at, TAIL_PIECE), :] = source[PIECE * k + PART_PIECE : PIECE * (k + 1), :].astype(F32)
    w_up[...] = part[0:WIDTH, :]
    w_down[...] = part[WIDTH : 2 * WIDTH, :]
    b_up[...] = part[2 * WIDTH : 2 * WIDTH + 1, :].reshape(WIDTH)
    for m in range(3):
        w_qkv[:, WIDTH * m : WIDTH * m + WIDTH] = tail[WIDTH * m : WIDTH * m + WIDTH, :]
    w_out[...] = tail[3 * WIDTH : 4 * WIDTH, :]
    for m, vector in enumerate((bias_q, gain1, bias_v, shift1, gain2, shift2, bias_down, bias_out)):
        vector[...] = tail[4 * WIDTH + m : 4 * WIDTH + m + 1, :].reshape(WIDTH)


def finish(me, mine, other):
    vmem = pl.BlockSpec(memory_space=pltpu.VMEM)
    shapes = [(WIDTH, WIDTH)] * 2 + [(WIDTH,), (WIDTH, 3 * WIDTH), (WIDTH, WIDTH)] + [(WIDTH,)] * 8
    return pl.pallas_call(
        finish_kernel,
        out_shape=[jax.ShapeDtypeStruct(shape, F32) for shape in shapes],
        in_specs=[pl.BlockSpec(memory_space=pltpu.SMEM), vmem, vmem],
        out_specs=[vmem] * len(shapes),
        scratch_shapes=[pltpu.VMEM((GROUP_ROWS, WIDTH), F32), pltpu.VMEM((TAIL_ROWS, WIDTH), F32)],
        compiler_params=pltpu.CompilerParams(vmem_limit_bytes=32 * MIB),
        name="finish",
    )(me, mine, other)


def shift_y(values, by):
    return lax.ppermute(values, "tensor", [(i, (i + by) % 4) for i in range(4)])


def swap_core(values):
    return lax.ppermute(values, "dp", [(i, i ^ 1) for i in range(32)])


def shift_x(values, by):
    return lax.ppermute(values, "dp", [(i, (i + 8 * by) % 32) for i in range(32)])


def shift_z(values, by):
    return lax.ppermute(values, "dp", [(i, i // 8 * 8 + (i + 2 * by) % 8) for i in range(32)])


def add_up(parts):
    total = parts[0].astype(F32)
    for part in parts[1:]:
        total = total + part.astype(F32)
    return total.astype(BF)


def pick_block(values, index, axis, size):
    return lax.dynamic_slice_in_dim(values, index * size, size, axis)


def scatter_x(values, axis):
    part = values.shape[axis] // 4
    x = lax.axis_index("dp") // 8
    own = pick_block(values, x, axis, part)
    return add_up([own] + [shift_x(pick_block(values, (x + d) % 4, axis, part), d) for d in (1, 3, 2)])


def scatter_core(values, axis):
    half = values.shape[axis] // 2
    core = lax.axis_index("dp") % 2
    return add_up([pick_block(values, core, axis, half), swap_core(pick_block(values, 1 - core, axis, half))])


def joined(*values):
    return lax.optimization_barrier(values)


def send_more(plan, out_more, grad_more):
    shape = (2 * (MAX_BINS - SENT_BINS), BIN, WIDTH)

    def send():
        both = jnp.concatenate([out_more, grad_more], 0)
        return tuple(shift_y(both, d) for d in (3, 2, 1))

    def leave():
        anywhere = pl.BlockSpec(memory_space=pl.ANY)
        return pl.pallas_call(
            lambda *refs: None,
            out_shape=[jax.ShapeDtypeStruct(shape, BF)] * 3,
            out_specs=[anywhere] * 3,
            name="leave",
        )()

    return lax.cond(plan[3, 0] > 4 * SENT_BINS, lambda: list(send()), lambda: list(leave()))


def local(
    tokens, keep_mask, norm1_gain, norm1_shift, w_qkv, bias_q, bias_v, w_out, bias_out,
    norm2_gain, norm2_shift, w_up, bias_up, w_down, bias_down, cotangent,
):
    dp = lax.axis_index("dp")
    me = jnp.stack([lax.axis_index("tensor"), dp // 8, dp % 2]).astype(jnp.int32)
    tok = jnp.transpose(tokens, (1, 0, 2))
    cot = jnp.transpose(cotangent, (1, 0, 2))

    own = pack_weights(w_up, w_down, bias_up)
    packs = [own, shift_y(own, 1), shift_y(own, 2), shift_y(own, 3)]
    plan, posm, places = prepare(keep_mask)

    xt, ct, stat, h1, qk, vtok, weights, linv, at, mid = attend(
        plan, me, tok, cot, posm, w_qkv, w_out, (norm1_gain, norm1_shift, bias_q, bias_v, bias_out)
    )
    sent, out_more, grad_mid, grad_att, *parts, gout, gvec = feed(
        plan, me, mid, at, ct, packs, w_out, (norm2_gain, norm2_shift, bias_down)
    )
    after, before = shift_y(sent, 1), shift_y(sent, 3)
    moved = [shift_x(parts[d], d) for d in (1, 3, 2)]
    grad_sent, grad_more, tail, other_tail = back(
        plan, me, (xt, stat, h1, qk, vtok, weights, linv, at, grad_mid, grad_att), w_qkv, norm1_gain, gout, gvec
    )
    after, before, moved[2], grad_sent, grad_more, tail, other_tail = joined(
        after, before, moved[2], grad_sent, grad_more, tail, other_tail
    )

    far_low, far_high = shift_y(after[:LOW_BINS], 1), shift_y(before[LOW_BINS:], 3)
    tail = add_up([tail, swap_core(other_tail)])
    part = add_up([parts[0]] + moved)
    tail, part, far_low, far_high = joined(tail, part, far_low, far_high)

    grad_after, grad_before = shift_y(grad_sent, 1), shift_y(grad_sent, 3)
    tail = scatter_x(tail, 0)
    part = scatter_core(part, 1)
    more = send_more(plan, out_more, grad_more)
    tail, part, *more = joined(tail, part, *more)

    piece = jnp.concatenate([part.reshape(4 * PART_PIECE, WIDTH), tail], 0)
    moved = [shift_z(piece, d) for d in (1, 3, 2)]
    out = unpack(0, plan, me, (sent, out_more, before, far_low, far_high, after), more, tok, places)
    *moved, out, grad_after, grad_before = joined(*moved, out, grad_after, grad_before)

    grad_far_low = shift_y(grad_after[:LOW_BINS], 1)
    grad_far_high = shift_y(grad_before[LOW_BINS:], 3)
    piece = add_up([piece] + moved)

    def toward(d):
        rows = piece[PART_PIECE * d : PART_PIECE * (d + 1)]
        return jnp.concatenate([rows, piece[4 * PART_PIECE :]], 0)

    piece = add_up([toward(0)] + [shift_y(toward(d), 4 - d) for d in (1, 3, 2)])
    piece, grad_far_low, grad_far_high = joined(piece, grad_far_low, grad_far_high)

    moved = [shift_x(piece, d) for d in (1, 2, 3)]
    grad_tokens = unpack(
        1, plan, me, (grad_sent, grad_more, grad_before, grad_far_low, grad_far_high, grad_after), more, cot, places
    )
    *moved, grad_tokens = joined(*moved, grad_tokens)
    mine = jnp.concatenate([piece] + moved, 0)
    other = swap_core(mine)
    (
        grad_up, grad_down, grad_bias_up, grad_qkv, grad_out, grad_bias_q, grad_gain1, grad_bias_v,
        grad_shift1, grad_gain2, grad_shift2, grad_bias_down, grad_bias_out,
    ) = finish(me, mine, other)
    return (
        jnp.transpose(out, (1, 0, 2)), jnp.transpose(grad_tokens, (1, 0, 2)), grad_gain1, grad_shift1,
        grad_qkv, grad_bias_q, grad_bias_v, grad_out, grad_bias_out, grad_gain2, grad_shift2,
        grad_up, grad_bias_up, grad_down, grad_bias_down,
    )


def solution(mesh):
    rows = P("dp", None, None)
    return jax.shard_map(
        local,
        mesh=mesh,
        in_specs=(
            rows, P("dp", None), P(), P(), P(), P(), P(), P(), P(), P(), P(),
            P(None, "tensor"), P("tensor"), P("tensor", None), P(), rows,
        ),
        out_specs=(
            rows, rows, P(), P(), P(), P(), P(), P(), P(), P(), P(),
            P(None, "tensor"), P("tensor"), P("tensor", None), P(),
        ),
        check_vma=False,
    )
```

```python
import functools

import jax
import jax.numpy as jnp
from jax import lax
from jax.experimental import pallas as pl
from jax.experimental.pallas import tpu as pltpu
from jax.sharding import PartitionSpec as P

HEADS = 6
HEAD_DIM = 64
WIDTH = 384
SLOTS = 198
SLOT_ROWS = 208
IMAGES = 32
BIN = 256
HALF = 128
MAX_BINS = 8
EPSILON = 1e-06
SENT_BINS = 5
MASKED = -1e30
ABSENT = -4096.0
MIB = 1024 * 1024
BF = jnp.bfloat16
F32 = jnp.float32
GELU_C = 0.7978845608028654
GELU_A = 0.044715


def nn(left, right):
    return lax.dot_general(left, right, (((1,), (0,)), ((), ())), preferred_element_type=F32)


def nt(left, right):
    return lax.dot_general(left, right, (((1,), (1,)), ((), ())), preferred_element_type=F32)


def iota(shape, dim):
    return lax.broadcasted_iota(jnp.int32, shape, dim)


def eye(size):
    return jnp.where(iota((size, size), 0) == iota((size, size), 1), 1.0, 0.0).astype(BF)


def bins_here(plan, me):
    return (plan[3, 0] - me + 3) // 4


WIRE_SHAPES = [
    jax.ShapeDtypeStruct((SENT_BINS, BIN, WIDTH), BF),
    jax.ShapeDtypeStruct((MAX_BINS - SENT_BINS, BIN, WIDTH), BF),
]


def step_spec(*tail):
    return pl.BlockSpec((None,) + tail, lambda j: (j,) + (0,) * len(tail))


STEP_WIRE_SPECS = [
    pl.BlockSpec((None, BIN, WIDTH), lambda j: (jnp.minimum(j, SENT_BINS - 1), 0, 0)),
    pl.BlockSpec((None, BIN, WIDTH), lambda j: (jnp.maximum(j - SENT_BINS, 0), 0, 0)),
]


def write_wire(j, rows, sent, more):
    wire = nt(eye(BIN), rows).astype(BF)

    @pl.when(j < SENT_BINS)
    def _():
        sent[...] = wire

    @pl.when(j >= SENT_BINS)
    def _():
        more[...] = wire


def add_columns(total, values):
    total[...] += values[:, 0:128] + values[:, 128:]


def column_sums(total):
    return jnp.sum(total.T, 0, keepdims=True)


def as_columns(vectors):
    rows = [v[...].reshape(1, WIDTH) for v in vectors]
    rows.append(jnp.zeros((8 - len(rows), WIDTH), F32))
    return jnp.concatenate(rows, 0).T


def spread_columns(vectors, to):
    columns = as_columns(vectors)
    for m in range(len(vectors)):
        to[m] = jnp.broadcast_to(columns[:, m : m + 1], (WIDTH, BIN))


def row_stats(values):
    mean = jnp.mean(values, 0, keepdims=True)
    centered = values - mean
    inverse = lax.rsqrt(jnp.mean(centered * centered, 0, keepdims=True) + EPSILON)
    return mean, inverse


def prepare_kernel(keep, plan, posm, places, wide, stage, table, order, load, last, sem):
    wide[...] = jnp.zeros_like(wide)
    wide[:, 0:SLOTS] = keep[...]
    kept = wide[...] > 0
    ones = jnp.where(kept, 1.0, 0.0)
    before = jnp.where(iota((BIN, BIN), 0) < iota((BIN, BIN), 1), 1.0, 0.0).astype(BF)
    posm[...] = jnp.where(kept, nn(ones.astype(BF), before), ABSENT)
    count = jnp.broadcast_to(jnp.sum(ones, 1, keepdims=True), (IMAGES, 128))
    across = count.T[0:IMAGES, :]
    down_count = count[:, 0:IMAGES]
    earlier = iota((IMAGES, IMAGES), 1) < iota((IMAGES, IMAGES), 0)
    ahead = (across > down_count) | ((across == down_count) & earlier)
    rank = jnp.sum(jnp.where(ahead, 1.0, 0.0), 1, keepdims=True)
    stage[0] = count.astype(jnp.int32)
    stage[1] = jnp.broadcast_to(rank, (IMAGES, 128)).astype(jnp.int32)
    copy = pltpu.make_async_copy(stage, table, sem)
    copy.start()
    for n in range(SLOT_ROWS):
        places[n] = jnp.broadcast_to(posm[:, n : n + 1], (IMAGES, 128))
    copy.wait()

    def clear(i, carry):
        order[table[1, i, 0]] = i
        load[i] = 0
        plan[4, i] = -1
        plan[5, i] = -1
        return carry

    lax.fori_loop(0, IMAGES, clear, 0)

    def place(k, used):
        image = order[k]
        size = table[0, image, 0]
        found, filled = lax.while_loop(
            lambda c: c[1] + size > BIN,
            lambda c: (c[0] + 1, load[jnp.minimum(c[0] + 1, IMAGES - 1)]),
            (0, load[0]),
        )
        plan[0, image] = found
        plan[1, image] = filled
        plan[2, image] = size

        @pl.when(filled == 0)
        def _():
            plan[4, found] = image

        @pl.when(filled > 0)
        def _():
            plan[5, last[found]] = image

        last[found] = image
        load[found] = filled + size
        return jnp.maximum(used, found + 1)

    plan[3, 0] = lax.fori_loop(0, IMAGES, place, 0)


def pack_kernel(up, down, bias, own):
    own[0:WIDTH, :] = up[...]
    own[WIDTH : 2 * WIDTH, :] = down[...]
    whole_bias = bias[...].reshape(1, WIDTH)
    high = whole_bias.astype(BF).astype(F32)
    middle = (whole_bias - high).astype(BF).astype(F32)
    lowest = whole_bias - high - middle
    rows = jnp.concatenate([high, middle, lowest, jnp.zeros((13, WIDTH), F32)], 0)
    own[2 * WIDTH :, :] = rows.astype(BF)


def pack_weights(up, down, bias):
    vmem = pl.BlockSpec(memory_space=pltpu.VMEM)
    return pl.pallas_call(
        pack_kernel,
        out_shape=jax.ShapeDtypeStruct((2 * WIDTH + 16, WIDTH), BF),
        in_specs=[vmem] * 3,
        out_specs=vmem,
        name="pack",
    )(up, down, bias)


def prepare(keep):
    vmem = pl.BlockSpec(memory_space=pltpu.VMEM)
    return pl.pallas_call(
        prepare_kernel,
        out_shape=[
            jax.ShapeDtypeStruct((6, IMAGES), jnp.int32),
            jax.ShapeDtypeStruct((IMAGES, BIN), F32),
            jax.ShapeDtypeStruct((SLOT_ROWS, IMAGES, 128), F32),
        ],
        in_specs=[vmem],
        out_specs=[pl.BlockSpec(memory_space=pltpu.SMEM), vmem, vmem],
        scratch_shapes=[
            pltpu.VMEM((IMAGES, BIN), jnp.int32),
            pltpu.VMEM((2, IMAGES, 128), jnp.int32),
            pltpu.SMEM((2, IMAGES, 128), jnp.int32),
            pltpu.SMEM((IMAGES,), jnp.int32),
            pltpu.SMEM((IMAGES,), jnp.int32),
            pltpu.SMEM((IMAGES,), jnp.int32),
            pltpu.SemaphoreType.DMA,
        ],
        name="prepare",
    )(keep)


PIECES = [(0, 48), (48, 48), (96, 48), (144, 48), (192, SLOTS - 192)]


def attend_kernel(plan, me, tok, cot, posm, wqkv, wout, v0, v1, v2, v3, v4, *rest):
    results = rest[:10]
    tok_i, cot_i, wqkv_t, wout_t, vecs, both, segr, segc, mask, tok_v, cot_v, step, sems = rest[10:]
    copies = []
    for n, (first, count) in enumerate(PIECES):
        part = pl.ds(first, count)
        for k, (source, target) in enumerate(((tok, tok_v), (cot, cot_v))):
            copies.append(pltpu.make_async_copy(source.at[part], target.at[part], sems.at[k, n]))
    for copy in copies:
        copy.start()
    one = eye(WIDTH)
    for m in range(3):
        cols = slice(WIDTH * m, WIDTH * m + WIDTH)
        wqkv_t[cols, :] = nt(one, wqkv[:, cols]).astype(BF)
    wout_t[...] = nt(one, wout[...]).astype(BF)
    spread_columns((v0, v1, v2, v3, v4), vecs)
    for source in (tok_v, cot_v):
        source[SLOTS:] = jnp.zeros((SLOT_ROWS - SLOTS, IMAGES, WIDTH), BF)
    for n, (first, count) in enumerate(PIECES):
        for k, (source, target) in enumerate(((tok_v, tok_i), (cot_v, cot_i))):
            copies[2 * n + k].wait()

            def turn(m, carry):
                at = pl.ds(pl.multiple_of(first + 16 * m, 16), 16)
                for g in range(0, IMAGES, 16):
                    for c in range(0, WIDTH, 128):
                        part = source[at, g : g + 16, c : c + 128].astype(F32)
                        for h in (0, 8):
                            moved = jnp.swapaxes(part[:, h : h + 8, :], 0, 1)
                            target[g + h : g + h + 8, at, c : c + 128] = moved.astype(BF)
                return carry

            lax.fori_loop(0, (count + 15) // 16, turn, 0)
    step[0] = 0

    def one_bin(xt_o, ct_o, stat_o, h1_o, qk_o, vtok_o, e_o, linv_o, at_o, mid_o):
        j = step[0]
        step[0] = j + 1
        here = 4 * j + me[0]
        lane = iota(segr.shape, 1)
        row = iota(segc.shape, 0)
        segr[...] = jnp.full(segr.shape, -1, jnp.int32)
        segc[...] = jnp.full(segc.shape, -1, jnp.int32)

        def pack(i):
            off = plan[1, i]
            size = plan[2, i]
            target = posm[pl.ds(i, 1), :SLOT_ROWS] + off.astype(F32)
            rows = jnp.concatenate([tok_i[i], cot_i[i]], 1)

            def picked(first, count):
                spots = (iota((count, SLOT_ROWS), 0) + first).astype(F32)
                return nn(jnp.where(spots == target, 1.0, 0.0).astype(BF), rows)

            @pl.when(off == 0)
            def _():
                both[...] = picked(0, BIN)

            @pl.when((off > 0) & (off < HALF))
            def _():
                both[0:HALF, :] += picked(0, HALF)

            @pl.when((off > 0) & (off + size > HALF))
            def _():
                both[HALF:, :] += picked(HALF, HALF)

            segr[...] = jnp.where((lane >= off) & (lane < off + size), i, segr[...])
            segc[...] = jnp.where((row >= off) & (row < off + size), i, segc[...])
            return plan[5, i]

        lax.while_loop(lambda i: i >= 0, pack, plan[4, here])
        same = jnp.concatenate([segc[...], segc[...]], 1) == segr[0:1, :]
        mask[...] = jnp.where(same, 0.0, MASKED)
        ct_o[...] = both[:, WIDTH:].T.astype(BF)
        x = both[:, 0:WIDTH].T
        xt_o[...] = x.astype(BF)
        mean, inverse = row_stats(x)
        stat_o[...] = jnp.concatenate([mean, inverse, jnp.zeros((6, BIN), F32)], 0)
        h1 = ((x - mean) * inverse * vecs[0] + vecs[1]).astype(BF)
        h1_o[...] = h1
        query = ((nn(wqkv_t[0:WIDTH, :], h1) + vecs[2]).astype(BF).astype(F32) * 0.125).astype(BF)
        key = nn(wqkv_t[WIDTH : 2 * WIDTH, :], h1)
        value = nn(wqkv_t[2 * WIDTH :, :], h1) + vecs[3]
        key_tok = key.T.astype(BF)
        vtok_o[...] = value.T.astype(BF)
        value = value.astype(BF)
        qk_o[0:WIDTH, :] = query
        qk_o[WIDTH:, :] = key.astype(BF)
        blank = jnp.zeros((HEAD_DIM, BIN), BF)
        parts = []
        inverses = []
        for h in range(HEADS):
            rows = slice(HEAD_DIM * h, HEAD_DIM * h + HEAD_DIM)
            pair = slice(128 * (h // 2), 128 * (h // 2) + 128)
            own = query[rows, :]
            spread = jnp.concatenate([own, blank] if h % 2 == 0 else [blank, own], 0)
            scores = nn(key_tok[:, pair], spread) + mask[...]
            weights = jnp.exp(scores - jnp.max(scores, 0, keepdims=True))
            low = weights.astype(BF)
            e_o[h] = low
            over = 1.0 / jnp.sum(weights, 0, keepdims=True)
            inverses.append(over)
            parts.append((nn(value[rows, :], low) * over).astype(BF))
        linv_o[...] = jnp.concatenate(inverses + [jnp.zeros((2, BIN), F32)], 0)
        attended = jnp.concatenate(parts, 0)
        at_o[...] = attended
        mid_o[...] = x + (nn(wout_t[...], attended) + vecs[4])

    count = bins_here(plan, me[0])

    @pl.when(count > 0)
    def _():
        specs = [step_spec(*shape) for shape, _ in ATTEND_SHAPES]
        pltpu.emit_pipeline(one_bin, grid=(count,), in_specs=[], out_specs=specs)(*results)


ATTEND_SHAPES = [
    ((WIDTH, BIN), BF), ((WIDTH, BIN), BF), ((8, BIN), F32), ((WIDTH, BIN), BF),
    ((2 * WIDTH, BIN), BF), ((BIN, WIDTH), BF), ((HEADS, BIN, BIN), BF), ((8, BIN), F32),
    ((WIDTH, BIN), BF), ((WIDTH, BIN), F32),
]


def attend(plan, me, tok, cot, posm, wqkv, wout, vectors):
    vmem = pl.BlockSpec(memory_space=pltpu.VMEM)
    smem = pl.BlockSpec(memory_space=pltpu.SMEM)
    anywhere = pl.BlockSpec(memory_space=pl.ANY)
    return pl.pallas_call(
        attend_kernel,
        in_specs=[smem] * 2 + [anywhere] * 2 + [vmem] * 8,
        out_specs=[anywhere] * 10,
        scratch_shapes=[
            pltpu.VMEM((IMAGES, SLOT_ROWS, WIDTH), BF),
            pltpu.VMEM((IMAGES, SLOT_ROWS, WIDTH), BF),
            pltpu.VMEM((3 * WIDTH, WIDTH), BF),
            pltpu.VMEM((WIDTH, WIDTH), BF),
            pltpu.VMEM((5, WIDTH, BIN), F32),
            pltpu.VMEM((BIN, 2 * WIDTH), F32),
            pltpu.VMEM((8, BIN), jnp.int32),
            pltpu.VMEM((BIN, 128), jnp.int32),
            pltpu.VMEM((BIN, BIN), F32),
            pltpu.VMEM((SLOT_ROWS, IMAGES, WIDTH), BF),
            pltpu.VMEM((SLOT_ROWS, IMAGES, WIDTH), BF),
            pltpu.SMEM((1,), jnp.int32),
            pltpu.SemaphoreType.DMA((2, len(PIECES))),
        ],
        out_shape=[jax.ShapeDtypeStruct((MAX_BINS,) + shape, dtype) for shape, dtype in ATTEND_SHAPES],
        compiler_params=pltpu.CompilerParams(vmem_limit_bytes=56 * MIB),
        cost_estimate=pl.CostEstimate(flops=10**6, bytes_accessed=10**5, transcendentals=0),
        name="attend",
    )(plan, me, tok, cot, posm, wqkv, wout, *vectors)


GROUP_ROWS = 832
X_ROWS = GROUP_ROWS // 4
DOWN_ROW = WIDTH + 16


def feed_kernel(
    plan, me, mid, at, ct, w0, w1, w2, w3, wout, v0, v1, v2,
    sent, more, gm, da, p0_o, p1_o, p2_o, p3_o, gout_o, gvec_o,
    up_t, down_t, vecs, biases, grads, gout, gvec, step,
):
    packs = (w0, w1, w2, w3)
    one = eye(WIDTH)
    for d in range(4):
        up_t[d] = nt(one, packs[d][0:WIDTH, :]).astype(BF)
        down_t[d] = nt(one, packs[d][WIDTH : 2 * WIDTH, :]).astype(BF)
        extra = packs[d][2 * WIDTH : 2 * WIDTH + 16, :].astype(F32)
        bias = extra[0:1, :] + extra[1:2, :] + extra[2:3, :]
        column = jnp.broadcast_to(bias, (8, WIDTH)).T
        biases[d] = jnp.broadcast_to(column[:, 0:1], (WIDTH, BIN))
    spread_columns((v0, v1, v2), vecs)
    grads[...] = jnp.zeros_like(grads)
    gout[...] = jnp.zeros_like(gout)
    gvec[...] = jnp.zeros_like(gvec)
    step[0] = 0

    def one_bin(mid_i, at_i, ct_i, sent_o, more_o, gm_o, da_o):
        j = step[0]
        step[0] = j + 1
        ones = jnp.ones((16, BIN), BF)
        middle = mid_i[...]
        mean, inverse = row_stats(middle)
        unit = (middle - mean) * inverse
        h2 = (unit * vecs[0] + vecs[1]).astype(BF)
        h2_ones = jnp.concatenate([h2, ones], 0)
        branch = ct_i[...]
        lowered = vecs[2]
        grad_h2 = jnp.zeros((WIDTH, BIN), F32)
        for d in range(4):
            up = nn(up_t[d], h2) + biases[d]
            square = up * up
            tanh = jnp.tanh(up * (GELU_C * GELU_A * square + GELU_C))
            half = 0.5 * tanh + 0.5
            act = up * half
            slope = half + act * (1.0 - tanh) * (3.0 * GELU_C * GELU_A * square + GELU_C)
            act = act.astype(BF)
            lowered = lowered + nn(down_t[d], act)
            grad_up = (nn(packs[d][WIDTH : 2 * WIDTH, :], branch) * slope).astype(BF)
            grads[d, 0:DOWN_ROW, :] += nt(h2_ones, grad_up)
            if d == 0:
                grads[d, DOWN_ROW : DOWN_ROW + WIDTH + 16, :] += nt(jnp.concatenate([act, ones], 0), branch)
            else:
                grads[d, DOWN_ROW : DOWN_ROW + WIDTH, :] += nt(act, branch)
            grad_h2 = grad_h2 + nn(packs[d][0:WIDTH, :], grad_up)
        result = (middle + lowered).astype(BF)
        write_wire(j, result, sent_o, more_o)
        scaled = grad_h2 * vecs[0]
        first = jnp.mean(scaled, 0, keepdims=True)
        second = jnp.mean(scaled * unit, 0, keepdims=True)
        grad_mid = branch.astype(F32) + inverse * (scaled - first - unit * second)
        gm_o[...] = grad_mid
        low_mid = grad_mid.astype(BF)
        gout[...] += nt(jnp.concatenate([at_i[...], ones], 0), low_mid)
        da_o[...] = nn(wout[...], low_mid).astype(BF)
        add_columns(gvec.at[0], grad_h2 * unit)
        add_columns(gvec.at[1], grad_h2)

    count = bins_here(plan, me[0])

    @pl.when(count > 0)
    def _():
        pltpu.emit_pipeline(
            one_bin,
            grid=(count,),
            in_specs=[step_spec(WIDTH, BIN)] * 3,
            out_specs=[*STEP_WIRE_SPECS, step_spec(WIDTH, BIN), step_spec(WIDTH, BIN)],
        )(mid, at, ct, sent, more, gm, da)

    for d, piece in enumerate((p0_o, p1_o, p2_o, p3_o)):
        rows = pl.ds(pl.multiple_of(((me[1] + d) & 3) * X_ROWS, 8), X_ROWS)
        piece[...] = grads[:, rows, :].astype(BF)
    gout_o[...] = gout[0:WIDTH, :].astype(BF)
    down_bias = grads[0, DOWN_ROW + WIDTH : DOWN_ROW + WIDTH + 1, :]
    rows = [column_sums(gvec[0]), column_sums(gvec[1]), down_bias, gout[WIDTH : WIDTH + 1, :]]
    gvec_o[...] = jnp.concatenate(rows + [jnp.zeros((4, WIDTH), F32)], 0)


def feed(plan, me, mid, at, ct, packs, wout, vectors):
    vmem = pl.BlockSpec(memory_space=pltpu.VMEM)
    smem = pl.BlockSpec(memory_space=pltpu.SMEM)
    anywhere = pl.BlockSpec(memory_space=pl.ANY)
    return pl.pallas_call(
        feed_kernel,
        in_specs=[smem] * 2 + [anywhere] * 3 + [vmem] * 8,
        out_specs=[anywhere] * 4 + [vmem] * 6,
        scratch_shapes=[
            pltpu.VMEM((4, WIDTH, WIDTH), BF),
            pltpu.VMEM((4, WIDTH, WIDTH), BF),
            pltpu.VMEM((3, WIDTH, BIN), F32),
            pltpu.VMEM((4, WIDTH, BIN), F32),
            pltpu.VMEM((4, GROUP_ROWS, WIDTH), F32),
            pltpu.VMEM((WIDTH + 16, WIDTH), F32),
            pltpu.VMEM((2, WIDTH, 128), F32),
            pltpu.SMEM((1,), jnp.int32),
        ],
        out_shape=[
            *WIRE_SHAPES,
            jax.ShapeDtypeStruct((MAX_BINS, WIDTH, BIN), F32),
            jax.ShapeDtypeStruct((MAX_BINS, WIDTH, BIN), BF),
            *[jax.ShapeDtypeStruct((4, X_ROWS, WIDTH), BF)] * 4,
            jax.ShapeDtypeStruct((WIDTH, WIDTH), BF),
            jax.ShapeDtypeStruct((8, WIDTH), F32),
        ],
        compiler_params=pltpu.CompilerParams(vmem_limit_bytes=56 * MIB),
        cost_estimate=pl.CostEstimate(flops=10**6, bytes_accessed=10**5, transcendentals=0),
        name="feed",
    )(plan, me, mid, at, ct, *packs, wout, *vectors)


TAIL_ROWS = 1600


def back_kernel(
    plan, me, xt, stat, h1, qk, vtok, e, linv, at, gm, da, wqkv, v0, gout, gvec_i,
    sent, more, mine_o, theirs_o, gain, grads, gvec, grads_o, step,
):
    gain[...] = jnp.broadcast_to(as_columns((v0,))[:, 0:1], (WIDTH, BIN))
    grads[...] = jnp.zeros_like(grads)
    gvec[...] = jnp.zeros_like(gvec)
    step[0] = 0

    def one_bin(xt_i, stat_i, h1_i, qk_i, vtok_i, e_i, linv_i, at_i, gm_i, da_i, sent_o, more_o):
        j = step[0]
        step[0] = j + 1
        ones = jnp.ones((16, BIN), BF)
        blank = jnp.zeros((HEAD_DIM, BIN), BF)
        queries = []
        keys = []
        values = []
        for h in range(HEADS):
            rows = slice(HEAD_DIM * h, HEAD_DIM * h + HEAD_DIM)
            krows = slice(WIDTH + HEAD_DIM * h, WIDTH + HEAD_DIM * h + HEAD_DIM)
            pair = slice(128 * (h // 2), 128 * (h // 2) + 128)
            grad_att = (da_i[rows, :].astype(F32) * linv_i[h : h + 1, :]).astype(BF)
            spread = jnp.concatenate([grad_att, blank] if h % 2 == 0 else [blank, grad_att], 0)
            inner = jnp.sum(grad_att.astype(F32) * at_i[rows, :].astype(F32), 0, keepdims=True)
            weights = e_i[h]
            grad_scores = (weights.astype(F32) * (nn(vtok_i[:, pair], spread) - inner)).astype(BF)
            values.append(nt(grad_att, weights).astype(BF))
            queries.append((nn(qk_i[krows, :], grad_scores) * 0.125).astype(BF))
            keys.append(nt(qk_i[rows, :], grad_scores).astype(BF))
        h1_ones = jnp.concatenate([h1_i[...], ones], 0)
        grad_h1 = jnp.zeros((WIDTH, BIN), F32)
        for m, parts in enumerate((queries, keys, values)):
            mixed = jnp.concatenate(parts, 0)
            grads[m] += nt(h1_ones, mixed)
            grad_h1 = grad_h1 + nn(wqkv[:, WIDTH * m : WIDTH * m + WIDTH], mixed)
        inverse = stat_i[1:2, :]
        unit = (xt_i[...].astype(F32) - stat_i[0:1, :]) * inverse
        scaled = grad_h1 * gain[...]
        first = jnp.mean(scaled, 0, keepdims=True)
        second = jnp.mean(scaled * unit, 0, keepdims=True)
        result = gm_i[...] + inverse * (scaled - first - unit * second)
        write_wire(j, result.astype(BF), sent_o, more_o)
        add_columns(gvec.at[0], grad_h1 * unit)
        add_columns(gvec.at[1], grad_h1)

    count = bins_here(plan, me[0])

    @pl.when(count > 0)
    def _():
        pltpu.emit_pipeline(
            one_bin,
            grid=(count,),
            in_specs=[
                step_spec(WIDTH, BIN), step_spec(8, BIN), step_spec(WIDTH, BIN), step_spec(2 * WIDTH, BIN),
                step_spec(BIN, WIDTH), step_spec(HEADS, BIN, BIN), step_spec(8, BIN), step_spec(WIDTH, BIN),
                step_spec(WIDTH, BIN), step_spec(WIDTH, BIN),
            ],
            out_specs=STEP_WIRE_SPECS,
        )(xt, stat, h1, qk, vtok, e, linv, at, gm, da, sent, more)

    for m in range(3):
        grads_o[WIDTH * m : WIDTH * m + WIDTH, :] = grads[m, 0:WIDTH, :].astype(BF)
    grads_o[3 * WIDTH : 4 * WIDTH, :] = gout[...]
    query_bias, value_bias = grads[0, WIDTH : WIDTH + 1, :], grads[2, WIDTH : WIDTH + 1, :]
    rows = [query_bias, column_sums(gvec[0]), value_bias, column_sums(gvec[1]), gvec_i[0:4, :]]
    grads_o[4 * WIDTH : 4 * WIDTH + 16, :] = jnp.concatenate(rows + [jnp.zeros((8, WIDTH), F32)], 0).astype(BF)
    grads_o[4 * WIDTH + 16 :, :] = jnp.zeros((TAIL_ROWS - 4 * WIDTH - 16, WIDTH), BF)
    half = TAIL_ROWS // 2
    mine_o[...] = grads_o[pl.ds(pl.multiple_of(me[2] * half, 16), half), :]
    theirs_o[...] = grads_o[pl.ds(pl.multiple_of((1 - me[2]) * half, 16), half), :]


def back(plan, me, saved, wqkv, gain, gout, gvec):
    vmem = pl.BlockSpec(memory_space=pltpu.VMEM)
    smem = pl.BlockSpec(memory_space=pltpu.SMEM)
    anywhere = pl.BlockSpec(memory_space=pl.ANY)
    return pl.pallas_call(
        back_kernel,
        in_specs=[smem] * 2 + [anywhere] * 10 + [vmem] * 4,
        out_specs=[anywhere] * 2 + [vmem] * 2,
        scratch_shapes=[
            pltpu.VMEM((WIDTH, BIN), F32),
            pltpu.VMEM((3, WIDTH + 16, WIDTH), F32),
            pltpu.VMEM((2, WIDTH, 128), F32),
            pltpu.VMEM((TAIL_ROWS, WIDTH), BF),
            pltpu.SMEM((1,), jnp.int32),
        ],
        out_shape=[*WIRE_SHAPES, *[jax.ShapeDtypeStruct((TAIL_ROWS // 2, WIDTH), BF)] * 2],
        compiler_params=pltpu.CompilerParams(vmem_limit_bytes=56 * MIB),
        cost_estimate=pl.CostEstimate(flops=10**6, bytes_accessed=10**5, transcendentals=0),
        name="back",
    )(plan, me, *saved, wqkv, gain, gout, gvec)


UNPACK_IMAGES = 8


def unpack_kernel(
    side, start, plan, me, own, own_more, before, far, after, more_before, more_far, more_after, base, places, *rest,
):
    out, near, columns, rows, sems = rest[-5:]
    group = pl.program_id(0) + start
    bins = before.shape[0]
    rest = MAX_BINS - bins
    extra = pl.ds(side * rest, rest)
    pieces = [(ref, near.at[k, pl.ds(0, bins)]) for k, ref in enumerate((own, before, far, after))]
    more = [(own_more, near.at[0, pl.ds(bins, rest)])] + [
        (ref.at[extra], near.at[k + 1, pl.ds(bins, rest)]) for k, ref in enumerate((more_before, more_far, more_after))
    ]

    @pl.when(group == start)
    def _():
        copies = [pltpu.make_async_copy(*pair, sems.at[k]) for k, pair in enumerate(pieces)]
        for copy in copies:
            copy.start()
        for copy in copies:
            copy.wait()

    @pl.when((group == start) & (plan[3, 0] > 4 * bins))
    def _():
        copies = [pltpu.make_async_copy(*pair, sems.at[4 + k]) for k, pair in enumerate(more)]
        for copy in copies:
            copy.start()
        for copy in copies:
            copy.wait()

    columns[...] = jnp.swapaxes(places[...], 0, 1)
    lane = iota((SLOT_ROWS, 128), 1).astype(F32)
    for i in range(UNPACK_IMAGES):
        at = plan[0, group * UNPACK_IMAGES + i]
        spot = columns[i] + plan[1, group * UNPACK_IMAGES + i].astype(F32)
        pick = [jnp.where(spot == lane + 128.0 * half, 1.0, 0.0) for half in range(2)]
        pick = jnp.concatenate(pick, 1).astype(BF)
        rows[i] = nn(pick, near[(at - me[0]) & 3, at // 4])
    kept = places[0:SLOTS] >= 0.0
    for half in range(2):

        @pl.when((group & 1) == half)
        def _():
            for c in range(3):
                lanes = slice(128 * c, 128 * c + 128)
                moved = jnp.swapaxes(rows[:, :, lanes], 0, 1)[0:SLOTS]
                dropped = base[:, 8 * half : 8 * half + 8, lanes].astype(F32)
                out[:, :, lanes] = jnp.where(kept, moved, dropped)


def unpack(side, start, count, plan, me, nears, more, base, places, rest=()):
    return pl.pallas_call(
        functools.partial(unpack_kernel, side, start),
        grid_spec=pltpu.PrefetchScalarGridSpec(
            num_scalar_prefetch=2,
            grid=(count,),
            in_specs=[pl.BlockSpec(memory_space=pl.ANY)] * 8
            + [
                pl.BlockSpec((SLOTS, 2 * UNPACK_IMAGES, WIDTH), lambda g, *_: (0, (g + start) // 2, 0)),
                pl.BlockSpec((SLOT_ROWS, UNPACK_IMAGES, 128), lambda g, *_: (0, g + start, 0)),
            ]
            + [pl.BlockSpec(memory_space=pl.ANY)] * len(rest),
            out_specs=pl.BlockSpec((SLOTS, UNPACK_IMAGES, WIDTH), lambda g, *_: (0, g + start, 0)),
            scratch_shapes=[
                pltpu.VMEM((4, MAX_BINS, BIN, WIDTH), BF),
                pltpu.VMEM((UNPACK_IMAGES, SLOT_ROWS, 128), F32),
                pltpu.VMEM((UNPACK_IMAGES, SLOT_ROWS, WIDTH), F32),
                pltpu.SemaphoreType.DMA((8,)),
            ],
        ),
        out_shape=jax.ShapeDtypeStruct((SLOTS, IMAGES, WIDTH), F32),
        input_output_aliases={12: 0} if rest else {},
        compiler_params=pltpu.CompilerParams(vmem_limit_bytes=48 * MIB),
        cost_estimate=pl.CostEstimate(flops=10**6, bytes_accessed=10**5, transcendentals=0),
        name="unpack",
    )(plan, me, *nears, *more, base, places, *rest)


PART_PIECE = GROUP_ROWS // 8
TAIL_PIECE = TAIL_ROWS // 8
PIECE = PART_PIECE + TAIL_PIECE


def finish_kernel(
    me, mine, other, w_up, w_down, b_up, w_qkv, w_out, bias_q, gain1, bias_v, shift1, gain2, shift2,
    bias_down, bias_out, part, tail,
):
    x, core = me[1], me[2]
    for k in range(4):
        place = (x + 4 - k) & 3
        for source, own in ((mine, core), (other, 1 - core)):
            at = pl.multiple_of(place * (2 * PART_PIECE) + own * PART_PIECE, 8)
            part[pl.ds(at, PART_PIECE), :] = source[PIECE * k : PIECE * k + PART_PIECE, :].astype(F32)
            at = pl.multiple_of(own * (4 * TAIL_PIECE) + place * TAIL_PIECE, 8)
            tail[pl.ds(at, TAIL_PIECE), :] = source[PIECE * k + PART_PIECE : PIECE * (k + 1), :].astype(F32)
    w_up[...] = part[0:WIDTH, :]
    w_down[...] = part[DOWN_ROW : DOWN_ROW + WIDTH, :]
    b_up[...] = part[WIDTH : WIDTH + 1, :].reshape(WIDTH)
    for m in range(3):
        w_qkv[:, WIDTH * m : WIDTH * m + WIDTH] = tail[WIDTH * m : WIDTH * m + WIDTH, :]
    w_out[...] = tail[3 * WIDTH : 4 * WIDTH, :]
    for m, vector in enumerate((bias_q, gain1, bias_v, shift1, gain2, shift2, bias_down, bias_out)):
        vector[...] = tail[4 * WIDTH + m : 4 * WIDTH + m + 1, :].reshape(WIDTH)


def finish(me, mine, other):
    vmem = pl.BlockSpec(memory_space=pltpu.VMEM)
    shapes = [(WIDTH, WIDTH)] * 2 + [(WIDTH,), (WIDTH, 3 * WIDTH), (WIDTH, WIDTH)] + [(WIDTH,)] * 8
    return pl.pallas_call(
        finish_kernel,
        out_shape=[jax.ShapeDtypeStruct(shape, F32) for shape in shapes],
        in_specs=[pl.BlockSpec(memory_space=pltpu.SMEM), vmem, vmem],
        out_specs=[vmem] * len(shapes),
        scratch_shapes=[pltpu.VMEM((GROUP_ROWS, WIDTH), F32), pltpu.VMEM((TAIL_ROWS, WIDTH), F32)],
        compiler_params=pltpu.CompilerParams(vmem_limit_bytes=32 * MIB),
        name="finish",
    )(me, mine, other)


def shift_y(values, by):
    return lax.ppermute(values, "tensor", [(i, (i + by) % 4) for i in range(4)])


def swap_core(values):
    return lax.ppermute(values, "dp", [(i, i ^ 1) for i in range(32)])


def shift_x(values, by):
    return lax.ppermute(values, "dp", [(i, (i + 8 * by) % 32) for i in range(32)])


def shift_z(values, by):
    return lax.ppermute(values, "dp", [(i, i // 8 * 8 + (i + 2 * by) % 8) for i in range(32)])


def add_up(parts):
    total = parts[0].astype(F32)
    for part in parts[1:]:
        total = total + part.astype(F32)
    return total.astype(BF)


def pick_block(values, index, axis, size):
    return lax.dynamic_slice_in_dim(values, index * size, size, axis)


def scatter_x(values, axis):
    part = values.shape[axis] // 4
    x = lax.axis_index("dp") // 8
    own = pick_block(values, x, axis, part)
    return add_up([own] + [shift_x(pick_block(values, (x + d) % 4, axis, part), d) for d in (1, 3, 2)])


def scatter_core(values, axis):
    half = values.shape[axis] // 2
    core = lax.axis_index("dp") % 2
    return add_up([pick_block(values, core, axis, half), swap_core(pick_block(values, 1 - core, axis, half))])


def joined(*values):
    return lax.optimization_barrier(values)


def send_more(plan, out_more, grad_more):
    shape = (2 * (MAX_BINS - SENT_BINS), BIN, WIDTH)

    def send():
        both = jnp.concatenate([out_more, grad_more], 0)
        return tuple(shift_y(both, d) for d in (3, 2, 1))

    def leave():
        anywhere = pl.BlockSpec(memory_space=pl.ANY)
        return pl.pallas_call(
            lambda *refs: None,
            out_shape=[jax.ShapeDtypeStruct(shape, BF)] * 3,
            out_specs=[anywhere] * 3,
            name="leave",
        )()

    return lax.cond(plan[3, 0] > 4 * SENT_BINS, lambda: list(send()), lambda: list(leave()))


def local(
    tokens, keep_mask, norm1_gain, norm1_shift, w_qkv, bias_q, bias_v, w_out, bias_out,
    norm2_gain, norm2_shift, w_up, bias_up, w_down, bias_down, cotangent,
):
    dp = lax.axis_index("dp")
    me = jnp.stack([lax.axis_index("tensor"), dp // 8, dp % 2]).astype(jnp.int32)
    tok = jnp.transpose(tokens, (1, 0, 2))
    cot = jnp.transpose(cotangent, (1, 0, 2))

    own = pack_weights(w_up, w_down, bias_up)
    packs = [own, shift_y(own, 1), shift_y(own, 2), shift_y(own, 3)]
    plan, posm, places = prepare(keep_mask)

    xt, ct, stat, h1, qk, vtok, weights, linv, at, mid = attend(
        plan, me, tok, cot, posm, w_qkv, w_out, (norm1_gain, norm1_shift, bias_q, bias_v, bias_out)
    )
    sent, out_more, grad_mid, grad_att, *parts, gout, gvec = feed(
        plan, me, mid, at, ct, packs, w_out, (norm2_gain, norm2_shift, bias_down)
    )
    after, before = shift_y(sent, 1), shift_y(sent, 3)
    moved = [shift_x(parts[d], d) for d in (1, 3, 2)]
    grad_sent, grad_more, tail, other_tail = back(
        plan, me, (xt, stat, h1, qk, vtok, weights, linv, at, grad_mid, grad_att), w_qkv, norm1_gain, gout, gvec
    )
    after, before, moved[2], grad_sent, grad_more, tail, other_tail = joined(
        after, before, moved[2], grad_sent, grad_more, tail, other_tail
    )

    far, grad_before = shift_y(after, 1), shift_y(grad_sent, 3)
    tail = add_up([tail, swap_core(other_tail)])
    part = add_up([parts[0]] + moved)
    tail, part = joined(tail, part)

    tail = scatter_x(tail, 0)
    part = scatter_core(part, 1)
    more = send_more(plan, out_more, grad_more)
    tail, part, far, grad_before, *more = joined(tail, part, far, grad_before, *more)

    grad_after, grad_far = shift_y(grad_sent, 1), shift_y(grad_before, 3)
    piece = jnp.concatenate([part.reshape(4 * PART_PIECE, WIDTH), tail], 0)
    moved = [shift_z(piece, d) for d in (1, 3, 2)]
    out = unpack(0, 0, 4, plan, me, (sent, out_more, before, far, after), more, tok, places)
    *moved, out, grad_after, grad_far = joined(*moved, out, grad_after, grad_far)
    piece = add_up([piece] + moved)

    def toward(d):
        rows = piece[PART_PIECE * d : PART_PIECE * (d + 1)]
        return jnp.concatenate([rows, piece[4 * PART_PIECE :]], 0)

    moved = [shift_y(toward(d), 4 - d) for d in (1, 3, 2)]
    grad_nears = (grad_sent, grad_more, grad_before, grad_far, grad_after)
    grad_tokens = unpack(1, 0, 2, plan, me, grad_nears, more, cot, places)
    *moved, grad_tokens = joined(*moved, grad_tokens)
    piece = add_up([toward(0)] + moved)
    moved = [shift_x(piece, d) for d in (1, 2, 3)]
    grad_tokens = unpack(1, 2, 2, plan, me, grad_nears, more, cot, places, (grad_tokens,))
    *moved, grad_tokens = joined(*moved, grad_tokens)
    mine = jnp.concatenate([piece] + moved, 0)
    other = swap_core(mine)
    (
        grad_up, grad_down, grad_bias_up, grad_qkv, grad_out, grad_bias_q, grad_gain1, grad_bias_v,
        grad_shift1, grad_gain2, grad_shift2, grad_bias_down, grad_bias_out,
    ) = finish(me, mine, other)
    return (
        jnp.transpose(out, (1, 0, 2)), jnp.transpose(grad_tokens, (1, 0, 2)), grad_gain1, grad_shift1,
        grad_qkv, grad_bias_q, grad_bias_v, grad_out, grad_bias_out, grad_gain2, grad_shift2,
        grad_up, grad_bias_up, grad_down, grad_bias_down,
    )


def solution(mesh):
    rows = P("dp", None, None)
    return jax.shard_map(
        local,
        mesh=mesh,
        in_specs=(
            rows, P("dp", None), P(), P(), P(), P(), P(), P(), P(), P(), P(),
            P(None, "tensor"), P("tensor"), P("tensor", None), P(), rows,
        ),
        out_specs=(
            rows, rows, P(), P(), P(), P(), P(), P(), P(), P(), P(),
            P(None, "tensor"), P("tensor"), P("tensor", None), P(),
        ),
        check_vma=False,
    )
```

```python
import functools

import jax
import jax.numpy as jnp
from jax import lax
from jax.experimental import pallas as pl
from jax.experimental.pallas import tpu as pltpu
from jax.sharding import PartitionSpec as P

HEADS = 6
HEAD_DIM = 64
WIDTH = 384
SLOTS = 198
SLOT_ROWS = 208
IMAGES = 32
BIN = 256
HALF = 128
MAX_BINS = 8
EPSILON = 1e-06
SENT_BINS = 5
MASKED = -1e30
ABSENT = -4096.0
MIB = 1024 * 1024
BF = jnp.bfloat16
F32 = jnp.float32
GELU_C = 0.7978845608028654
GELU_A = 0.044715


def nn(left, right):
    return lax.dot_general(left, right, (((1,), (0,)), ((), ())), preferred_element_type=F32)


def nt(left, right):
    return lax.dot_general(left, right, (((1,), (1,)), ((), ())), preferred_element_type=F32)


def iota(shape, dim):
    return lax.broadcasted_iota(jnp.int32, shape, dim)


def eye(size):
    return jnp.where(iota((size, size), 0) == iota((size, size), 1), 1.0, 0.0).astype(BF)


def bins_here(plan, me):
    return (plan[3, 0] - me + 3) // 4


WIRE_SHAPES = [
    jax.ShapeDtypeStruct((SENT_BINS, BIN, WIDTH), BF),
    jax.ShapeDtypeStruct((MAX_BINS - SENT_BINS, BIN, WIDTH), BF),
]


def step_spec(*tail):
    return pl.BlockSpec((None,) + tail, lambda j: (j,) + (0,) * len(tail))


STEP_WIRE_SPECS = [
    pl.BlockSpec((None, BIN, WIDTH), lambda j: (jnp.minimum(j, SENT_BINS - 1), 0, 0)),
    pl.BlockSpec((None, BIN, WIDTH), lambda j: (jnp.maximum(j - SENT_BINS, 0), 0, 0)),
]


def write_wire(j, rows, sent, more):
    wire = nt(eye(BIN), rows).astype(BF)

    @pl.when(j < SENT_BINS)
    def _():
        sent[...] = wire

    @pl.when(j >= SENT_BINS)
    def _():
        more[...] = wire


def add_columns(total, values):
    total[...] += values[:, 0:128] + values[:, 128:]


def column_sums(total):
    return jnp.sum(total.T, 0, keepdims=True)


def as_columns(vectors):
    rows = [v[...].reshape(1, WIDTH) for v in vectors]
    rows.append(jnp.zeros((8 - len(rows), WIDTH), F32))
    return jnp.concatenate(rows, 0).T


def spread_columns(vectors, to):
    columns = as_columns(vectors)
    for m in range(len(vectors)):
        to[m] = jnp.broadcast_to(columns[:, m : m + 1], (WIDTH, BIN))


def row_stats(values):
    mean = jnp.mean(values, 0, keepdims=True)
    centered = values - mean
    inverse = lax.rsqrt(jnp.mean(centered * centered, 0, keepdims=True) + EPSILON)
    return mean, inverse


def prepare_kernel(keep, plan, used, posm, wide, stage, table, order, load, last, sem):
    wide[...] = jnp.zeros_like(wide)
    wide[:, 0:SLOTS] = keep[...]
    kept = wide[...] > 0
    ones = jnp.where(kept, 1.0, 0.0)
    before = jnp.where(iota((BIN, BIN), 0) < iota((BIN, BIN), 1), 1.0, 0.0).astype(BF)
    posm[...] = jnp.where(kept, nn(ones.astype(BF), before), ABSENT)
    count = jnp.broadcast_to(jnp.sum(ones, 1, keepdims=True), (IMAGES, 128))
    across = count.T[0:IMAGES, :]
    down_count = count[:, 0:IMAGES]
    earlier = iota((IMAGES, IMAGES), 1) < iota((IMAGES, IMAGES), 0)
    ahead = (across > down_count) | ((across == down_count) & earlier)
    rank = jnp.sum(jnp.where(ahead, 1.0, 0.0), 1, keepdims=True)
    stage[0] = count.astype(jnp.int32)
    stage[1] = jnp.broadcast_to(rank, (IMAGES, 128)).astype(jnp.int32)
    copy = pltpu.make_async_copy(stage, table, sem)
    copy.start()
    copy.wait()

    def clear(i, carry):
        order[table[1, i, 0]] = i
        load[i] = 0
        plan[4, i] = -1
        plan[5, i] = -1
        return carry

    lax.fori_loop(0, IMAGES, clear, 0)

    def place(k, most):
        image = order[k]
        size = table[0, image, 0]
        begin = jnp.where(size > HALF, k, 0)
        found, filled = lax.while_loop(
            lambda c: c[1] + size > BIN,
            lambda c: (c[0] + 1, load[jnp.minimum(c[0] + 1, IMAGES - 1)]),
            (begin, load[begin]),
        )
        plan[0, image] = found
        plan[1, image] = filled
        plan[2, image] = size

        @pl.when(filled == 0)
        def _():
            plan[4, found] = image

        @pl.when(filled > 0)
        def _():
            plan[5, last[found]] = image

        last[found] = image
        load[found] = filled + size
        return jnp.maximum(most, found + 1)

    bins = lax.fori_loop(0, IMAGES, place, 0)
    plan[3, 0] = bins
    used[0] = bins


def pack_kernel(up, down, bias, own):
    own[0:WIDTH, :] = up[...]
    own[WIDTH : 2 * WIDTH, :] = down[...]
    whole_bias = bias[...].reshape(1, WIDTH)
    high = whole_bias.astype(BF).astype(F32)
    middle = (whole_bias - high).astype(BF).astype(F32)
    lowest = whole_bias - high - middle
    rows = jnp.concatenate([high, middle, lowest, jnp.zeros((13, WIDTH), F32)], 0)
    own[2 * WIDTH :, :] = rows.astype(BF)


def pack_weights(up, down, bias):
    vmem = pl.BlockSpec(memory_space=pltpu.VMEM)
    return pl.pallas_call(
        pack_kernel,
        out_shape=jax.ShapeDtypeStruct((2 * WIDTH + 16, WIDTH), BF),
        in_specs=[vmem] * 3,
        out_specs=vmem,
        name="pack",
    )(up, down, bias)


def prepare(keep):
    vmem = pl.BlockSpec(memory_space=pltpu.VMEM)
    return pl.pallas_call(
        prepare_kernel,
        out_shape=[
            jax.ShapeDtypeStruct((6, IMAGES), jnp.int32),
            jax.ShapeDtypeStruct((1,), jnp.int32),
            jax.ShapeDtypeStruct((IMAGES, BIN), F32),
        ],
        in_specs=[vmem],
        out_specs=[pl.BlockSpec(memory_space=pltpu.SMEM)] * 2 + [vmem],
        scratch_shapes=[
            pltpu.VMEM((IMAGES, BIN), jnp.int32),
            pltpu.VMEM((2, IMAGES, 128), jnp.int32),
            pltpu.SMEM((2, IMAGES, 128), jnp.int32),
            pltpu.SMEM((IMAGES,), jnp.int32),
            pltpu.SMEM((IMAGES,), jnp.int32),
            pltpu.SMEM((IMAGES,), jnp.int32),
            pltpu.SemaphoreType.DMA,
        ],
        name="prepare",
    )(keep)


PIECES = [(0, 48), (48, 48), (96, 48), (144, 48), (192, SLOTS - 192)]


def attend_kernel(plan, me, tok, cot, posm, wqkv, wout, v0, v1, v2, v3, v4, *rest):
    results = rest[:10]
    tok_i, cot_i, wqkv_t, wout_t, vecs, both, segr, segc, mask, tok_v, cot_v, step, sems = rest[10:]
    copies = []
    for n, (first, count) in enumerate(PIECES):
        part = pl.ds(first, count)
        for k, (source, target) in enumerate(((tok, tok_v), (cot, cot_v))):
            copies.append(pltpu.make_async_copy(source.at[part], target.at[part], sems.at[k, n]))
    for copy in copies:
        copy.start()
    one = eye(WIDTH)
    for m in range(3):
        cols = slice(WIDTH * m, WIDTH * m + WIDTH)
        wqkv_t[cols, :] = nt(one, wqkv[:, cols]).astype(BF)
    wout_t[...] = nt(one, wout[...]).astype(BF)
    spread_columns((v0, v1, v2, v3, v4), vecs)
    for source in (tok_v, cot_v):
        source[SLOTS:] = jnp.zeros((SLOT_ROWS - SLOTS, IMAGES, WIDTH), BF)
    for n, (first, count) in enumerate(PIECES):
        for k, (source, target) in enumerate(((tok_v, tok_i), (cot_v, cot_i))):
            copies[2 * n + k].wait()

            def turn(m, carry):
                at = pl.ds(pl.multiple_of(first + 16 * m, 16), 16)
                for g in range(0, IMAGES, 16):
                    for c in range(0, WIDTH, 128):
                        part = source[at, g : g + 16, c : c + 128].astype(F32)
                        for h in (0, 8):
                            moved = jnp.swapaxes(part[:, h : h + 8, :], 0, 1)
                            target[g + h : g + h + 8, at, c : c + 128] = moved.astype(BF)
                return carry

            lax.fori_loop(0, (count + 15) // 16, turn, 0)
    step[0] = 0

    def one_bin(xt_o, ct_o, stat_o, h1_o, qk_o, vtok_o, e_o, linv_o, at_o, mid_o):
        j = step[0]
        step[0] = j + 1
        here = 4 * j + me[0]
        lane = iota(segr.shape, 1)
        row = iota(segc.shape, 0)
        segr[...] = jnp.full(segr.shape, -1, jnp.int32)
        segc[...] = jnp.full(segc.shape, -1, jnp.int32)

        def pack(i):
            off = plan[1, i]
            size = plan[2, i]
            target = posm[pl.ds(i, 1), :SLOT_ROWS] + off.astype(F32)
            rows = jnp.concatenate([tok_i[i], cot_i[i]], 1)

            def picked(first, count):
                spots = (iota((count, SLOT_ROWS), 0) + first).astype(F32)
                return nn(jnp.where(spots == target, 1.0, 0.0).astype(BF), rows)

            @pl.when(off == 0)
            def _():
                both[...] = picked(0, BIN)

            @pl.when((off > 0) & (off < HALF))
            def _():
                both[0:HALF, :] += picked(0, HALF)

            @pl.when((off > 0) & (off + size > HALF))
            def _():
                both[HALF:, :] += picked(HALF, HALF)

            segr[...] = jnp.where((lane >= off) & (lane < off + size), i, segr[...])
            segc[...] = jnp.where((row >= off) & (row < off + size), i, segc[...])
            return plan[5, i]

        lax.while_loop(lambda i: i >= 0, pack, plan[4, here])
        same = jnp.concatenate([segc[...], segc[...]], 1) == segr[0:1, :]
        mask[...] = jnp.where(same, 0.0, MASKED)
        ct_o[...] = both[:, WIDTH:].T.astype(BF)
        x = both[:, 0:WIDTH].T
        xt_o[...] = x.astype(BF)
        mean, inverse = row_stats(x)
        stat_o[...] = jnp.concatenate([mean, inverse, jnp.zeros((6, BIN), F32)], 0)
        h1 = ((x - mean) * inverse * vecs[0] + vecs[1]).astype(BF)
        h1_o[...] = h1
        query = ((nn(wqkv_t[0:WIDTH, :], h1) + vecs[2]).astype(BF).astype(F32) * 0.125).astype(BF)
        key = nn(wqkv_t[WIDTH : 2 * WIDTH, :], h1)
        value = nn(wqkv_t[2 * WIDTH :, :], h1) + vecs[3]
        key_tok = key.T.astype(BF)
        vtok_o[...] = value.T.astype(BF)
        value = value.astype(BF)
        qk_o[0:WIDTH, :] = query
        qk_o[WIDTH:, :] = key.astype(BF)
        blank = jnp.zeros((HEAD_DIM, BIN), BF)
        parts = []
        inverses = []
        for h in range(HEADS):
            rows = slice(HEAD_DIM * h, HEAD_DIM * h + HEAD_DIM)
            pair = slice(128 * (h // 2), 128 * (h // 2) + 128)
            own = query[rows, :]
            spread = jnp.concatenate([own, blank] if h % 2 == 0 else [blank, own], 0)
            scores = nn(key_tok[:, pair], spread) + mask[...]
            weights = jnp.exp(scores - jnp.max(scores, 0, keepdims=True))
            low = weights.astype(BF)
            e_o[h] = low
            over = 1.0 / jnp.sum(weights, 0, keepdims=True)
            inverses.append(over)
            parts.append((nn(value[rows, :], low) * over).astype(BF))
        linv_o[...] = jnp.concatenate(inverses + [jnp.zeros((2, BIN), F32)], 0)
        attended = jnp.concatenate(parts, 0)
        at_o[...] = attended
        mid_o[...] = x + (nn(wout_t[...], attended) + vecs[4])

    count = bins_here(plan, me[0])

    @pl.when(count > 0)
    def _():
        specs = [step_spec(*shape) for shape, _ in ATTEND_SHAPES]
        pltpu.emit_pipeline(one_bin, grid=(count,), in_specs=[], out_specs=specs)(*results)


ATTEND_SHAPES = [
    ((WIDTH, BIN), BF), ((WIDTH, BIN), BF), ((8, BIN), F32), ((WIDTH, BIN), BF),
    ((2 * WIDTH, BIN), BF), ((BIN, WIDTH), BF), ((HEADS, BIN, BIN), BF), ((8, BIN), F32),
    ((WIDTH, BIN), BF), ((WIDTH, BIN), F32),
]


def attend(plan, me, tok, cot, posm, wqkv, wout, vectors):
    vmem = pl.BlockSpec(memory_space=pltpu.VMEM)
    smem = pl.BlockSpec(memory_space=pltpu.SMEM)
    anywhere = pl.BlockSpec(memory_space=pl.ANY)
    return pl.pallas_call(
        attend_kernel,
        in_specs=[smem] * 2 + [anywhere] * 2 + [vmem] * 8,
        out_specs=[anywhere] * 10,
        scratch_shapes=[
            pltpu.VMEM((IMAGES, SLOT_ROWS, WIDTH), BF),
            pltpu.VMEM((IMAGES, SLOT_ROWS, WIDTH), BF),
            pltpu.VMEM((3 * WIDTH, WIDTH), BF),
            pltpu.VMEM((WIDTH, WIDTH), BF),
            pltpu.VMEM((5, WIDTH, BIN), F32),
            pltpu.VMEM((BIN, 2 * WIDTH), F32),
            pltpu.VMEM((8, BIN), jnp.int32),
            pltpu.VMEM((BIN, 128), jnp.int32),
            pltpu.VMEM((BIN, BIN), F32),
            pltpu.VMEM((SLOT_ROWS, IMAGES, WIDTH), BF),
            pltpu.VMEM((SLOT_ROWS, IMAGES, WIDTH), BF),
            pltpu.SMEM((1,), jnp.int32),
            pltpu.SemaphoreType.DMA((2, len(PIECES))),
        ],
        out_shape=[jax.ShapeDtypeStruct((MAX_BINS,) + shape, dtype) for shape, dtype in ATTEND_SHAPES],
        compiler_params=pltpu.CompilerParams(vmem_limit_bytes=56 * MIB),
        cost_estimate=pl.CostEstimate(flops=10**6, bytes_accessed=10**5, transcendentals=0),
        name="attend",
    )(plan, me, tok, cot, posm, wqkv, wout, *vectors)


GROUP_ROWS = 768
X_ROWS = GROUP_ROWS // 4


def feed_kernel(
    plan, me, mid, at, ct, w0, w1, w2, w3, wout, v0, v1, v2,
    sent, more, gm, da, p0_o, p1_o, p2_o, p3_o, gout_o, gvec_o,
    up_t, down_t, up_all, down_all, vecs, biases, ups, gacts, acts, gups, up_sum, down_sum, gout, gvec, group, step,
):
    packs = (w0, w1, w2, w3)
    one = eye(WIDTH)
    for d in range(4):
        cols = slice(WIDTH * d, WIDTH * d + WIDTH)
        up_all[:, cols] = packs[d][0:WIDTH, :]
        down_all[cols, :] = packs[d][WIDTH : 2 * WIDTH, :]
        up_t[cols, :] = nt(one, packs[d][0:WIDTH, :]).astype(BF)
        down_t[:, cols] = nt(one, packs[d][WIDTH : 2 * WIDTH, :]).astype(BF)
        extra = packs[d][2 * WIDTH : 2 * WIDTH + 16, :].astype(F32)
        bias = extra[0:1, :] + extra[1:2, :] + extra[2:3, :]
        column = jnp.broadcast_to(bias, (8, WIDTH)).T
        biases[d] = jnp.broadcast_to(column[:, 0:1], (WIDTH, BIN))
    spread_columns((v0, v1, v2), vecs)
    up_sum[...] = jnp.zeros_like(up_sum)
    down_sum[...] = jnp.zeros_like(down_sum)
    gout[...] = jnp.zeros_like(gout)
    gvec[...] = jnp.zeros_like(gvec)
    step[0] = 0

    def one_bin(mid_i, at_i, ct_i, sent_o, more_o, gm_o, da_o):
        j = step[0]
        step[0] = j + 1
        ones = jnp.ones((16, BIN), BF)
        middle = mid_i[...]
        mean, inverse = row_stats(middle)
        unit = (middle - mean) * inverse
        h2 = (unit * vecs[0] + vecs[1]).astype(BF)
        branch = ct_i[...]
        ups[...] = nn(up_t[...], h2)
        gacts[...] = nn(down_all[...], branch)
        for d in range(4):
            cols = slice(WIDTH * d, WIDTH * d + WIDTH)
            up = ups[cols, :] + biases[d]
            square = up * up
            tanh = jnp.tanh(up * (GELU_C * GELU_A * square + GELU_C))
            half = 0.5 * tanh + 0.5
            act = up * half
            slope = half + act * (1.0 - tanh) * (3.0 * GELU_C * GELU_A * square + GELU_C)
            acts[cols, :] = act.astype(BF)
            grad_up = gacts[cols, :] * slope
            add_columns(gvec.at[3 + d], grad_up)
            gups[cols, :] = grad_up.astype(BF)
        grad_h2 = nn(up_all[...], gups[...])
        result = (middle + (nn(down_t[...], acts[...]) + vecs[2])).astype(BF)
        up_sum[...] += nt(gups[...], h2)
        down_sum[...] += nt(acts[...], branch)
        write_wire(j, result, sent_o, more_o)
        scaled = grad_h2 * vecs[0]
        first = jnp.mean(scaled, 0, keepdims=True)
        second = jnp.mean(scaled * unit, 0, keepdims=True)
        grad_mid = branch.astype(F32) + inverse * (scaled - first - unit * second)
        gm_o[...] = grad_mid
        low_mid = grad_mid.astype(BF)
        gout[...] += nt(jnp.concatenate([at_i[...], ones], 0), low_mid)
        da_o[...] = nn(wout[...], low_mid).astype(BF)
        add_columns(gvec.at[0], grad_h2 * unit)
        add_columns(gvec.at[1], grad_h2)
        add_columns(gvec.at[2], branch.astype(F32))

    count = bins_here(plan, me[0])

    @pl.when(count > 0)
    def _():
        pltpu.emit_pipeline(
            one_bin,
            grid=(count,),
            in_specs=[step_spec(WIDTH, BIN)] * 3,
            out_specs=[*STEP_WIRE_SPECS, step_spec(WIDTH, BIN), step_spec(WIDTH, BIN)],
        )(mid, at, ct, sent, more, gm, da)

    for d in range(4):
        cols = slice(WIDTH * d, WIDTH * d + WIDTH)
        group[d, 0:WIDTH, :] = up_sum[cols, :].astype(BF)
        group[d, WIDTH : 2 * WIDTH, :] = down_sum[cols, :].astype(BF)
    for d, piece in enumerate((p0_o, p1_o, p2_o, p3_o)):
        rows = pl.ds(pl.multiple_of(((me[1] + d) & 3) * X_ROWS, 16), X_ROWS)
        piece[...] = group[:, rows, :]
    gout_o[...] = gout[0:WIDTH, :].astype(BF)
    rows = [column_sums(gvec[m]) for m in range(3)] + [gout[WIDTH : WIDTH + 1, :]]
    gvec_o[...] = jnp.concatenate(rows + [jnp.zeros((4, WIDTH), F32)], 0)
    for d in range(4):
        gvec_o[pl.ds(4 + ((me[0] + 4 - d) & 3), 1), :] = column_sums(gvec[3 + d])


def feed(plan, me, mid, at, ct, packs, wout, vectors):
    vmem = pl.BlockSpec(memory_space=pltpu.VMEM)
    smem = pl.BlockSpec(memory_space=pltpu.SMEM)
    anywhere = pl.BlockSpec(memory_space=pl.ANY)
    return pl.pallas_call(
        feed_kernel,
        in_specs=[smem] * 2 + [anywhere] * 3 + [vmem] * 8,
        out_specs=[anywhere] * 4 + [vmem] * 6,
        scratch_shapes=[
            pltpu.VMEM((4 * WIDTH, WIDTH), BF),
            pltpu.VMEM((WIDTH, 4 * WIDTH), BF),
            pltpu.VMEM((WIDTH, 4 * WIDTH), BF),
            pltpu.VMEM((4 * WIDTH, WIDTH), BF),
            pltpu.VMEM((3, WIDTH, BIN), F32),
            pltpu.VMEM((4, WIDTH, BIN), F32),
            pltpu.VMEM((4 * WIDTH, BIN), F32),
            pltpu.VMEM((4 * WIDTH, BIN), F32),
            pltpu.VMEM((4 * WIDTH, BIN), BF),
            pltpu.VMEM((4 * WIDTH, BIN), BF),
            pltpu.VMEM((4 * WIDTH, WIDTH), F32),
            pltpu.VMEM((4 * WIDTH, WIDTH), F32),
            pltpu.VMEM((WIDTH + 16, WIDTH), F32),
            pltpu.VMEM((7, WIDTH, 128), F32),
            pltpu.VMEM((4, GROUP_ROWS, WIDTH), BF),
            pltpu.SMEM((1,), jnp.int32),
        ],
        out_shape=[
            *WIRE_SHAPES,
            jax.ShapeDtypeStruct((MAX_BINS, WIDTH, BIN), F32),
            jax.ShapeDtypeStruct((MAX_BINS, WIDTH, BIN), BF),
            *[jax.ShapeDtypeStruct((4, X_ROWS, WIDTH), BF)] * 4,
            jax.ShapeDtypeStruct((WIDTH, WIDTH), BF),
            jax.ShapeDtypeStruct((8, WIDTH), F32),
        ],
        compiler_params=pltpu.CompilerParams(vmem_limit_bytes=56 * MIB),
        cost_estimate=pl.CostEstimate(flops=10**6, bytes_accessed=10**5, transcendentals=0),
        name="feed",
    )(plan, me, mid, at, ct, *packs, wout, *vectors)


TAIL_ROWS = 1600


def back_kernel(
    plan, me, xt, stat, h1, qk, vtok, e, linv, at, gm, da, wqkv, v0, gout, gvec_i,
    sent, more, mine_o, theirs_o, gain, grads, gvec, grads_o, step,
):
    gain[...] = jnp.broadcast_to(as_columns((v0,))[:, 0:1], (WIDTH, BIN))
    grads[...] = jnp.zeros_like(grads)
    gvec[...] = jnp.zeros_like(gvec)
    step[0] = 0

    def one_bin(xt_i, stat_i, h1_i, qk_i, vtok_i, e_i, linv_i, at_i, gm_i, da_i, sent_o, more_o):
        j = step[0]
        step[0] = j + 1
        ones = jnp.ones((16, BIN), BF)
        blank = jnp.zeros((HEAD_DIM, BIN), BF)
        queries = []
        keys = []
        values = []
        for h in range(HEADS):
            rows = slice(HEAD_DIM * h, HEAD_DIM * h + HEAD_DIM)
            krows = slice(WIDTH + HEAD_DIM * h, WIDTH + HEAD_DIM * h + HEAD_DIM)
            pair = slice(128 * (h // 2), 128 * (h // 2) + 128)
            grad_att = (da_i[rows, :].astype(F32) * linv_i[h : h + 1, :]).astype(BF)
            spread = jnp.concatenate([grad_att, blank] if h % 2 == 0 else [blank, grad_att], 0)
            inner = jnp.sum(grad_att.astype(F32) * at_i[rows, :].astype(F32), 0, keepdims=True)
            weights = e_i[h]
            grad_scores = (weights.astype(F32) * (nn(vtok_i[:, pair], spread) - inner)).astype(BF)
            values.append(nt(grad_att, weights).astype(BF))
            queries.append((nn(qk_i[krows, :], grad_scores) * 0.125).astype(BF))
            keys.append(nt(qk_i[rows, :], grad_scores).astype(BF))
        h1_ones = jnp.concatenate([h1_i[...], ones], 0)
        grad_h1 = jnp.zeros((WIDTH, BIN), F32)
        for m, parts in enumerate((queries, keys, values)):
            mixed = jnp.concatenate(parts, 0)
            grads[m] += nt(h1_ones, mixed)
            grad_h1 = grad_h1 + nn(wqkv[:, WIDTH * m : WIDTH * m + WIDTH], mixed)
        inverse = stat_i[1:2, :]
        unit = (xt_i[...].astype(F32) - stat_i[0:1, :]) * inverse
        scaled = grad_h1 * gain[...]
        first = jnp.mean(scaled, 0, keepdims=True)
        second = jnp.mean(scaled * unit, 0, keepdims=True)
        result = gm_i[...] + inverse * (scaled - first - unit * second)
        write_wire(j, result.astype(BF), sent_o, more_o)
        add_columns(gvec.at[0], grad_h1 * unit)
        add_columns(gvec.at[1], grad_h1)

    count = bins_here(plan, me[0])

    @pl.when(count > 0)
    def _():
        pltpu.emit_pipeline(
            one_bin,
            grid=(count,),
            in_specs=[
                step_spec(WIDTH, BIN), step_spec(8, BIN), step_spec(WIDTH, BIN), step_spec(2 * WIDTH, BIN),
                step_spec(BIN, WIDTH), step_spec(HEADS, BIN, BIN), step_spec(8, BIN), step_spec(WIDTH, BIN),
                step_spec(WIDTH, BIN), step_spec(WIDTH, BIN),
            ],
            out_specs=STEP_WIRE_SPECS,
        )(xt, stat, h1, qk, vtok, e, linv, at, gm, da, sent, more)

    for m in range(3):
        grads_o[WIDTH * m : WIDTH * m + WIDTH, :] = grads[m, 0:WIDTH, :].astype(BF)
    grads_o[3 * WIDTH : 4 * WIDTH, :] = gout[...]
    query_bias, value_bias = grads[0, WIDTH : WIDTH + 1, :], grads[2, WIDTH : WIDTH + 1, :]
    rows = [query_bias, column_sums(gvec[0]), value_bias, column_sums(gvec[1]), gvec_i[...]]
    grads_o[4 * WIDTH : 4 * WIDTH + 16, :] = jnp.concatenate(rows + [jnp.zeros((4, WIDTH), F32)], 0).astype(BF)
    grads_o[4 * WIDTH + 16 :, :] = jnp.zeros((TAIL_ROWS - 4 * WIDTH - 16, WIDTH), BF)
    half = TAIL_ROWS // 2
    mine_o[...] = grads_o[pl.ds(pl.multiple_of(me[2] * half, 16), half), :]
    theirs_o[...] = grads_o[pl.ds(pl.multiple_of((1 - me[2]) * half, 16), half), :]


def back(plan, me, saved, wqkv, gain, gout, gvec):
    vmem = pl.BlockSpec(memory_space=pltpu.VMEM)
    smem = pl.BlockSpec(memory_space=pltpu.SMEM)
    anywhere = pl.BlockSpec(memory_space=pl.ANY)
    return pl.pallas_call(
        back_kernel,
        in_specs=[smem] * 2 + [anywhere] * 10 + [vmem] * 4,
        out_specs=[anywhere] * 2 + [vmem] * 2,
        scratch_shapes=[
            pltpu.VMEM((WIDTH, BIN), F32),
            pltpu.VMEM((3, WIDTH + 16, WIDTH), F32),
            pltpu.VMEM((2, WIDTH, 128), F32),
            pltpu.VMEM((TAIL_ROWS, WIDTH), BF),
            pltpu.SMEM((1,), jnp.int32),
        ],
        out_shape=[*WIRE_SHAPES, *[jax.ShapeDtypeStruct((TAIL_ROWS // 2, WIDTH), BF)] * 2],
        compiler_params=pltpu.CompilerParams(vmem_limit_bytes=56 * MIB),
        cost_estimate=pl.CostEstimate(flops=10**6, bytes_accessed=10**5, transcendentals=0),
        name="back",
    )(plan, me, *saved, wqkv, gain, gout, gvec)


UNPACK_IMAGES = 8


def unpack_kernel(
    side, start, plan, me, own, own_more, before, far, after, more_before, more_far, more_after, base, posm, *rest,
):
    out, near, columns, rows, sems = rest[-5:]
    group = pl.program_id(0) + start
    bins = before.shape[0]
    rest = MAX_BINS - bins
    extra = pl.ds(side * rest, rest)
    pieces = [(ref, near.at[k, pl.ds(0, bins)]) for k, ref in enumerate((own, before, far, after))]
    more = [(own_more, near.at[0, pl.ds(bins, rest)])] + [
        (ref.at[extra], near.at[k + 1, pl.ds(bins, rest)]) for k, ref in enumerate((more_before, more_far, more_after))
    ]

    @pl.when(group == start)
    def _():
        copies = [pltpu.make_async_copy(*pair, sems.at[k]) for k, pair in enumerate(pieces)]
        for copy in copies:
            copy.start()
        for copy in copies:
            copy.wait()

    @pl.when((group == start) & (plan[3, 0] > 4 * bins))
    def _():
        copies = [pltpu.make_async_copy(*pair, sems.at[4 + k]) for k, pair in enumerate(more)]
        for copy in copies:
            copy.start()
        for copy in copies:
            copy.wait()

    turned = posm[...].T
    for i in range(UNPACK_IMAGES):
        columns[i] = jnp.broadcast_to(turned[0:SLOT_ROWS, i : i + 1], (SLOT_ROWS, 128))
    lane = iota((SLOT_ROWS, 128), 1).astype(F32)
    for i in range(UNPACK_IMAGES):
        at = plan[0, group * UNPACK_IMAGES + i]
        spot = columns[i] + plan[1, group * UNPACK_IMAGES + i].astype(F32)
        pick = [jnp.where(spot == lane + 128.0 * half, 1.0, 0.0) for half in range(2)]
        pick = jnp.concatenate(pick, 1).astype(BF)
        rows[i] = nn(pick, near[(at - me[0]) & 3, at // 4])
    kept = jnp.swapaxes(columns[...], 0, 1)[0:SLOTS] >= 0.0
    for half in range(2):

        @pl.when((group & 1) == half)
        def _():
            for c in range(3):
                lanes = slice(128 * c, 128 * c + 128)
                moved = jnp.swapaxes(rows[:, :, lanes], 0, 1)[0:SLOTS]
                dropped = base[:, 8 * half : 8 * half + 8, lanes].astype(F32)
                out[:, :, lanes] = jnp.where(kept, moved, dropped)


def unpack(side, start, count, plan, me, nears, more, base, posm, rest=()):
    return pl.pallas_call(
        functools.partial(unpack_kernel, side, start),
        grid_spec=pltpu.PrefetchScalarGridSpec(
            num_scalar_prefetch=2,
            grid=(count,),
            in_specs=[pl.BlockSpec(memory_space=pl.ANY)] * 8
            + [
                pl.BlockSpec((SLOTS, 2 * UNPACK_IMAGES, WIDTH), lambda g, *_: (0, (g + start) // 2, 0)),
                pl.BlockSpec((UNPACK_IMAGES, BIN), lambda g, *_: (g + start, 0)),
            ]
            + [pl.BlockSpec(memory_space=pl.ANY)] * len(rest),
            out_specs=pl.BlockSpec((SLOTS, UNPACK_IMAGES, WIDTH), lambda g, *_: (0, g + start, 0)),
            scratch_shapes=[
                pltpu.VMEM((4, MAX_BINS, BIN, WIDTH), BF),
                pltpu.VMEM((UNPACK_IMAGES, SLOT_ROWS, 128), F32),
                pltpu.VMEM((UNPACK_IMAGES, SLOT_ROWS, WIDTH), F32),
                pltpu.SemaphoreType.DMA((8,)),
            ],
        ),
        out_shape=jax.ShapeDtypeStruct((SLOTS, IMAGES, WIDTH), F32),
        input_output_aliases={12: 0} if rest else {},
        compiler_params=pltpu.CompilerParams(vmem_limit_bytes=48 * MIB),
        cost_estimate=pl.CostEstimate(flops=10**6, bytes_accessed=10**5, transcendentals=0),
        name="unpack",
    )(plan, me, *nears, *more, base, posm, *rest)


PART_PIECE = GROUP_ROWS // 8
TAIL_PIECE = TAIL_ROWS // 8
PIECE = PART_PIECE + TAIL_PIECE


def finish_kernel(
    me, mine, other, w_up, w_down, b_up, w_qkv, w_out, bias_q, gain1, bias_v, shift1, gain2, shift2,
    bias_down, bias_out, part, tail,
):
    x, core = me[1], me[2]
    for k in range(4):
        place = (x + 4 - k) & 3
        for source, own in ((mine, core), (other, 1 - core)):
            at = pl.multiple_of(place * (2 * PART_PIECE) + own * PART_PIECE, 8)
            part[pl.ds(at, PART_PIECE), :] = source[PIECE * k : PIECE * k + PART_PIECE, :].astype(F32)
            at = pl.multiple_of(own * (4 * TAIL_PIECE) + place * TAIL_PIECE, 8)
            tail[pl.ds(at, TAIL_PIECE), :] = source[PIECE * k + PART_PIECE : PIECE * (k + 1), :].astype(F32)
    w_up[...] = part[0:WIDTH, :].T
    w_down[...] = part[WIDTH : 2 * WIDTH, :]
    b_up[...] = tail[pl.ds(4 * WIDTH + 8 + me[0], 1), :].reshape(WIDTH)
    for m in range(3):
        w_qkv[:, WIDTH * m : WIDTH * m + WIDTH] = tail[WIDTH * m : WIDTH * m + WIDTH, :]
    w_out[...] = tail[3 * WIDTH : 4 * WIDTH, :]
    for m, vector in enumerate((bias_q, gain1, bias_v, shift1, gain2, shift2, bias_down, bias_out)):
        vector[...] = tail[4 * WIDTH + m : 4 * WIDTH + m + 1, :].reshape(WIDTH)


def finish(me, mine, other):
    vmem = pl.BlockSpec(memory_space=pltpu.VMEM)
    shapes = [(WIDTH, WIDTH)] * 2 + [(WIDTH,), (WIDTH, 3 * WIDTH), (WIDTH, WIDTH)] + [(WIDTH,)] * 8
    return pl.pallas_call(
        finish_kernel,
        out_shape=[jax.ShapeDtypeStruct(shape, F32) for shape in shapes],
        in_specs=[pl.BlockSpec(memory_space=pltpu.SMEM), vmem, vmem],
        out_specs=[vmem] * len(shapes),
        scratch_shapes=[pltpu.VMEM((GROUP_ROWS, WIDTH), F32), pltpu.VMEM((TAIL_ROWS, WIDTH), F32)],
        compiler_params=pltpu.CompilerParams(vmem_limit_bytes=32 * MIB),
        name="finish",
    )(me, mine, other)


def shift_y(values, by):
    return lax.ppermute(values, "tensor", [(i, (i + by) % 4) for i in range(4)])


def swap_core(values):
    return lax.ppermute(values, "dp", [(i, i ^ 1) for i in range(32)])


def shift_x(values, by):
    return lax.ppermute(values, "dp", [(i, (i + 8 * by) % 32) for i in range(32)])


def shift_z(values, by):
    return lax.ppermute(values, "dp", [(i, i // 8 * 8 + (i + 2 * by) % 8) for i in range(32)])


def add_up(parts):
    total = parts[0].astype(F32)
    for part in parts[1:]:
        total = total + part.astype(F32)
    return total.astype(BF)


def pick_block(values, index, axis, size):
    return lax.dynamic_slice_in_dim(values, index * size, size, axis)


def scatter_x(values, axis):
    part = values.shape[axis] // 4
    x = lax.axis_index("dp") // 8
    own = pick_block(values, x, axis, part)
    return add_up([own] + [shift_x(pick_block(values, (x + d) % 4, axis, part), d) for d in (1, 3, 2)])


def scatter_core(values, axis):
    half = values.shape[axis] // 2
    core = lax.axis_index("dp") % 2
    return add_up([pick_block(values, core, axis, half), swap_core(pick_block(values, 1 - core, axis, half))])


def joined(*values):
    return lax.optimization_barrier(values)


def send_more(used, out_more, grad_more):
    shape = (2 * (MAX_BINS - SENT_BINS), BIN, WIDTH)

    def send():
        both = jnp.concatenate([out_more, grad_more], 0)
        return tuple(shift_y(both, d) for d in (3, 2, 1))

    def leave():
        anywhere = pl.BlockSpec(memory_space=pl.ANY)
        return pl.pallas_call(
            lambda *refs: None,
            out_shape=[jax.ShapeDtypeStruct(shape, BF)] * 3,
            out_specs=[anywhere] * 3,
            name="leave",
        )()

    return lax.cond(used[0] > 4 * SENT_BINS, lambda: list(send()), lambda: list(leave()))


def local(
    tokens, keep_mask, norm1_gain, norm1_shift, w_qkv, bias_q, bias_v, w_out, bias_out,
    norm2_gain, norm2_shift, w_up, bias_up, w_down, bias_down, cotangent,
):
    dp = lax.axis_index("dp")
    me = jnp.stack([lax.axis_index("tensor"), dp // 8, dp % 2]).astype(jnp.int32)
    tok = jnp.transpose(tokens, (1, 0, 2))
    cot = jnp.transpose(cotangent, (1, 0, 2))

    own = pack_weights(w_up, w_down, bias_up)
    packs = [own, shift_y(own, 1), shift_y(own, 2), shift_y(own, 3)]
    plan, used, posm = prepare(keep_mask)

    xt, ct, stat, h1, qk, vtok, weights, linv, at, mid = attend(
        plan, me, tok, cot, posm, w_qkv, w_out, (norm1_gain, norm1_shift, bias_q, bias_v, bias_out)
    )
    sent, out_more, grad_mid, grad_att, *parts, gout, gvec = feed(
        plan, me, mid, at, ct, packs, w_out, (norm2_gain, norm2_shift, bias_down)
    )
    after, before = shift_y(sent, 1), shift_y(sent, 3)
    moved = [shift_x(parts[d], d) for d in (1, 3, 2)]
    grad_sent, grad_more, tail, other_tail = back(
        plan, me, (xt, stat, h1, qk, vtok, weights, linv, at, grad_mid, grad_att), w_qkv, norm1_gain, gout, gvec
    )
    after, before, moved[2], grad_sent, grad_more, tail, other_tail = joined(
        after, before, moved[2], grad_sent, grad_more, tail, other_tail
    )

    far, grad_before = shift_y(after, 1), shift_y(grad_sent, 3)
    tail = add_up([tail, swap_core(other_tail)])
    part = add_up([parts[0]] + moved)
    tail, part = joined(tail, part)

    tail = scatter_x(tail, 0)
    part = scatter_core(part, 1)
    more = send_more(used, out_more, grad_more)
    tail, part, far, grad_before, *more = joined(tail, part, far, grad_before, *more)

    grad_after, grad_far = shift_y(grad_sent, 1), shift_y(grad_before, 3)
    piece = jnp.concatenate([part.reshape(4 * PART_PIECE, WIDTH), tail], 0)
    moved = [shift_z(piece, d) for d in (1, 3, 2)]
    out = unpack(0, 0, 4, plan, me, (sent, out_more, before, far, after), more, tok, posm)
    *moved, out, grad_after, grad_far = joined(*moved, out, grad_after, grad_far)
    piece = add_up([piece] + moved)

    def toward(d):
        rows = piece[PART_PIECE * d : PART_PIECE * (d + 1)]
        return jnp.concatenate([rows, piece[4 * PART_PIECE :]], 0)

    moved = [shift_y(toward(d), 4 - d) for d in (1, 3, 2)]
    grad_nears = (grad_sent, grad_more, grad_before, grad_far, grad_after)
    grad_tokens = unpack(1, 0, 2, plan, me, grad_nears, more, cot, posm)
    *moved, grad_tokens = joined(*moved, grad_tokens)
    piece = add_up([toward(0)] + moved)
    moved = [shift_x(piece, d) for d in (1, 2, 3)]
    grad_tokens = unpack(1, 2, 2, plan, me, grad_nears, more, cot, posm, (grad_tokens,))
    *moved, grad_tokens = joined(*moved, grad_tokens)
    mine = jnp.concatenate([piece] + moved, 0)
    other = swap_core(mine)
    (
        grad_up, grad_down, grad_bias_up, grad_qkv, grad_out, grad_bias_q, grad_gain1, grad_bias_v,
        grad_shift1, grad_gain2, grad_shift2, grad_bias_down, grad_bias_out,
    ) = finish(me, mine, other)
    return (
        jnp.transpose(out, (1, 0, 2)), jnp.transpose(grad_tokens, (1, 0, 2)), grad_gain1, grad_shift1,
        grad_qkv, grad_bias_q, grad_bias_v, grad_out, grad_bias_out, grad_gain2, grad_shift2,
        grad_up, grad_bias_up, grad_down, grad_bias_down,
    )


def solution(mesh):
    rows = P("dp", None, None)
    return jax.shard_map(
        local,
        mesh=mesh,
        in_specs=(
            rows, P("dp", None), P(), P(), P(), P(), P(), P(), P(), P(), P(),
            P(None, "tensor"), P("tensor"), P("tensor", None), P(), rows,
        ),
        out_specs=(
            rows, rows, P(), P(), P(), P(), P(), P(), P(), P(), P(),
            P(None, "tensor"), P("tensor"), P("tensor", None), P(),
        ),
        check_vma=False,
    )
```

```python
import functools

import jax
import jax.numpy as jnp
from jax import lax
from jax.experimental import pallas as pl
from jax.experimental.pallas import tpu as pltpu
from jax.sharding import PartitionSpec as P

HEADS = 6
HEAD_DIM = 64
WIDTH = 384
SLOTS = 198
SLOT_ROWS = 208
IMAGES = 32
BIN = 256
HALF = 128
MAX_BINS = 8
EPSILON = 1e-06
SENT_BINS = 5
MASKED = -1e30
ABSENT = -4096.0
MIB = 1024 * 1024
BF = jnp.bfloat16
F32 = jnp.float32
GELU_C = 0.7978845608028654
GELU_A = 0.044715


def nn(left, right):
    return lax.dot_general(left, right, (((1,), (0,)), ((), ())), preferred_element_type=F32)


def nt(left, right):
    return lax.dot_general(left, right, (((1,), (1,)), ((), ())), preferred_element_type=F32)


def iota(shape, dim):
    return lax.broadcasted_iota(jnp.int32, shape, dim)


def eye(size):
    return jnp.where(iota((size, size), 0) == iota((size, size), 1), 1.0, 0.0).astype(BF)


def bins_here(plan, me):
    return (plan[3, 0] - me + 3) // 4


WIRE_SHAPES = [
    jax.ShapeDtypeStruct((SENT_BINS, BIN, WIDTH), BF),
    jax.ShapeDtypeStruct((MAX_BINS - SENT_BINS, BIN, WIDTH), BF),
]


def step_spec(*tail):
    return pl.BlockSpec((None,) + tail, lambda j: (j,) + (0,) * len(tail))


STEP_WIRE_SPECS = [
    pl.BlockSpec((None, BIN, WIDTH), lambda j: (jnp.minimum(j, SENT_BINS - 1), 0, 0)),
    pl.BlockSpec((None, BIN, WIDTH), lambda j: (jnp.maximum(j - SENT_BINS, 0), 0, 0)),
]


def write_wire(j, rows, sent, more):
    wire = rows.T.astype(BF)

    @pl.when(j < SENT_BINS)
    def _():
        sent[...] = wire

    @pl.when(j >= SENT_BINS)
    def _():
        more[...] = wire


def add_columns(total, values):
    total[...] += values[:, 0:128] + values[:, 128:]


def column_sums(total):
    return jnp.sum(total.T, 0, keepdims=True)


def as_columns(vectors):
    rows = [v[...].reshape(1, WIDTH) for v in vectors]
    rows.append(jnp.zeros((8 - len(rows), WIDTH), F32))
    return jnp.concatenate(rows, 0).T


def spread_columns(vectors, to):
    columns = as_columns(vectors)
    for m in range(len(vectors)):
        to[m] = jnp.broadcast_to(columns[:, m : m + 1], (WIDTH, BIN))


def row_stats(values):
    mean = jnp.mean(values, 0, keepdims=True)
    centered = values - mean
    inverse = lax.rsqrt(jnp.mean(centered * centered, 0, keepdims=True) + EPSILON)
    return mean, inverse


def prepare_kernel(keep, plan, used, posm, wide, stage, table, order, load, last, sem):
    wide[...] = jnp.zeros_like(wide)
    wide[:, 0:SLOTS] = keep[...]
    kept = wide[...] > 0
    ones = jnp.where(kept, 1.0, 0.0)
    before = jnp.where(iota((BIN, BIN), 0) < iota((BIN, BIN), 1), 1.0, 0.0).astype(BF)
    posm[...] = jnp.where(kept, nn(ones.astype(BF), before), ABSENT)
    count = jnp.broadcast_to(jnp.sum(ones, 1, keepdims=True), (IMAGES, 128))
    across = count.T[0:IMAGES, :]
    down_count = count[:, 0:IMAGES]
    earlier = iota((IMAGES, IMAGES), 1) < iota((IMAGES, IMAGES), 0)
    ahead = (across > down_count) | ((across == down_count) & earlier)
    rank = jnp.sum(jnp.where(ahead, 1.0, 0.0), 1, keepdims=True)
    stage[0] = count.astype(jnp.int32)
    stage[1] = jnp.broadcast_to(rank, (IMAGES, 128)).astype(jnp.int32)
    copy = pltpu.make_async_copy(stage, table, sem)
    copy.start()
    copy.wait()

    def clear(i, carry):
        order[table[1, i, 0]] = i
        load[i] = 0
        plan[4, i] = -1
        plan[5, i] = -1
        return carry

    lax.fori_loop(0, IMAGES, clear, 0)

    def place(k, most):
        image = order[k]
        size = table[0, image, 0]
        begin = jnp.where(size > HALF, k, 0)
        found, filled = lax.while_loop(
            lambda c: c[1] + size > BIN,
            lambda c: (c[0] + 1, load[jnp.minimum(c[0] + 1, IMAGES - 1)]),
            (begin, load[begin]),
        )
        plan[0, image] = found
        plan[1, image] = filled
        plan[2, image] = size

        @pl.when(filled == 0)
        def _():
            plan[4, found] = image

        @pl.when(filled > 0)
        def _():
            plan[5, last[found]] = image

        last[found] = image
        load[found] = filled + size
        return jnp.maximum(most, found + 1)

    bins = lax.fori_loop(0, IMAGES, place, 0)
    plan[3, 0] = bins
    used[0] = bins


def pack_kernel(up, down, bias, own):
    own[0:WIDTH, :] = up[...]
    own[WIDTH : 2 * WIDTH, :] = down[...]
    whole_bias = bias[...].reshape(1, WIDTH)
    high = whole_bias.astype(BF).astype(F32)
    middle = (whole_bias - high).astype(BF).astype(F32)
    lowest = whole_bias - high - middle
    rows = jnp.concatenate([high, middle, lowest, jnp.zeros((13, WIDTH), F32)], 0)
    own[2 * WIDTH :, :] = rows.astype(BF)


def pack_weights(up, down, bias):
    vmem = pl.BlockSpec(memory_space=pltpu.VMEM)
    return pl.pallas_call(
        pack_kernel,
        out_shape=jax.ShapeDtypeStruct((2 * WIDTH + 16, WIDTH), BF),
        in_specs=[vmem] * 3,
        out_specs=vmem,
        name="pack",
    )(up, down, bias)


def prepare(keep):
    vmem = pl.BlockSpec(memory_space=pltpu.VMEM)
    return pl.pallas_call(
        prepare_kernel,
        out_shape=[
            jax.ShapeDtypeStruct((6, IMAGES), jnp.int32),
            jax.ShapeDtypeStruct((1,), jnp.int32),
            jax.ShapeDtypeStruct((IMAGES, BIN), F32),
        ],
        in_specs=[vmem],
        out_specs=[pl.BlockSpec(memory_space=pltpu.SMEM)] * 2 + [vmem],
        scratch_shapes=[
            pltpu.VMEM((IMAGES, BIN), jnp.int32),
            pltpu.VMEM((2, IMAGES, 128), jnp.int32),
            pltpu.SMEM((2, IMAGES, 128), jnp.int32),
            pltpu.SMEM((IMAGES,), jnp.int32),
            pltpu.SMEM((IMAGES,), jnp.int32),
            pltpu.SMEM((IMAGES,), jnp.int32),
            pltpu.SemaphoreType.DMA,
        ],
        name="prepare",
    )(keep)


PIECES = [(0, 48), (48, 48), (96, 48), (144, 48), (192, SLOTS - 192)]


def attend_kernel(plan, me, tok, cot, posm, wqkv, wout, v0, v1, v2, v3, v4, *rest):
    results = rest[:10]
    tok_i, cot_i, wqkv_t, wout_t, vecs, both, segr, segc, mask, tok_v, cot_v, step, sems = rest[10:]
    copies = []
    for n, (first, count) in enumerate(PIECES):
        part = pl.ds(first, count)
        for k, (source, target) in enumerate(((tok, tok_v), (cot, cot_v))):
            copies.append(pltpu.make_async_copy(source.at[part], target.at[part], sems.at[k, n]))
    for copy in copies:
        copy.start()
    one = eye(WIDTH)
    for m in range(3):
        cols = slice(WIDTH * m, WIDTH * m + WIDTH)
        wqkv_t[cols, :] = nt(one, wqkv[:, cols]).astype(BF)
    wout_t[...] = nt(one, wout[...]).astype(BF)
    spread_columns((v0, v1, v2, v3, v4), vecs)
    for source in (tok_v, cot_v):
        source[SLOTS:] = jnp.zeros((SLOT_ROWS - SLOTS, IMAGES, WIDTH), BF)
    for n, (first, count) in enumerate(PIECES):
        for k, (source, target) in enumerate(((tok_v, tok_i), (cot_v, cot_i))):
            copies[2 * n + k].wait()

            def turn(m, carry):
                at = pl.ds(pl.multiple_of(first + 16 * m, 16), 16)
                for g in range(0, IMAGES, 16):
                    for c in range(0, WIDTH, 128):
                        part = source[at, g : g + 16, c : c + 128].astype(F32)
                        for h in (0, 8):
                            moved = jnp.swapaxes(part[:, h : h + 8, :], 0, 1)
                            target[g + h : g + h + 8, at, c : c + 128] = moved.astype(BF)
                return carry

            lax.fori_loop(0, (count + 15) // 16, turn, 0)
    step[0] = 0

    def one_bin(xt_o, ct_o, stat_o, h1_o, qk_o, vtok_o, e_o, linv_o, at_o, mid_o):
        j = step[0]
        step[0] = j + 1
        here = 4 * j + me[0]
        lane = iota(segr.shape, 1)
        row = iota(segc.shape, 0)
        segr[...] = jnp.full(segr.shape, -1, jnp.int32)
        segc[...] = jnp.full(segc.shape, -1, jnp.int32)

        def pack(i):
            off = plan[1, i]
            size = plan[2, i]
            target = posm[pl.ds(i, 1), :SLOT_ROWS] + off.astype(F32)
            rows = jnp.concatenate([tok_i[i], cot_i[i]], 1)

            def picked(first, count):
                spots = (iota((count, SLOT_ROWS), 0) + first).astype(F32)
                return nn(jnp.where(spots == target, 1.0, 0.0).astype(BF), rows)

            @pl.when(off == 0)
            def _():
                both[...] = picked(0, BIN)

            @pl.when((off > 0) & (off < HALF))
            def _():
                both[0:HALF, :] += picked(0, HALF)

            @pl.when((off > 0) & (off + size > HALF))
            def _():
                both[HALF:, :] += picked(HALF, HALF)

            segr[...] = jnp.where((lane >= off) & (lane < off + size), i, segr[...])
            segc[...] = jnp.where((row >= off) & (row < off + size), i, segc[...])
            return plan[5, i]

        lax.while_loop(lambda i: i >= 0, pack, plan[4, here])
        same = jnp.concatenate([segc[...], segc[...]], 1) == segr[0:1, :]
        mask[...] = jnp.where(same, 0.0, MASKED)
        ct_o[...] = both[:, WIDTH:].T.astype(BF)
        x = both[:, 0:WIDTH].T
        xt_o[...] = x.astype(BF)
        mean, inverse = row_stats(x)
        stat_o[...] = jnp.concatenate([mean, inverse, jnp.zeros((6, BIN), F32)], 0)
        h1 = ((x - mean) * inverse * vecs[0] + vecs[1]).astype(BF)
        h1_o[...] = h1
        query = ((nn(wqkv_t[0:WIDTH, :], h1) + vecs[2]).astype(BF).astype(F32) * 0.125).astype(BF)
        key = nn(wqkv_t[WIDTH : 2 * WIDTH, :], h1)
        value = nn(wqkv_t[2 * WIDTH :, :], h1) + vecs[3]
        key_tok = key.T.astype(BF)
        vtok_o[...] = value.T.astype(BF)
        value = value.astype(BF)
        qk_o[0:WIDTH, :] = query
        qk_o[WIDTH:, :] = key.astype(BF)
        blank = jnp.zeros((HEAD_DIM, BIN), BF)
        parts = []
        inverses = []
        for h in range(HEADS):
            rows = slice(HEAD_DIM * h, HEAD_DIM * h + HEAD_DIM)
            pair = slice(128 * (h // 2), 128 * (h // 2) + 128)
            own = query[rows, :]
            spread = jnp.concatenate([own, blank] if h % 2 == 0 else [blank, own], 0)
            scores = nn(key_tok[:, pair], spread) + mask[...]
            weights = jnp.exp(scores - jnp.max(scores, 0, keepdims=True))
            low = weights.astype(BF)
            e_o[h] = low
            over = 1.0 / jnp.sum(weights, 0, keepdims=True)
            inverses.append(over)
            parts.append((nn(value[rows, :], low) * over).astype(BF))
        linv_o[...] = jnp.concatenate(inverses + [jnp.zeros((2, BIN), F32)], 0)
        attended = jnp.concatenate(parts, 0)
        at_o[...] = attended
        mid_o[...] = x + (nn(wout_t[...], attended) + vecs[4])

    count = bins_here(plan, me[0])

    @pl.when(count > 0)
    def _():
        specs = [step_spec(*shape) for shape, _ in ATTEND_SHAPES]
        pltpu.emit_pipeline(one_bin, grid=(count,), in_specs=[], out_specs=specs)(*results)


ATTEND_SHAPES = [
    ((WIDTH, BIN), BF), ((WIDTH, BIN), BF), ((8, BIN), F32), ((WIDTH, BIN), BF),
    ((2 * WIDTH, BIN), BF), ((BIN, WIDTH), BF), ((HEADS, BIN, BIN), BF), ((8, BIN), F32),
    ((WIDTH, BIN), BF), ((WIDTH, BIN), F32),
]


def attend(plan, me, tok, cot, posm, wqkv, wout, vectors):
    vmem = pl.BlockSpec(memory_space=pltpu.VMEM)
    smem = pl.BlockSpec(memory_space=pltpu.SMEM)
    anywhere = pl.BlockSpec(memory_space=pl.ANY)
    return pl.pallas_call(
        attend_kernel,
        in_specs=[smem] * 2 + [anywhere] * 2 + [vmem] * 8,
        out_specs=[anywhere] * 10,
        scratch_shapes=[
            pltpu.VMEM((IMAGES, SLOT_ROWS, WIDTH), BF),
            pltpu.VMEM((IMAGES, SLOT_ROWS, WIDTH), BF),
            pltpu.VMEM((3 * WIDTH, WIDTH), BF),
            pltpu.VMEM((WIDTH, WIDTH), BF),
            pltpu.VMEM((5, WIDTH, BIN), F32),
            pltpu.VMEM((BIN, 2 * WIDTH), F32),
            pltpu.VMEM((8, BIN), jnp.int32),
            pltpu.VMEM((BIN, 128), jnp.int32),
            pltpu.VMEM((BIN, BIN), F32),
            pltpu.VMEM((SLOT_ROWS, IMAGES, WIDTH), BF),
            pltpu.VMEM((SLOT_ROWS, IMAGES, WIDTH), BF),
            pltpu.SMEM((1,), jnp.int32),
            pltpu.SemaphoreType.DMA((2, len(PIECES))),
        ],
        out_shape=[jax.ShapeDtypeStruct((MAX_BINS,) + shape, dtype) for shape, dtype in ATTEND_SHAPES],
        compiler_params=pltpu.CompilerParams(vmem_limit_bytes=56 * MIB),
        cost_estimate=pl.CostEstimate(flops=10**6, bytes_accessed=10**5, transcendentals=0),
        name="attend",
    )(plan, me, tok, cot, posm, wqkv, wout, *vectors)


GROUP_ROWS = 768
X_ROWS = GROUP_ROWS // 4


def feed_kernel(
    plan, me, mid, at, ct, w0, w1, w2, w3, wout, v0, v1, v2,
    sent, more, gm, da, p0_o, p1_o, p2_o, p3_o, gout_o, gvec_o,
    up_t, down_t, up_all, down_all, vecs, biases, ups, gacts, acts, gups, up_sum, down_sum, gout, gvec, group, step,
):
    packs = (w0, w1, w2, w3)
    one = eye(WIDTH)
    for d in range(4):
        cols = slice(WIDTH * d, WIDTH * d + WIDTH)
        up_all[:, cols] = packs[d][0:WIDTH, :]
        down_all[cols, :] = packs[d][WIDTH : 2 * WIDTH, :]
        up_t[cols, :] = nt(one, packs[d][0:WIDTH, :]).astype(BF)
        down_t[:, cols] = nt(one, packs[d][WIDTH : 2 * WIDTH, :]).astype(BF)
        extra = packs[d][2 * WIDTH : 2 * WIDTH + 16, :].astype(F32)
        bias = extra[0:1, :] + extra[1:2, :] + extra[2:3, :]
        column = jnp.broadcast_to(bias, (8, WIDTH)).T
        biases[d] = jnp.broadcast_to(column[:, 0:1], (WIDTH, BIN))
    spread_columns((v0, v1, v2), vecs)
    up_sum[...] = jnp.zeros_like(up_sum)
    down_sum[...] = jnp.zeros_like(down_sum)
    gout[...] = jnp.zeros_like(gout)
    gvec[...] = jnp.zeros_like(gvec)
    step[0] = 0

    def one_bin(mid_i, at_i, ct_i, sent_o, more_o, gm_o, da_o):
        j = step[0]
        step[0] = j + 1
        ones = jnp.ones((16, BIN), BF)
        middle = mid_i[...]
        mean, inverse = row_stats(middle)
        unit = (middle - mean) * inverse
        h2 = (unit * vecs[0] + vecs[1]).astype(BF)
        branch = ct_i[...]
        ups[...] = nn(up_t[...], h2)
        gacts[...] = nn(down_all[...], branch)
        for d in range(4):
            cols = slice(WIDTH * d, WIDTH * d + WIDTH)
            up = ups[cols, :] + biases[d]
            square = up * up
            tanh = jnp.tanh(up * (GELU_C * GELU_A * square + GELU_C))
            half = 0.5 * tanh + 0.5
            act = up * half
            slope = half + act * (1.0 - tanh) * (3.0 * GELU_C * GELU_A * square + GELU_C)
            acts[cols, :] = act.astype(BF)
            grad_up = gacts[cols, :] * slope
            add_columns(gvec.at[3 + d], grad_up)
            gups[cols, :] = grad_up.astype(BF)
        grad_h2 = nn(up_all[...], gups[...])
        result = middle + (nn(down_t[...], acts[...]) + vecs[2])
        up_sum[...] += nt(gups[...], h2)
        down_sum[...] += nt(acts[...], branch)
        write_wire(j, result, sent_o, more_o)
        scaled = grad_h2 * vecs[0]
        first = jnp.mean(scaled, 0, keepdims=True)
        second = jnp.mean(scaled * unit, 0, keepdims=True)
        grad_mid = branch.astype(F32) + inverse * (scaled - first - unit * second)
        gm_o[...] = grad_mid
        low_mid = grad_mid.astype(BF)
        gout[...] += nt(jnp.concatenate([at_i[...], ones], 0), low_mid)
        da_o[...] = nn(wout[...], low_mid).astype(BF)
        add_columns(gvec.at[0], grad_h2 * unit)
        add_columns(gvec.at[1], grad_h2)
        add_columns(gvec.at[2], branch.astype(F32))

    count = bins_here(plan, me[0])

    @pl.when(count > 0)
    def _():
        pltpu.emit_pipeline(
            one_bin,
            grid=(count,),
            in_specs=[step_spec(WIDTH, BIN)] * 3,
            out_specs=[*STEP_WIRE_SPECS, step_spec(WIDTH, BIN), step_spec(WIDTH, BIN)],
        )(mid, at, ct, sent, more, gm, da)

    for d in range(4):
        cols = slice(WIDTH * d, WIDTH * d + WIDTH)
        group[d, 0:WIDTH, :] = up_sum[cols, :].astype(BF)
        group[d, WIDTH : 2 * WIDTH, :] = down_sum[cols, :].astype(BF)
    for d, piece in enumerate((p0_o, p1_o, p2_o, p3_o)):
        rows = pl.ds(pl.multiple_of(((me[1] + d) & 3) * X_ROWS, 16), X_ROWS)
        piece[...] = group[:, rows, :]
    gout_o[...] = gout[0:WIDTH, :].astype(BF)
    rows = [column_sums(gvec[m]) for m in range(3)] + [gout[WIDTH : WIDTH + 1, :]]
    gvec_o[...] = jnp.concatenate(rows + [jnp.zeros((4, WIDTH), F32)], 0)
    for d in range(4):
        gvec_o[pl.ds(4 + ((me[0] + 4 - d) & 3), 1), :] = column_sums(gvec[3 + d])


def feed(plan, me, mid, at, ct, packs, wout, vectors):
    vmem = pl.BlockSpec(memory_space=pltpu.VMEM)
    smem = pl.BlockSpec(memory_space=pltpu.SMEM)
    anywhere = pl.BlockSpec(memory_space=pl.ANY)
    return pl.pallas_call(
        feed_kernel,
        in_specs=[smem] * 2 + [anywhere] * 3 + [vmem] * 8,
        out_specs=[anywhere] * 4 + [vmem] * 6,
        scratch_shapes=[
            pltpu.VMEM((4 * WIDTH, WIDTH), BF),
            pltpu.VMEM((WIDTH, 4 * WIDTH), BF),
            pltpu.VMEM((WIDTH, 4 * WIDTH), BF),
            pltpu.VMEM((4 * WIDTH, WIDTH), BF),
            pltpu.VMEM((3, WIDTH, BIN), F32),
            pltpu.VMEM((4, WIDTH, BIN), F32),
            pltpu.VMEM((4 * WIDTH, BIN), F32),
            pltpu.VMEM((4 * WIDTH, BIN), F32),
            pltpu.VMEM((4 * WIDTH, BIN), BF),
            pltpu.VMEM((4 * WIDTH, BIN), BF),
            pltpu.VMEM((4 * WIDTH, WIDTH), F32),
            pltpu.VMEM((4 * WIDTH, WIDTH), F32),
            pltpu.VMEM((WIDTH + 16, WIDTH), F32),
            pltpu.VMEM((7, WIDTH, 128), F32),
            pltpu.VMEM((4, GROUP_ROWS, WIDTH), BF),
            pltpu.SMEM((1,), jnp.int32),
        ],
        out_shape=[
            *WIRE_SHAPES,
            jax.ShapeDtypeStruct((MAX_BINS, WIDTH, BIN), F32),
            jax.ShapeDtypeStruct((MAX_BINS, WIDTH, BIN), BF),
            *[jax.ShapeDtypeStruct((4, X_ROWS, WIDTH), BF)] * 4,
            jax.ShapeDtypeStruct((WIDTH, WIDTH), BF),
            jax.ShapeDtypeStruct((8, WIDTH), F32),
        ],
        compiler_params=pltpu.CompilerParams(vmem_limit_bytes=56 * MIB),
        cost_estimate=pl.CostEstimate(flops=10**6, bytes_accessed=10**5, transcendentals=0),
        name="feed",
    )(plan, me, mid, at, ct, *packs, wout, *vectors)


TAIL_ROWS = 1600


def back_kernel(
    plan, me, xt, stat, h1, qk, vtok, e, linv, at, gm, da, wqkv, v0, gout, gvec_i,
    sent, more, mine_o, theirs_o, gain, grads, gvec, grads_o, step,
):
    gain[...] = jnp.broadcast_to(as_columns((v0,))[:, 0:1], (WIDTH, BIN))
    grads[...] = jnp.zeros_like(grads)
    gvec[...] = jnp.zeros_like(gvec)
    step[0] = 0

    def one_bin(xt_i, stat_i, h1_i, qk_i, vtok_i, e_i, linv_i, at_i, gm_i, da_i, sent_o, more_o):
        j = step[0]
        step[0] = j + 1
        ones = jnp.ones((16, BIN), BF)
        blank = jnp.zeros((HEAD_DIM, BIN), BF)
        queries = []
        keys = []
        values = []
        for h in range(HEADS):
            rows = slice(HEAD_DIM * h, HEAD_DIM * h + HEAD_DIM)
            krows = slice(WIDTH + HEAD_DIM * h, WIDTH + HEAD_DIM * h + HEAD_DIM)
            pair = slice(128 * (h // 2), 128 * (h // 2) + 128)
            grad_att = (da_i[rows, :].astype(F32) * linv_i[h : h + 1, :]).astype(BF)
            spread = jnp.concatenate([grad_att, blank] if h % 2 == 0 else [blank, grad_att], 0)
            inner = jnp.sum(grad_att.astype(F32) * at_i[rows, :].astype(F32), 0, keepdims=True)
            weights = e_i[h]
            grad_scores = (weights.astype(F32) * (nn(vtok_i[:, pair], spread) - inner)).astype(BF)
            values.append(nt(grad_att, weights).astype(BF))
            queries.append((nn(qk_i[krows, :], grad_scores) * 0.125).astype(BF))
            keys.append(nt(qk_i[rows, :], grad_scores).astype(BF))
        h1_ones = jnp.concatenate([h1_i[...], ones], 0)
        grad_h1 = jnp.zeros((WIDTH, BIN), F32)
        for m, parts in enumerate((queries, keys, values)):
            mixed = jnp.concatenate(parts, 0)
            grads[m] += nt(h1_ones, mixed)
            grad_h1 = grad_h1 + nn(wqkv[:, WIDTH * m : WIDTH * m + WIDTH], mixed)
        inverse = stat_i[1:2, :]
        unit = (xt_i[...].astype(F32) - stat_i[0:1, :]) * inverse
        scaled = grad_h1 * gain[...]
        first = jnp.mean(scaled, 0, keepdims=True)
        second = jnp.mean(scaled * unit, 0, keepdims=True)
        result = gm_i[...] + inverse * (scaled - first - unit * second)
        write_wire(j, result, sent_o, more_o)
        add_columns(gvec.at[0], grad_h1 * unit)
        add_columns(gvec.at[1], grad_h1)

    count = bins_here(plan, me[0])

    @pl.when(count > 0)
    def _():
        pltpu.emit_pipeline(
            one_bin,
            grid=(count,),
            in_specs=[
                step_spec(WIDTH, BIN), step_spec(8, BIN), step_spec(WIDTH, BIN), step_spec(2 * WIDTH, BIN),
                step_spec(BIN, WIDTH), step_spec(HEADS, BIN, BIN), step_spec(8, BIN), step_spec(WIDTH, BIN),
                step_spec(WIDTH, BIN), step_spec(WIDTH, BIN),
            ],
            out_specs=STEP_WIRE_SPECS,
        )(xt, stat, h1, qk, vtok, e, linv, at, gm, da, sent, more)

    for m in range(3):
        grads_o[WIDTH * m : WIDTH * m + WIDTH, :] = grads[m, 0:WIDTH, :].astype(BF)
    grads_o[3 * WIDTH : 4 * WIDTH, :] = gout[...]
    query_bias, value_bias = grads[0, WIDTH : WIDTH + 1, :], grads[2, WIDTH : WIDTH + 1, :]
    rows = [query_bias, column_sums(gvec[0]), value_bias, column_sums(gvec[1]), gvec_i[...]]
    grads_o[4 * WIDTH : 4 * WIDTH + 16, :] = jnp.concatenate(rows + [jnp.zeros((4, WIDTH), F32)], 0).astype(BF)
    grads_o[4 * WIDTH + 16 :, :] = jnp.zeros((TAIL_ROWS - 4 * WIDTH - 16, WIDTH), BF)
    half = TAIL_ROWS // 2
    mine_o[...] = grads_o[pl.ds(pl.multiple_of(me[2] * half, 16), half), :]
    theirs_o[...] = grads_o[pl.ds(pl.multiple_of((1 - me[2]) * half, 16), half), :]


def back(plan, me, saved, wqkv, gain, gout, gvec):
    vmem = pl.BlockSpec(memory_space=pltpu.VMEM)
    smem = pl.BlockSpec(memory_space=pltpu.SMEM)
    anywhere = pl.BlockSpec(memory_space=pl.ANY)
    return pl.pallas_call(
        back_kernel,
        in_specs=[smem] * 2 + [anywhere] * 10 + [vmem] * 4,
        out_specs=[anywhere] * 2 + [vmem] * 2,
        scratch_shapes=[
            pltpu.VMEM((WIDTH, BIN), F32),
            pltpu.VMEM((3, WIDTH + 16, WIDTH), F32),
            pltpu.VMEM((2, WIDTH, 128), F32),
            pltpu.VMEM((TAIL_ROWS, WIDTH), BF),
            pltpu.SMEM((1,), jnp.int32),
        ],
        out_shape=[*WIRE_SHAPES, *[jax.ShapeDtypeStruct((TAIL_ROWS // 2, WIDTH), BF)] * 2],
        compiler_params=pltpu.CompilerParams(vmem_limit_bytes=56 * MIB),
        cost_estimate=pl.CostEstimate(flops=10**6, bytes_accessed=10**5, transcendentals=0),
        name="back",
    )(plan, me, *saved, wqkv, gain, gout, gvec)


UNPACK_IMAGES = 8


def unpack_kernel(
    side, start, plan, me, own, own_more, before, far, after, more_before, more_far, more_after, base, posm, *rest,
):
    out, near, columns, rows, sems = rest[-5:]
    group = pl.program_id(0) + start
    bins = before.shape[0]
    rest = MAX_BINS - bins
    extra = pl.ds(side * rest, rest)
    pieces = [(ref, near.at[k, pl.ds(0, bins)]) for k, ref in enumerate((own, before, far, after))]
    more = [(own_more, near.at[0, pl.ds(bins, rest)])] + [
        (ref.at[extra], near.at[k + 1, pl.ds(bins, rest)]) for k, ref in enumerate((more_before, more_far, more_after))
    ]

    @pl.when(group == start)
    def _():
        copies = [pltpu.make_async_copy(*pair, sems.at[k]) for k, pair in enumerate(pieces)]
        for copy in copies:
            copy.start()
        for copy in copies:
            copy.wait()

    @pl.when((group == start) & (plan[3, 0] > 4 * bins))
    def _():
        copies = [pltpu.make_async_copy(*pair, sems.at[4 + k]) for k, pair in enumerate(more)]
        for copy in copies:
            copy.start()
        for copy in copies:
            copy.wait()

    turned = posm[...].T
    for i in range(UNPACK_IMAGES):
        columns[i] = jnp.broadcast_to(turned[0:SLOT_ROWS, i : i + 1], (SLOT_ROWS, 128))
    lane = iota((SLOT_ROWS, 128), 1).astype(F32)
    for i in range(UNPACK_IMAGES):
        at = plan[0, group * UNPACK_IMAGES + i]
        spot = columns[i] + plan[1, group * UNPACK_IMAGES + i].astype(F32)
        pick = [jnp.where(spot == lane + 128.0 * half, 1.0, 0.0) for half in range(2)]
        pick = jnp.concatenate(pick, 1).astype(BF)
        rows[i] = nn(pick, near[(at - me[0]) & 3, at // 4])
    kept = jnp.swapaxes(columns[...], 0, 1)[0:SLOTS] >= 0.0
    for half in range(2):

        @pl.when((group & 1) == half)
        def _():
            for c in range(3):
                lanes = slice(128 * c, 128 * c + 128)
                moved = jnp.swapaxes(rows[:, :, lanes], 0, 1)[0:SLOTS]
                dropped = base[:, 8 * half : 8 * half + 8, lanes].astype(F32)
                out[:, :, lanes] = jnp.where(kept, moved, dropped)


def unpack(side, start, count, plan, me, nears, more, base, posm, rest=()):
    return pl.pallas_call(
        functools.partial(unpack_kernel, side, start),
        grid_spec=pltpu.PrefetchScalarGridSpec(
            num_scalar_prefetch=2,
            grid=(count,),
            in_specs=[pl.BlockSpec(memory_space=pl.ANY)] * 8
            + [
                pl.BlockSpec((SLOTS, 2 * UNPACK_IMAGES, WIDTH), lambda g, *_: (0, (g + start) // 2, 0)),
                pl.BlockSpec((UNPACK_IMAGES, BIN), lambda g, *_: (g + start, 0)),
            ]
            + [pl.BlockSpec(memory_space=pl.ANY)] * len(rest),
            out_specs=pl.BlockSpec((SLOTS, UNPACK_IMAGES, WIDTH), lambda g, *_: (0, g + start, 0)),
            scratch_shapes=[
                pltpu.VMEM((4, MAX_BINS, BIN, WIDTH), BF),
                pltpu.VMEM((UNPACK_IMAGES, SLOT_ROWS, 128), F32),
                pltpu.VMEM((UNPACK_IMAGES, SLOT_ROWS, WIDTH), F32),
                pltpu.SemaphoreType.DMA((8,)),
            ],
        ),
        out_shape=jax.ShapeDtypeStruct((SLOTS, IMAGES, WIDTH), F32),
        input_output_aliases={12: 0} if rest else {},
        compiler_params=pltpu.CompilerParams(vmem_limit_bytes=48 * MIB),
        cost_estimate=pl.CostEstimate(flops=10**6, bytes_accessed=10**5, transcendentals=0),
        name="unpack",
    )(plan, me, *nears, *more, base, posm, *rest)


PART_PIECE = GROUP_ROWS // 8
TAIL_PIECE = TAIL_ROWS // 8
PIECE = PART_PIECE + TAIL_PIECE


def finish_kernel(
    me, mine, other, w_up, w_down, b_up, w_qkv, w_out, bias_q, gain1, bias_v, shift1, gain2, shift2,
    bias_down, bias_out, part, tail,
):
    x, core = me[1], me[2]
    for k in range(4):
        place = (x + 4 - k) & 3
        for source, own in ((mine, core), (other, 1 - core)):
            at = pl.multiple_of(place * (2 * PART_PIECE) + own * PART_PIECE, 8)
            part[pl.ds(at, PART_PIECE), :] = source[PIECE * k : PIECE * k + PART_PIECE, :].astype(F32)
            at = pl.multiple_of(own * (4 * TAIL_PIECE) + place * TAIL_PIECE, 8)
            tail[pl.ds(at, TAIL_PIECE), :] = source[PIECE * k + PART_PIECE : PIECE * (k + 1), :].astype(F32)
    w_up[...] = part[0:WIDTH, :].T
    w_down[...] = part[WIDTH : 2 * WIDTH, :]
    b_up[...] = tail[pl.ds(4 * WIDTH + 8 + me[0], 1), :].reshape(WIDTH)
    for m in range(3):
        w_qkv[:, WIDTH * m : WIDTH * m + WIDTH] = tail[WIDTH * m : WIDTH * m + WIDTH, :]
    w_out[...] = tail[3 * WIDTH : 4 * WIDTH, :]
    for m, vector in enumerate((bias_q, gain1, bias_v, shift1, gain2, shift2, bias_down, bias_out)):
        vector[...] = tail[4 * WIDTH + m : 4 * WIDTH + m + 1, :].reshape(WIDTH)


def finish(me, mine, other):
    vmem = pl.BlockSpec(memory_space=pltpu.VMEM)
    shapes = [(WIDTH, WIDTH)] * 2 + [(WIDTH,), (WIDTH, 3 * WIDTH), (WIDTH, WIDTH)] + [(WIDTH,)] * 8
    return pl.pallas_call(
        finish_kernel,
        out_shape=[jax.ShapeDtypeStruct(shape, F32) for shape in shapes],
        in_specs=[pl.BlockSpec(memory_space=pltpu.SMEM), vmem, vmem],
        out_specs=[vmem] * len(shapes),
        scratch_shapes=[pltpu.VMEM((GROUP_ROWS, WIDTH), F32), pltpu.VMEM((TAIL_ROWS, WIDTH), F32)],
        compiler_params=pltpu.CompilerParams(vmem_limit_bytes=32 * MIB),
        name="finish",
    )(me, mine, other)


def shift_y(values, by):
    return lax.ppermute(values, "tensor", [(i, (i + by) % 4) for i in range(4)])


def swap_core(values):
    return lax.ppermute(values, "dp", [(i, i ^ 1) for i in range(32)])


def shift_x(values, by):
    return lax.ppermute(values, "dp", [(i, (i + 8 * by) % 32) for i in range(32)])


def shift_z(values, by):
    return lax.ppermute(values, "dp", [(i, i // 8 * 8 + (i + 2 * by) % 8) for i in range(32)])


def add_up(parts):
    total = parts[0].astype(F32)
    for part in parts[1:]:
        total = total + part.astype(F32)
    return total.astype(BF)


def pick_block(values, index, axis, size):
    return lax.dynamic_slice_in_dim(values, index * size, size, axis)


def scatter_x(values, axis):
    part = values.shape[axis] // 4
    x = lax.axis_index("dp") // 8
    own = pick_block(values, x, axis, part)
    return add_up([own] + [shift_x(pick_block(values, (x + d) % 4, axis, part), d) for d in (1, 3, 2)])


def scatter_core(values, axis):
    half = values.shape[axis] // 2
    core = lax.axis_index("dp") % 2
    return add_up([pick_block(values, core, axis, half), swap_core(pick_block(values, 1 - core, axis, half))])


def joined(*values):
    return lax.optimization_barrier(values)


def send_more(used, out_more, grad_more):
    shape = (2 * (MAX_BINS - SENT_BINS), BIN, WIDTH)

    def send():
        both = jnp.concatenate([out_more, grad_more], 0)
        return tuple(shift_y(both, d) for d in (3, 2, 1))

    def leave():
        anywhere = pl.BlockSpec(memory_space=pl.ANY)
        return pl.pallas_call(
            lambda *refs: None,
            out_shape=[jax.ShapeDtypeStruct(shape, BF)] * 3,
            out_specs=[anywhere] * 3,
            name="leave",
        )()

    return lax.cond(used[0] > 4 * SENT_BINS, lambda: list(send()), lambda: list(leave()))


def local(
    tokens, keep_mask, norm1_gain, norm1_shift, w_qkv, bias_q, bias_v, w_out, bias_out,
    norm2_gain, norm2_shift, w_up, bias_up, w_down, bias_down, cotangent,
):
    dp = lax.axis_index("dp")
    me = jnp.stack([lax.axis_index("tensor"), dp // 8, dp % 2]).astype(jnp.int32)
    tok = jnp.transpose(tokens, (1, 0, 2))
    cot = jnp.transpose(cotangent, (1, 0, 2))

    own = pack_weights(w_up, w_down, bias_up)
    packs = [own, shift_y(own, 1), shift_y(own, 2), shift_y(own, 3)]
    plan, used, posm = prepare(keep_mask)

    xt, ct, stat, h1, qk, vtok, weights, linv, at, mid = attend(
        plan, me, tok, cot, posm, w_qkv, w_out, (norm1_gain, norm1_shift, bias_q, bias_v, bias_out)
    )
    sent, out_more, grad_mid, grad_att, *parts, gout, gvec = feed(
        plan, me, mid, at, ct, packs, w_out, (norm2_gain, norm2_shift, bias_down)
    )
    after, before = shift_y(sent, 1), shift_y(sent, 3)
    moved = [shift_x(parts[d], d) for d in (1, 3, 2)]
    grad_sent, grad_more, tail, other_tail = back(
        plan, me, (xt, stat, h1, qk, vtok, weights, linv, at, grad_mid, grad_att), w_qkv, norm1_gain, gout, gvec
    )
    after, before, moved[2], grad_sent, grad_more, tail, other_tail = joined(
        after, before, moved[2], grad_sent, grad_more, tail, other_tail
    )

    far, grad_before = shift_y(after, 1), shift_y(grad_sent, 3)
    tail = add_up([tail, swap_core(other_tail)])
    part = add_up([parts[0]] + moved)
    tail = scatter_x(tail, 0)
    part = scatter_core(part, 1)
    more = send_more(used, out_more, grad_more)
    tail, part, far, grad_before, *more = joined(tail, part, far, grad_before, *more)

    grad_after, grad_far = shift_y(grad_sent, 1), shift_y(grad_before, 3)
    piece = jnp.concatenate([part.reshape(4 * PART_PIECE, WIDTH), tail], 0)
    moved = [shift_z(piece, d) for d in (1, 3, 2)]
    out = unpack(0, 0, 4, plan, me, (sent, out_more, before, far, after), more, tok, posm)
    *moved, out, grad_after, grad_far = joined(*moved, out, grad_after, grad_far)
    piece = add_up([piece] + moved)

    def toward(d):
        rows = piece[PART_PIECE * d : PART_PIECE * (d + 1)]
        return jnp.concatenate([rows, piece[4 * PART_PIECE :]], 0)

    moved = [shift_y(toward(d), 4 - d) for d in (1, 3, 2)]
    grad_nears = (grad_sent, grad_more, grad_before, grad_far, grad_after)
    grad_tokens = unpack(1, 0, 2, plan, me, grad_nears, more, cot, posm)
    *moved, grad_tokens = joined(*moved, grad_tokens)
    piece = add_up([toward(0)] + moved)
    moved = [shift_x(piece, d) for d in (1, 2, 3)]
    grad_tokens = unpack(1, 2, 2, plan, me, grad_nears, more, cot, posm, (grad_tokens,))
    *moved, grad_tokens = joined(*moved, grad_tokens)
    mine = jnp.concatenate([piece] + moved, 0)
    other = swap_core(mine)
    (
        grad_up, grad_down, grad_bias_up, grad_qkv, grad_out, grad_bias_q, grad_gain1, grad_bias_v,
        grad_shift1, grad_gain2, grad_shift2, grad_bias_down, grad_bias_out,
    ) = finish(me, mine, other)
    return (
        jnp.transpose(out, (1, 0, 2)), jnp.transpose(grad_tokens, (1, 0, 2)), grad_gain1, grad_shift1,
        grad_qkv, grad_bias_q, grad_bias_v, grad_out, grad_bias_out, grad_gain2, grad_shift2,
        grad_up, grad_bias_up, grad_down, grad_bias_down,
    )


def solution(mesh):
    rows = P("dp", None, None)
    return jax.shard_map(
        local,
        mesh=mesh,
        in_specs=(
            rows, P("dp", None), P(), P(), P(), P(), P(), P(), P(), P(), P(),
            P(None, "tensor"), P("tensor"), P("tensor", None), P(), rows,
        ),
        out_specs=(
            rows, rows, P(), P(), P(), P(), P(), P(), P(), P(), P(),
            P(None, "tensor"), P("tensor"), P("tensor", None), P(),
        ),
        check_vma=False,
    )
```
